256 devices in a mesh: gx: 8 (over z), gy: 32 (over x, y, core).
Axes of the slice: x: 4, y: 4, z: 8, core: 2. Of those that a mesh axis runs over, the one named last changes fastest.
Arguments:
- design: float32 [64, 256, 4], P('gx', 'gy'), may hold values from 0.1 to 1
- element_matrix: float32 [24, 24], replicated, as said below
- fixed: int32 [3, 64, 256, 4], P(None, 'gx', 'gy'), may hold values 0 or 1
- inverses: float32 [32, 128, 2, 192, 192], P('gx', 'gy'), as said below
- state: float32 [3, 64, 256, 4], P(None, 'gx', 'gy'), may hold values from -6 to 6
- load: float32 [3, 64, 256, 4], P(None, 'gx', 'gy'), may hold values from -24 to 24
Outputs:
- adjoint: float32 [3, 64, 256, 4], P(None, 'gx', 'gy')
- design_gradient: float32 [64, 256, 4], P('gx', 'gy')
The draws below stay inside these ranges and needn't reach their ends.
Inputs may be any that keep to these rules, and one draw needn't show every extreme that they name: `element_matrix`: symmetric positive definite. `inverses`: each block symmetric positive definite.
All inputs are finite; a program needn't handle non-finite values. No bound on the sum of `fixed` on one device may be relied on, other than what follows from the above.
Results may differ from the reference program's by a relative error of at most 0.00024.
Values sent between devices are 32-bit elements; how exact they have to be, the bound alone decides.
No kernel may reach another device: no remote copies, remote signals or barrier semaphores. Data moves between devices by JAX's collectives and lax.ppermute only.
A program may use at most 128 MiB of HBM per device.

```python
import math
import jax
import jax.numpy as jnp
from jax import lax

NZ = 4
ITERS = 2
ORDER = 192
NX = 64
NY = 256


def draw_element_matrix(key, part):
    key = jax.random.fold_in(key, 11)
    first_key, second_key = jax.random.split(key)
    factor = jnp.clip(jax.random.normal(first_key, (24, 24), jnp.float32), -3.0, 3.0)
    product = jnp.dot(factor, factor.T, precision=lax.Precision.HIGHEST) / 24.0
    product = 0.5 * (product + product.T)
    scales = jnp.exp(0.5 * jax.random.uniform(second_key, (24,), jnp.float32, 0.0, math.log(2.0)))
    dense = product + 0.25 * jnp.eye(24, dtype=jnp.float32)
    return scales[:, None] * dense * scales[None, :]


def draw_inverses(key, part):
    key = jax.random.fold_in(key, 23)
    first_key, second_key = jax.random.split(key)
    extent = (NY // 2, NZ // 2, ORDER, ORDER)
    identity = jnp.eye(ORDER, dtype=jnp.float32)
    lowest = math.log(0.5)

    def one_row(index):
        row_key = jax.random.fold_in(first_key, index)
        scale_key = jax.random.fold_in(second_key, index)
        factor = jnp.clip(jax.random.normal(row_key, extent, jnp.float32), -3.0, 3.0)
        product = jnp.einsum('bcik,bcjk->bcij', factor, factor, precision=lax.Precision.HIGHEST) / ORDER
        product = 0.5 * (product + jnp.swapaxes(product, -1, -2))
        scales = jnp.exp(0.5 * jax.random.uniform(scale_key, extent[:3], jnp.float32, lowest, math.log(2.0)))
        return scales[..., :, None] * (product + 0.25 * identity) * scales[..., None, :]
    return lax.map(one_row, jnp.arange(NX // 2, dtype=jnp.int32))


def draw_load(key, part):
    key = jax.random.fold_in(key, 37)
    across_x = jnp.arange(NX, dtype=jnp.float32) / max(NX - 1, 1)
    across_y = jnp.arange(NY, dtype=jnp.float32) / max(NY - 1, 1)
    amplitude = 1.0 + across_x[:, None, None] + across_y[None, :, None]
    values = jnp.clip(jax.random.normal(key, (3, NX, NY, NZ), jnp.float32), -8.0, 8.0)
    return values * amplitude[None]


def set_ends(values, rng, smallest, largest):
    shape = values.shape
    index_at = [jax.random.randint(jax.random.fold_in(rng, axis), (), 0, shape[axis]) for axis in range(len(shape))]
    values = values.at[tuple(index_at)].set(smallest)
    longest = shape.index(max(shape))
    index_at[longest] = (index_at[longest] + 1) % shape[longest]
    return values.at[tuple(index_at)].set(largest)


def steps_of(stream_key, dims, cuts, smallest, largest):
    def one(dim, blocks):
        steps = jax.random.uniform(jax.random.fold_in(jax.random.fold_in(stream_key, 6), dim), (blocks,), jnp.float32, smallest / len(cuts), largest / len(cuts))
        return jnp.repeat(jnp.exp(steps), dims[dim] // blocks).reshape((-1,) + (1,) * (len(dims) - dim - 1))

    gain = one(*cuts[0])
    for cut in cuts[1:]:
        gain = gain * one(*cut)
    return gain


def centred(rng, shape, deviation, most, cuts=(), kind=jnp.bfloat16):
    level = steps_of(rng, shape, cuts, -0.22, 0.18) if cuts else 1.0
    array = jax.random.normal(rng, shape, jnp.float32) * deviation * level
    return jnp.minimum(jnp.maximum(array, -most), most).astype(kind)


def setup_inputs(seed: int = 0) -> dict:
    seeds = jax.random.split(jax.random.key(seed), 7)
    return {
        "design": jnp.clip(0.1 + 0.9 * jax.random.uniform(seeds[0], (NX, NY, NZ), jnp.float32) ** steps_of(seeds[0], (NX, NY, NZ), ((0, 8), (1, 32)), -0.2, 0.2), 0.1, 1.0),
        "element_matrix": draw_element_matrix(jax.random.fold_in(seeds[6], 71), 0),
        "fixed": set_ends((jax.random.randint(seeds[2], (3, NX, NY, NZ), 0, 8) < 1).astype(jnp.int32), jax.random.fold_in(seeds[2], 1), 0, 1),
        "inverses": draw_inverses(jax.random.fold_in(seeds[6], 71), 0),
        "state": centred(seeds[4], (3, NX, NY, NZ), 1.0, 6.0, ((1, 8), (2, 32)), jnp.float32),
        "load": draw_load(jax.random.fold_in(seeds[6], 71), 0),
    }


def hat_filter_axis(values, along, start_at, extent):
    summed = None
    for offset in range(-3, 4):
        portion = lax.slice_in_dim(values, start_at + offset, start_at + offset + extent, axis=along)
        weighted = (4.0 - abs(offset)) * portion
        summed = weighted if summed is None else summed + weighted
    return summed


def edge_weight(position, length):
    summed = jnp.zeros(position.shape, jnp.float32)
    for offset in range(-3, 4):
        inside = (position + offset >= 0) & (position + offset < length)
        summed = summed + (4.0 - abs(offset)) * inside.astype(jnp.float32)
    return summed


def split_blocks(values, along):
    halves = values.shape[along] // 2
    shaped = values.reshape(values.shape[:along] + (halves, 2) + values.shape[along + 1:])
    bottom = lax.slice_in_dim(shaped, 0, halves - 1, axis=along)
    higher = lax.slice_in_dim(shaped, 1, halves, axis=along)
    return jnp.concatenate([bottom, higher], axis=along + 1)


def merge_blocks(values, along):
    number = values.shape[along]
    target = values.shape[:along] + (2 * number,) + values.shape[along + 2:]
    bottom = lax.slice_in_dim(values, 0, 2, axis=along + 1).reshape(target)
    higher = lax.slice_in_dim(values, 2, 4, axis=along + 1).reshape(target)
    widths_bottom = [(0, 0)] * len(target)
    widths_higher = [(0, 0)] * len(target)
    widths_bottom[along] = (0, 2)
    widths_higher[along] = (2, 0)
    return jnp.pad(bottom, widths_bottom) + jnp.pad(higher, widths_higher)


def to_blocks(extended):
    blocks = split_blocks(extended, 3)
    blocks = split_blocks(blocks, 2)
    blocks = split_blocks(blocks, 1)
    blocks = blocks.transpose(1, 3, 5, 0, 2, 4, 6)
    return blocks.reshape(blocks.shape[:3] + (192,))


def from_blocks(solved):
    values = solved.reshape(solved.shape[:3] + (3, 4, 4, 4))
    values = values.transpose(3, 0, 4, 1, 5, 2, 6)
    values = merge_blocks(values, 1)
    values = merge_blocks(values, 2)
    return merge_blocks(values, 3)


def smooth_global(values):
    padded = jnp.pad(values, ((3, 3), (3, 3), (3, 3)))
    padded = hat_filter_axis(padded, 0, 3, NX)
    padded = hat_filter_axis(padded, 1, 3, NY)
    return hat_filter_axis(padded, 2, 3, NZ)


def element_values(vector):
    padded = jnp.pad(vector, ((0, 0), (0, 1), (0, 1), (0, 1)))
    corners = []
    for corner_z in range(2):
        for corner_y in range(2):
            for corner_x in range(2):
                corners.append(padded[:, corner_x:corner_x + NX, corner_y:corner_y + NY, corner_z:corner_z + NZ])
    return jnp.stack(corners)


def stiffness(vector, scale_field, element_matrix):
    stacked = element_values(vector).reshape((24, NX, NY, NZ))
    forces = jnp.einsum("ij,jxyz->ixyz", element_matrix, stacked, precision=lax.Precision.HIGHEST) * scale_field
    forces = jnp.pad(forces.reshape((8, 3, NX, NY, NZ)), ((0, 0), (0, 0), (1, 0), (1, 0), (1, 0)))
    result = jnp.zeros((3, NX, NY, NZ), jnp.float32)
    number = 0
    for corner_z in range(2):
        for corner_y in range(2):
            for corner_x in range(2):
                result = result + forces[number][:, 1 - corner_x:1 - corner_x + NX, 1 - corner_y:1 - corner_y + NY, 1 - corner_z:1 - corner_z + NZ]
                number = number + 1
    return result


def precondition(vector, inverses, movable):
    extended = jnp.pad(vector * movable, ((0, 0), (1, 1), (1, 1), (1, 1)))
    blocks = to_blocks(extended)

    def one_row(operands):
        matrices, entries = operands
        return jnp.einsum("bcji,bcj->bci", matrices, entries, precision=lax.Precision.HIGHEST)

    solved = lax.map(one_row, (inverses, blocks))
    summed = from_blocks(solved)
    return summed[:, 1:-1, 1:-1, 1:-1] * movable


def reference(design, element_matrix, fixed, inverses, state, load):
    movable = (1 - fixed).astype(jnp.float32)
    weight_x = edge_weight(jnp.arange(NX, dtype=jnp.int32), NX)
    weight_y = edge_weight(jnp.arange(NY, dtype=jnp.int32), NY)
    weight_z = edge_weight(jnp.arange(NZ, dtype=jnp.int32), NZ)
    normalizer = weight_x[:, None, None] * weight_y[None, :, None] * weight_z[None, None, :]
    density = smooth_global(design) / normalizer
    scale_field = density * density * density

    def operator(vector):
        return movable * stiffness(movable * vector, scale_field, element_matrix)

    adjoint = jnp.zeros((3, NX, NY, NZ), jnp.float32)
    residual = movable * load
    preconditioned = precondition(residual, inverses, movable)
    direction = preconditioned
    norm_now = jnp.sum(residual * preconditioned)
    for iteration in range(ITERS):
        image = operator(direction)
        step_size = norm_now / jnp.sum(direction * image)
        adjoint = adjoint + step_size * direction
        residual = residual - step_size * image
        if iteration + 1 < ITERS:
            preconditioned = precondition(residual, inverses, movable)
            norm_next = jnp.sum(residual * preconditioned)
            direction = preconditioned + (norm_next / norm_now) * direction
            norm_now = norm_next
    adjoint_elements = element_values(adjoint).reshape((24, NX, NY, NZ))
    state_elements = element_values(state).reshape((24, NX, NY, NZ))
    pushed = jnp.einsum("ij,jxyz->ixyz", element_matrix, state_elements, precision=lax.Precision.HIGHEST)
    energy = jnp.sum(adjoint_elements * pushed, axis=0)
    sensitivity = -3.0 * density * density * energy
    design_gradient = smooth_global(sensitivity / normalizer)
    return adjoint, design_gradient
```

```python
import functools
import jax
import jax.numpy as jnp
from jax import lax
from jax.experimental import pallas as pl
from jax.experimental.pallas import tpu as pltpu
from jax.sharding import PartitionSpec as P

C = 8
NZ = 4
F32 = jnp.float32
HIGHEST = lax.Precision.HIGHEST
VMEM_LIMIT = 20 * 1024 * 1024
VM = pl.BlockSpec(memory_space=pltpu.VMEM)


def iota(shape, dim):
    return lax.broadcasted_iota(jnp.int32, shape, dim)


def dot(left, right):
    return jnp.dot(left, right, precision=HIGHEST, preferred_element_type=F32)


def roll(value, shift, axis):
    size = value.shape[axis]
    return pltpu.roll(value, shift % size, axis)


def lanes_of(value):
    return iota(value.shape, 1)


def spread_matrix(z):
    y, lane = iota((8, 128), 0), iota((8, 128), 1)
    return (lane == 8 * (y + 4) + z + 1).astype(F32)


def pack_kernel(load_ref, fixed_ref, state_ref, design_ref, own_ref, right_ref, left_ref):
    own = jnp.zeros((80, 128), F32)
    for z in range(NZ):
        rows = pl.ds(z, 24, stride=NZ)
        movable = (1 - fixed_ref[rows, :]).astype(F32)
        piece = jnp.concatenate(
            [movable * load_ref[rows, :], movable, state_ref[rows, :], design_ref[pl.ds(z, 8, stride=NZ), :]],
            axis=0,
        )
        own = own + dot(piece, spread_matrix(z))
    own_ref[...] = own
    lane = iota((8, 128), 1)
    row = iota((8, 128), 0)
    design = roll(own[72:80], -32, 1)
    for out_ref, edge, first in ((right_ref, 7, 4), (left_ref, 0, 0)):
        edges = jnp.zeros((8, 128), F32)
        for field in range(6):
            line = own[8 * field + edge : 8 * field + edge + 1]
            edges = jnp.where(row == field, line, edges)
        out_ref[0:8, :] = jnp.where(lane < 64, design, roll(edges, 32, 1))
        upper = [own[48 + 8 * c : 56 + 8 * c] for c in range(3)]
        if first == 4:
            upper = [upper[0], upper[1], upper[2]]
            a = jnp.where(row < 4, roll(upper[0], 4, 0), upper[1])
            b = roll(upper[2], 4, 0)
        else:
            a = jnp.where(row < 4, upper[0], roll(upper[1], 4, 0))
            b = upper[2]
        out_ref[8:16, :] = jnp.where(lane < 64, roll(a, -32, 1), roll(b, 32, 1))


def widen_kernel(flag_ref, own_ref, from_left_ref, from_right_ref, fields_ref, design_ref, up_ref, down_ref):
    has_left, has_right = flag_ref[0:1, :], flag_ref[1:2, :]
    lane = iota((8, 128), 1)
    row = iota((8, 128), 0)
    middle = (lane >= 32) & (lane < 96)
    left, right = from_left_ref[...] * has_left, from_right_ref[...] * has_right
    rows_left = jnp.where(middle, roll(left[0:8], -32, 1), 0.0)
    rows_right = jnp.where(middle, roll(right[0:8], -32, 1), 0.0)
    design = jnp.concatenate([left[0:8], roll(own_ref[72:80, :], -32, 1), right[0:8]], axis=0)
    design_ref[...] = design
    tall_lane = iota((24, 128), 1)
    design = jnp.where(tall_lane < 64, design, 0.0)
    edges_up = [jnp.zeros((8, 128), F32), jnp.zeros((8, 128), F32)]
    edges_down = [jnp.zeros((8, 128), F32), jnp.zeros((8, 128), F32)]
    for field in range(6):
        own = own_ref[8 * field : 8 * field + 8, :]
        turned = roll(own, 4, 0)
        low = jnp.where(row >= 4, turned, jnp.where(row == 3, rows_left[field : field + 1], 0.0))
        high = jnp.where(row < 4, turned, jnp.where(row == 4, rows_right[field : field + 1], 0.0))
        fields_ref[16 * field : 16 * field + 8, :] = low
        fields_ref[16 * field + 8 : 16 * field + 16, :] = high
        at = 64 + 8 * field
        place = (lane >= at) & (lane < at + 8)
        for half, value in enumerate((low, high)):
            edges_up[half] = jnp.where(place, roll(value, at - 88, 1), edges_up[half])
            edges_down[half] = jnp.where(place, roll(value, at - 32, 1), edges_down[half])
    zeros = jnp.zeros((8, 128), F32)
    up_ref[0:24, :] = jnp.where(tall_lane < 64, design, jnp.concatenate(edges_up + [zeros], axis=0))
    down_ref[0:24, :] = jnp.where(tall_lane < 64, design, jnp.concatenate(edges_down + [zeros], axis=0))
    state_left, state_right = left[8:16], right[8:16]
    ups = [zeros, zeros]
    downs = [zeros, zeros]
    for c in range(3):
        turned = roll(own_ref[48 + 8 * c : 56 + 8 * c, :], 4, 0)
        lane_turn = 32 if c < 2 else -32
        got_left = jnp.where(middle, roll(state_left, lane_turn, 1), 0.0)
        got_right = jnp.where(middle, roll(state_right, lane_turn, 1), 0.0)
        if c == 1:
            got_left = roll(got_left, 4, 0)
        else:
            got_right = roll(got_right, 4, 0)
        low = jnp.where(row >= 4, turned, got_left)
        high = jnp.where(row < 4, turned, got_right)
        fields_ref[96 + 16 * c : 104 + 16 * c, :] = low
        fields_ref[104 + 16 * c : 112 + 16 * c, :] = high
        place = (lane >= 32 * c) & (lane < 32 * c + 32)
        for half, value in enumerate((low, high)):
            ups[half] = jnp.where(place, roll(value, 32 * c - 64, 1), ups[half])
            downs[half] = jnp.where(place, roll(value, 32 * c - 32, 1), downs[half])
    for half in range(2):
        up_ref[24 + 8 * half : 32 + 8 * half, :] = ups[half]
        down_ref[24 + 8 * half : 32 + 8 * half, :] = downs[half]


def gather_matrix():
    row, lane = iota((128, 128), 0), iota((128, 128), 1)
    block_y, block_z = row // 32, (row // 16) % 2
    t, u = (row // 4) % 4, row % 4
    return (lane == 8 * (2 * block_y + t + 3) + 2 * block_z + u).astype(F32)


def group_transpose(value):
    row, group = iota((8, 128), 0), iota((8, 128), 1) // 16
    for d in (1, 2, 4):
        row_bit, group_bit = (row // d) % 2, (group // d) % 2
        down = roll(roll(value, d, 0), -16 * d, 1)
        up = roll(roll(value, -d, 0), 16 * d, 1)
        moved = jnp.where(row_bit == 1, down, up)
        value = jnp.where(row_bit == group_bit, value, moved)
    return value


def solve_blocks(field, matrices_ref, turned_ref, solved_ref, placed_ref):
    gather = gather_matrix()
    turned_ref[:, 0:48] = lax.dot_general(
        gather, field, (((1,), (1,)), ((), ())), precision=HIGHEST, preferred_element_type=F32
    )

    def column(k, carry):
        block_y, block_z = k // 2, k % 2
        values = turned_ref[pl.ds(pl.multiple_of(16 * k, 16), 16), 0:48]
        totals = [jnp.zeros((16, 192), F32) for _ in range(4)]
        for c in range(3):
            for x in range(10):
                entry = values[:, 16 * c + x + 3 : 16 * c + x + 4]
                for a in range(4):
                    s = x - 2 * a
                    if 0 <= s < 4:
                        j = 64 * c + 16 * s
                        totals[a] = totals[a] + matrices_ref[a, block_y, block_z, j : j + 16, :] * entry
        for a in range(4):
            solved_ref[pl.ds(8 * a + k, 1), 0:192] = jnp.sum(totals[a], axis=0, keepdims=True)
        return carry

    lax.fori_loop(0, 8, column, 0)
    placed_ref[...] = jnp.zeros((48, 128), F32)
    for a in range(4):
        first = group_transpose(solved_ref[8 * a : 8 * a + 8, 0:128])
        second = group_transpose(solved_ref[8 * a : 8 * a + 8, 128:256])
        for c, piece in enumerate((first[0:4], first[4:8], second[0:4])):
            at = 16 * c + 2 * a + 3
            placed_ref[at : at + 4, :] = placed_ref[at : at + 4, :] + piece
    return dot(placed_ref[...], gather)


SOLVE_SCRATCH = [
    pltpu.VMEM((128, 128), F32),
    pltpu.VMEM((32, 256), F32),
    pltpu.VMEM((48, 128), F32),
]


def sum_rows(value):
    total = value[0:8]
    for at in range(8, value.shape[0], 8):
        total = total + value[at : at + 8]
    return total


def halves(value, low_ref, high_ref):
    for c in range(3):
        low_ref[8 * c : 8 * c + 8, :] = value[16 * c : 16 * c + 8]
        high_ref[8 * c : 8 * c + 8, :] = value[16 * c + 8 : 16 * c + 16]


def joined(low, high):
    parts = []
    for c in range(3):
        parts += [low[8 * c : 8 * c + 8], high[8 * c : 8 * c + 8]]
    return jnp.concatenate(parts, axis=0)


def first_kernel(
    flag_ref, fields_ref, from_below_ref, from_above_ref, matrices_ref,
    residual_ref, movable_ref, low_ref, high_ref, rho_ref,
    turned_ref, solved_ref, placed_ref,
):
    has_below, has_above = flag_ref[2:3, :], flag_ref[3:4, :]
    lane = iota((16, 128), 1)
    below = from_below_ref[0:16, :] * has_below
    above = from_above_ref[0:16, :] * has_above
    at_below = (lane >= 24) & (lane < 32)
    at_above = (lane >= 96) & (lane < 104)
    for field in range(6):
        value = fields_ref[16 * field : 16 * field + 16, :]
        at = 64 + 8 * field
        value = jnp.where(at_below, roll(below, 24 - at, 1), value)
        value = jnp.where(at_above, roll(above, 96 - at, 1), value)
        out_ref = residual_ref if field < 3 else movable_ref
        out_ref[16 * (field % 3) : 16 * (field % 3) + 16, :] = value
    residual = residual_ref[...]
    solved = solve_blocks(residual, matrices_ref, turned_ref, solved_ref, placed_ref) * movable_ref[...]
    halves(solved, low_ref, high_ref)
    rho_ref[...] = sum_rows(residual * solved)


def cross_kernel(flag_ref, low_ref, high_ref, from_left_ref, from_right_ref, low_out, high_out, up_ref, down_ref):
    low = low_ref[...] + from_left_ref[...] * flag_ref[0:1, :]
    high = high_ref[...] + from_right_ref[...] * flag_ref[1:2, :]
    low_out[...] = low
    high_out[...] = high
    lane = iota((24, 128), 1)
    up_ref[...] = jnp.where(lane < 64, roll(low, 64, 1), high)
    down_ref[...] = jnp.where(lane < 64, low, roll(high, 64, 1))


def add_sides(flag_ref, low_ref, high_ref, from_below_ref, from_above_ref):
    lane = iota((24, 128), 1)
    below = from_below_ref[...] * flag_ref[2:3, :]
    above = from_above_ref[...] * flag_ref[3:4, :]
    low = low_ref[...] + jnp.where(lane < 64, below, roll(above, 64, 1))
    high = high_ref[...] + jnp.where(lane < 64, roll(below, 64, 1), above)
    return joined(low, high)


def corner_fields(vector):
    fields = []
    for q in range(8):
        a, b, c_z = q % 2, (q // 2) % 2, q // 4
        for c in range(3):
            value = vector[16 * c : 16 * c + 16]
            if a:
                value = roll(value, -1, 0)
            if b or c_z:
                value = roll(value, -(8 * b + c_z), 1)
            fields.append(value)
    return fields


def push(stiff_ref, stack_ref, rows):
    totals = [None] * len(rows)
    for j in range(24):
        value = stack_ref[16 * j : 16 * j + 16, :]
        for n, i in enumerate(rows):
            product = stiff_ref[24 * j + i : 24 * j + i + 1, :] * value
            totals[n] = product if j == 0 else totals[n] + product
    return totals


def stack_fields(vector, stack_ref):
    for j, value in enumerate(corner_fields(vector)):
        stack_ref[16 * j : 16 * j + 16, :] = value


def global_weights(shape, position, total):
    weight = jnp.zeros(shape, F32)
    for d in range(-3, 4):
        inside = (position + d >= 0) & (position + d < total)
        weight = weight + jnp.where(inside, 4.0 - abs(d), 0.0)
    return weight


def hat(distance):
    return jnp.maximum(0, 4 - jnp.abs(distance)).astype(F32)


def side_kernel(
    sizes, flag_ref, place_ref, matrix_ref, fields_ref, design_ref, from_below_ref, from_above_ref,
    stiff_ref, scale_ref, weight_ref, pushed_ref, stack_ref,
):
    total_x, total_y = sizes
    for j in range(24):
        stiff_ref[24 * j : 24 * j + 24, :] = jnp.broadcast_to(matrix_ref[:, j : j + 1], (24, 128))
    below = from_below_ref[...] * flag_ref[2:3, :]
    above = from_above_ref[...] * flag_ref[3:4, :]
    lane24 = iota((24, 128), 1)
    design = jnp.where(lane24 < 64, design_ref[...], roll(above[0:24], 64, 1))
    row, col = iota((16, 24), 0), iota((16, 24), 1)
    along_x = hat((col - 8) - (row - 4))
    source, target = iota((128, 128), 0), iota((128, 128), 1)
    y_target, z_target = target // 8 - 4, target % 8 - 1
    y_source, z_source = source // 8, source % 8 - 1
    z_valid = (z_target >= 0) & (z_target < NZ) & (z_source >= 0) & (z_source < NZ)
    along_z = jnp.where(z_valid, hat(z_source - z_target), 0.0)
    smooth_in = along_z * hat(y_source - y_target)
    smooth_below = jnp.where(source < 64, along_z * hat(y_source - 8 - y_target), 0.0)
    summed = dot(dot(along_x, design), smooth_in) + dot(dot(along_x, below[0:24]), smooth_below)
    row16, lane16 = iota((16, 128), 0), iota((16, 128), 1)
    z = lane16 % 8 - 1
    x = row16 - 4 + place_ref[0:1, :]
    y = lane16 // 8 - 4 + place_ref[1:2, :]
    shape = (16, 128)
    normalizer = (
        global_weights(shape, x, total_x) * global_weights(shape, y, total_y) * global_weights(shape, z, NZ)
    )
    inside = (x >= 0) & (x < total_x) & (y >= 0) & (y < total_y) & (z >= 0) & (z < NZ)
    normalizer = jnp.where(inside, normalizer, 1.0)
    density = jnp.where(inside, summed / normalizer, 0.0)
    scale_ref[...] = density * density * density
    weight_ref[...] = -3.0 * density * density / normalizer
    lane = iota((16, 128), 1)
    parts = []
    for c in range(3):
        value = fields_ref[96 + 16 * c : 112 + 16 * c, :]
        value = jnp.where(lane < 32, roll(below[24:40], -32 * c, 1), value)
        value = jnp.where(lane >= 96, roll(above[24:40], 96 - 32 * c, 1), value)
        parts.append(value)
    stack_fields(jnp.concatenate(parts, axis=0), stack_ref)
    for i in range(0, 24, 4):
        rows = list(range(i, i + 4))
        for n, value in zip(rows, push(stiff_ref, stack_ref, rows)):
            pushed_ref[16 * n : 16 * n + 16, :] = value


def second_kernel(
    flag_ref, low_ref, high_ref, from_below_ref, from_above_ref, stiff_ref, scale_ref,
    residual_ref, movable_ref, matrices_ref,
    direction_ref, low_out, high_out, sums_ref,
    stack_ref, turned_ref, solved_ref, placed_ref,
):
    direction = add_sides(flag_ref, low_ref, high_ref, from_below_ref, from_above_ref)
    direction_ref[...] = direction
    stack_fields(direction, stack_ref)
    scale = scale_ref[...]
    row16, lane16 = iota((16, 128), 0), iota((16, 128), 1)
    own = (row16 >= 4) & (row16 < 12) & (lane16 >= 32) & (lane16 < 96)
    parts = {}
    energy = jnp.zeros((16, 128), F32)
    for q in range(8):
        a, lanes = q % 2, 8 * ((q // 2) % 2) + q // 4
        rows = [3 * q, 3 * q + 1, 3 * q + 2]
        for c, value in enumerate(push(stiff_ref, stack_ref, rows)):
            value = value * scale
            energy = energy + value * stack_ref[16 * (3 * q + c) : 16 * (3 * q + c) + 16, :]
            if a:
                value = roll(value, 1, 0)
            parts[c, lanes] = parts[c, lanes] + value if (c, lanes) in parts else value
    image = []
    for c in range(3):
        value = parts[c, 0]
        for lanes in (1, 8, 9):
            value = value + roll(parts[c, lanes], lanes, 1)
        image.append(value)
    image = jnp.concatenate(image, axis=0) * movable_ref[...]
    solved = solve_blocks(image, matrices_ref, turned_ref, solved_ref, placed_ref) * movable_ref[...]
    halves(solved, low_out, high_out)
    sums_ref[0:8, :] = sum_rows(jnp.where(own, energy, 0.0))
    sums_ref[8:16, :] = sum_rows(residual_ref[...] * solved)
    sums_ref[16:24, :] = sum_rows(image * solved)


def third_kernel(
    flag_ref, low_ref, high_ref, from_below_ref, from_above_ref, stiff_ref, scale_ref,
    direction_ref, rho_ref, sums_ref,
    wide_ref, share_ref, stack_ref, other_ref,
):
    wide = add_sides(flag_ref, low_ref, high_ref, from_below_ref, from_above_ref)
    wide_ref[...] = wide
    stack_fields(wide, stack_ref)
    stack_fields(direction_ref[...], other_ref)
    row16, lane16 = iota((16, 128), 0), iota((16, 128), 1)
    own = (row16 >= 4) & (row16 < 12) & (lane16 >= 32) & (lane16 < 96)
    scale = jnp.where(own, scale_ref[...], 0.0)
    both = jnp.zeros((16, 128), F32)
    mixed = jnp.zeros((16, 128), F32)
    for i in range(0, 24, 4):
        rows = list(range(i, i + 4))
        for n, value in zip(rows, push(stiff_ref, stack_ref, rows)):
            both = both + value * stack_ref[16 * n : 16 * n + 16, :]
            mixed = mixed + value * other_ref[16 * n : 16 * n + 16, :]
    sums = [
        rho_ref[...], sums_ref[0:8, :], sums_ref[8:16, :], sums_ref[16:24, :],
        sum_rows(mixed * scale), sum_rows(both * scale),
    ]
    lane = iota((1, 128), 1)
    line = jnp.zeros((1, 128), F32)
    for n, value in enumerate(sums):
        total = jnp.sum(jnp.sum(value, axis=0, keepdims=True), axis=1, keepdims=True)
        line = jnp.where(lane == n, total, line)
    share_ref[...] = jnp.broadcast_to(line, share_ref.shape)


def last_kernel(shares_ref, direction_ref, wide_ref, weight_ref, pushed_ref, adjoint_ref, gradient_ref):
    line = jnp.sum(sum_rows(shares_ref[...]), axis=0, keepdims=True)
    lane = iota((1, 128), 1)
    rho, curve, cross, image_wide, mixed, both = [
        jnp.sum(jnp.where(lane == n, line, 0.0), axis=1, keepdims=True) for n in range(6)
    ]
    step = rho / curve
    rho_next = rho - step * (cross + curve) + step * step * image_wide
    grow = 1.0 + rho_next / rho
    curve_next = grow * grow * curve - grow * step * (mixed + image_wide) + step * step * both
    step_next = rho_next / curve_next
    adjoint = (step + step_next * grow) * direction_ref[...] - (step_next * step) * wide_ref[...]
    for z in range(NZ):
        lane_, y = iota((128, 8), 0), iota((128, 8), 1)
        pick = (lane_ == 8 * (y + 4) + z + 1).astype(F32)
        own = jnp.concatenate([adjoint[16 * c + 4 : 16 * c + 12] for c in range(3)], axis=0)
        adjoint_ref[pl.ds(z, 24, stride=NZ), :] = dot(own, pick)
    energy = jnp.zeros((16, 128), F32)
    for j, value in enumerate(corner_fields(adjoint)):
        energy = energy + value * pushed_ref[16 * j : 16 * j + 16, :]
    sensitivity = energy * weight_ref[...]
    row, col = iota((8, 16), 0), iota((8, 16), 1)
    along_x = dot(hat(col - 4 - row), sensitivity)
    source, y = iota((128, 8), 0), iota((128, 8), 1)
    y_source, z_source = source // 8 - 4, source % 8 - 1
    for z in range(NZ):
        valid = (z_source >= 0) & (z_source < NZ)
        along = jnp.where(valid, hat(y_source - y) * hat(z_source - z), 0.0)
        gradient_ref[pl.ds(z, 8, stride=NZ), :] = dot(along_x, along)


def call(kernel, outs, scratch=(), flops=10**6):
    shapes = [jax.ShapeDtypeStruct(shape, F32) for shape in outs]
    return lambda *args: pl.pallas_call(
        kernel,
        out_shape=shapes,
        in_specs=[VM] * len(args),
        out_specs=[VM] * len(shapes),
        scratch_shapes=list(scratch),
        compiler_params=pltpu.CompilerParams(vmem_limit_bytes=VMEM_LIMIT),
        cost_estimate=pl.CostEstimate(flops=flops, bytes_accessed=10**6, transcendentals=0),
    )(*args)


def shifted(value, axis, step):
    size = lax.axis_size(axis)
    return lax.ppermute(value, axis, [(i, (i + step) % size) for i in range(size)])


def both_ways(to_next, to_previous, axis):
    return shifted(to_next, axis, 1), shifted(to_previous, axis, -1)


def as_rows(values):
    return jnp.swapaxes(values, -1, -2).reshape((-1, C))


def from_rows(values, shape):
    return jnp.swapaxes(values.reshape(shape[:-2] + (NZ, C)), -1, -2)


def local(design, element_matrix, fixed, inverses, state, load):
    size_x, size_y = lax.axis_size("gx"), lax.axis_size("gy")
    at_x, at_y = lax.axis_index("gx"), lax.axis_index("gy")
    flags = jnp.stack([at_x > 0, at_x < size_x - 1, at_y > 0, at_y < size_y - 1] + [False] * 4).astype(F32)
    flags = jnp.broadcast_to(flags[:, None], (8, 128))
    place = jnp.stack([at_x * C, at_y * C] + [0 * at_x] * 6).astype(jnp.int32)
    place = jnp.broadcast_to(place[:, None], (8, 128))

    own, to_right, to_left = call(pack_kernel, [(80, 128), (16, 128), (16, 128)])(
        as_rows(load), as_rows(fixed), as_rows(state), as_rows(design)
    )
    left, right = both_ways(to_right, to_left, "gx")
    fields, design_wide, up, down = call(widen_kernel, [(144, 128), (24, 128), (40, 128), (40, 128)])(
        flags, own, left, right
    )
    below, above = both_ways(up, down, "gy")
    residual, movable, low, high, rho = call(
        first_kernel, [(48, 128), (48, 128), (24, 128), (24, 128), (8, 128)], SOLVE_SCRATCH
    )(flags, fields, below, above, inverses)
    stiff, scale, weight, pushed = call(
        functools.partial(side_kernel, (C * size_x, C * size_y)),
        [(576, 128), (16, 128), (16, 128), (384, 128)],
        [pltpu.VMEM((384, 128), F32)],
    )(flags, place, element_matrix, fields, design_wide, below, above)

    def crossed(low, high):
        left, right = both_ways(high, low, "gx")
        low, high, up, down = call(cross_kernel, [(24, 128)] * 4)(flags, low, high, left, right)
        below, above = both_ways(up, down, "gy")
        return low, high, below, above

    sides = crossed(low, high)
    direction, low, high, sums = call(
        second_kernel,
        [(48, 128), (24, 128), (24, 128), (24, 128)],
        [pltpu.VMEM((384, 128), F32)] + SOLVE_SCRATCH,
    )(flags, *sides, stiff, scale, residual, movable, inverses)
    sides = crossed(low, high)
    devices = size_x * size_y
    wide, share = call(
        third_kernel, [(48, 128), (devices, 128)], [pltpu.VMEM((384, 128), F32), pltpu.VMEM((384, 128), F32)]
    )(flags, *sides, stiff, scale, direction, rho, sums)
    shares = lax.all_to_all(share, ("gx", "gy"), 0, 0, tiled=True)
    adjoint, gradient = call(last_kernel, [(96, C), (32, C)])(shares, direction, wide, weight, pushed)
    return from_rows(adjoint, (3, C, C, NZ)), from_rows(gradient, (C, C, NZ))


def solution(mesh):
    placed = (
        P("gx", "gy", None),
        P(),
        P(None, "gx", "gy", None),
        P("gx", "gy", None, None, None),
        P(None, "gx", "gy", None),
        P(None, "gx", "gy", None),
    )
    return jax.shard_map(
        local,
        mesh=mesh,
        in_specs=placed,
        out_specs=(P(None, "gx", "gy", None), P("gx", "gy", None)),
        check_vma=False,
    )
```

```python
import jax
import jax.numpy as jnp
from jax import lax
from jax.experimental import pallas as pl
from jax.experimental.pallas import tpu as pltpu
from jax.sharding import PartitionSpec as P

C = 8
NZ = 4
F32 = jnp.float32
HIGHEST = lax.Precision.HIGHEST
VMEM_LIMIT = 20 * 1024 * 1024
VM = pl.BlockSpec(memory_space=pltpu.VMEM)


def iota(shape, dim):
    return lax.broadcasted_iota(jnp.int32, shape, dim)


def dot(left, right):
    return jnp.dot(left, right, precision=HIGHEST, preferred_element_type=F32)


def roll(value, shift, axis):
    size = value.shape[axis]
    return pltpu.roll(value, shift % size, axis)


def lanes_of(value):
    return iota(value.shape, 1)


def neighbours(axis):
    at = lax.axis_index(axis)
    return (at > 0).astype(F32), (at < lax.axis_size(axis) - 1).astype(F32)


def spread_matrix(z):
    y, lane = iota((8, 128), 0), iota((8, 128), 1)
    return (lane == 8 * (y + 4) + z + 1).astype(F32)


def pack_kernel(inputs_ref, own_ref, right_ref, left_ref):
    own = jnp.zeros((80, 128), F32)
    for z in range(NZ):
        values = inputs_ref[pl.ds(z, 80, stride=NZ), :]
        movable = 1.0 - values[24:48]
        piece = jnp.concatenate([movable * values[0:24], movable, values[48:80]], axis=0)
        own = own + dot(piece, spread_matrix(z))
    own_ref[...] = own
    lane = iota((8, 128), 1)
    row = iota((8, 128), 0)
    design = roll(own[72:80], -32, 1)
    for out_ref, edge, first in ((right_ref, 7, 4), (left_ref, 0, 0)):
        edges = jnp.zeros((8, 128), F32)
        for field in range(6):
            line = own[8 * field + edge : 8 * field + edge + 1]
            edges = jnp.where(row == field, line, edges)
        out_ref[0:8, :] = jnp.where(lane < 64, design, roll(edges, 32, 1))
        upper = [own[48 + 8 * c : 56 + 8 * c] for c in range(3)]
        if first == 4:
            upper = [upper[0], upper[1], upper[2]]
            a = jnp.where(row < 4, roll(upper[0], 4, 0), upper[1])
            b = roll(upper[2], 4, 0)
        else:
            a = jnp.where(row < 4, upper[0], roll(upper[1], 4, 0))
            b = upper[2]
        out_ref[8:16, :] = jnp.where(lane < 64, roll(a, -32, 1), roll(b, 32, 1))


def widen_kernel(own_ref, from_left_ref, from_right_ref, fields_ref, design_ref, up_ref, down_ref):
    has_left, has_right = neighbours("gx")
    lane = iota((8, 128), 1)
    row = iota((8, 128), 0)
    middle = (lane >= 32) & (lane < 96)
    left, right = from_left_ref[...] * has_left, from_right_ref[...] * has_right
    rows_left = jnp.where(middle, roll(left[0:8], -32, 1), 0.0)
    rows_right = jnp.where(middle, roll(right[0:8], -32, 1), 0.0)
    design = jnp.concatenate([left[0:8], roll(own_ref[72:80, :], -32, 1), right[0:8]], axis=0)
    design_ref[...] = design
    tall_lane = iota((24, 128), 1)
    design = jnp.where(tall_lane < 64, design, 0.0)
    edges_up = [jnp.zeros((8, 128), F32), jnp.zeros((8, 128), F32)]
    edges_down = [jnp.zeros((8, 128), F32), jnp.zeros((8, 128), F32)]
    for field in range(6):
        own = own_ref[8 * field : 8 * field + 8, :]
        turned = roll(own, 4, 0)
        low = jnp.where(row >= 4, turned, jnp.where(row == 3, rows_left[field : field + 1], 0.0))
        high = jnp.where(row < 4, turned, jnp.where(row == 4, rows_right[field : field + 1], 0.0))
        fields_ref[16 * field : 16 * field + 8, :] = low
        fields_ref[16 * field + 8 : 16 * field + 16, :] = high
        at = 64 + 8 * field
        place = (lane >= at) & (lane < at + 8)
        for half, value in enumerate((low, high)):
            edges_up[half] = jnp.where(place, roll(value, at - 88, 1), edges_up[half])
            edges_down[half] = jnp.where(place, roll(value, at - 32, 1), edges_down[half])
    zeros = jnp.zeros((8, 128), F32)
    up_ref[0:24, :] = jnp.where(tall_lane < 64, design, jnp.concatenate(edges_up + [zeros], axis=0))
    down_ref[0:24, :] = jnp.where(tall_lane < 64, design, jnp.concatenate(edges_down + [zeros], axis=0))
    state_left, state_right = left[8:16], right[8:16]
    ups = [zeros, zeros]
    downs = [zeros, zeros]
    for c in range(3):
        turned = roll(own_ref[48 + 8 * c : 56 + 8 * c, :], 4, 0)
        lane_turn = 32 if c < 2 else -32
        got_left = jnp.where(middle, roll(state_left, lane_turn, 1), 0.0)
        got_right = jnp.where(middle, roll(state_right, lane_turn, 1), 0.0)
        if c == 1:
            got_left = roll(got_left, 4, 0)
        else:
            got_right = roll(got_right, 4, 0)
        low = jnp.where(row >= 4, turned, got_left)
        high = jnp.where(row < 4, turned, got_right)
        fields_ref[96 + 16 * c : 104 + 16 * c, :] = low
        fields_ref[104 + 16 * c : 112 + 16 * c, :] = high
        place = (lane >= 32 * c) & (lane < 32 * c + 32)
        for half, value in enumerate((low, high)):
            ups[half] = jnp.where(place, roll(value, 32 * c - 64, 1), ups[half])
            downs[half] = jnp.where(place, roll(value, 32 * c - 32, 1), downs[half])
    for half in range(2):
        up_ref[24 + 8 * half : 32 + 8 * half, :] = ups[half]
        down_ref[24 + 8 * half : 32 + 8 * half, :] = downs[half]


def gather_matrix():
    row, lane = iota((128, 128), 0), iota((128, 128), 1)
    block_y, block_z = row // 32, (row // 16) % 2
    t, u = (row // 4) % 4, row % 4
    return (lane == 8 * (2 * block_y + t + 3) + 2 * block_z + u).astype(F32)


def group_transpose(value):
    row, group = iota((8, 128), 0), iota((8, 128), 1) // 16
    for d in (1, 2, 4):
        row_bit, group_bit = (row // d) % 2, (group // d) % 2
        down = roll(roll(value, d, 0), -16 * d, 1)
        up = roll(roll(value, -d, 0), 16 * d, 1)
        moved = jnp.where(row_bit == 1, down, up)
        value = jnp.where(row_bit == group_bit, value, moved)
    return value


def solve_columns(columns, field, matrices_ref, turned_ref, solved_ref):
    turned_ref[:, 0:48] = lax.dot_general(
        gather_matrix(), field, (((1,), (1,)), ((), ())), precision=HIGHEST, preferred_element_type=F32
    )
    for k in columns:
        values = turned_ref[16 * k : 16 * k + 16, 0:48]
        totals = [jnp.zeros((16, 192), F32) for _ in range(4)]
        for c in range(3):
            for x in range(10):
                entry = values[:, 16 * c + x + 3 : 16 * c + x + 4]
                for a in range(4):
                    s = x - 2 * a
                    if 0 <= s < 4:
                        j = 64 * c + 16 * s
                        totals[a] = totals[a] + matrices_ref[a, k // 2, k % 2, j : j + 16, :] * entry
        for a in range(4):
            solved_ref[8 * a + k : 8 * a + k + 1, 0:192] = jnp.sum(
                totals[a][0:8] + totals[a][8:16], axis=0, keepdims=True
            )


def place_blocks(solved_ref, placed_ref):
    placed_ref[...] = jnp.zeros((48, 128), F32)
    for a in range(4):
        first = group_transpose(solved_ref[8 * a : 8 * a + 8, 0:128])
        second = group_transpose(solved_ref[8 * a : 8 * a + 8, 128:256])
        for c, piece in enumerate((first[0:4], first[4:8], second[0:4])):
            at = 16 * c + 2 * a + 3
            placed_ref[at : at + 4, :] = placed_ref[at : at + 4, :] + piece
    return dot(placed_ref[...], gather_matrix())


def solve_blocks(field, matrices_ref, turned_ref, solved_ref, placed_ref):
    solve_columns(range(8), field, matrices_ref, turned_ref, solved_ref)
    return place_blocks(solved_ref, placed_ref)


INNER, OUTER = (2, 3, 4, 5), (0, 1, 6, 7)


def inner_kernel(fields_ref, to_keep_ref, matrices_ref, solved_ref, turned_ref, copied):
    copy = pltpu.make_async_copy(to_keep_ref, matrices_ref, copied)
    copy.start()
    solve_columns(INNER, fields_ref[0:48, :], to_keep_ref, turned_ref, solved_ref)
    copy.wait()


SOLVE_SCRATCH = [
    pltpu.VMEM((128, 128), F32),
    pltpu.VMEM((32, 256), F32),
    pltpu.VMEM((48, 128), F32),
]


def sum_rows(value):
    total = value[0:8]
    for at in range(8, value.shape[0], 8):
        total = total + value[at : at + 8]
    return total


def halves(value, low_ref, high_ref):
    for c in range(3):
        low_ref[8 * c : 8 * c + 8, :] = value[16 * c : 16 * c + 8]
        high_ref[8 * c : 8 * c + 8, :] = value[16 * c + 8 : 16 * c + 16]


def joined(low, high):
    parts = []
    for c in range(3):
        parts += [low[8 * c : 8 * c + 8], high[8 * c : 8 * c + 8]]
    return jnp.concatenate(parts, axis=0)


def first_kernel(
    fields_ref, from_below_ref, from_above_ref, matrices_ref, inner_ref,
    residual_ref, movable_ref, low_ref, high_ref, rho_ref,
    turned_ref, solved_ref, placed_ref,
):
    has_below, has_above = neighbours("gy")
    lane = iota((16, 128), 1)
    below = from_below_ref[0:16, :] * has_below
    above = from_above_ref[0:16, :] * has_above
    at_below = (lane >= 24) & (lane < 32)
    at_above = (lane >= 96) & (lane < 104)
    for field in range(6):
        value = fields_ref[16 * field : 16 * field + 16, :]
        at = 64 + 8 * field
        value = jnp.where(at_below, roll(below, 24 - at, 1), value)
        value = jnp.where(at_above, roll(above, 96 - at, 1), value)
        out_ref = residual_ref if field < 3 else movable_ref
        out_ref[16 * (field % 3) : 16 * (field % 3) + 16, :] = value
    residual = residual_ref[...]
    solved_ref[...] = inner_ref[...]
    solve_columns(OUTER, residual, matrices_ref, turned_ref, solved_ref)
    solved = place_blocks(solved_ref, placed_ref) * movable_ref[...]
    halves(solved, low_ref, high_ref)
    rho_ref[...] = sum_rows(residual * solved)


def cross_kernel(low_ref, high_ref, from_left_ref, from_right_ref, low_out, high_out, up_ref, down_ref):
    has_left, has_right = neighbours("gx")
    low = low_ref[...] + from_left_ref[...] * has_left
    high = high_ref[...] + from_right_ref[...] * has_right
    low_out[...] = low
    high_out[...] = high
    lane = iota((24, 128), 1)
    up_ref[...] = jnp.where(lane < 64, roll(low, 64, 1), high)
    down_ref[...] = jnp.where(lane < 64, low, roll(high, 64, 1))


def add_sides(low_ref, high_ref, from_below_ref, from_above_ref):
    lane = iota((24, 128), 1)
    has_below, has_above = neighbours("gy")
    below = from_below_ref[...] * has_below
    above = from_above_ref[...] * has_above
    low = low_ref[...] + jnp.where(lane < 64, below, roll(above, 64, 1))
    high = high_ref[...] + jnp.where(lane < 64, roll(below, 64, 1), above)
    return joined(low, high)


def corner_fields(vector):
    fields = []
    for q in range(8):
        a, b, c_z = q % 2, (q // 2) % 2, q // 4
        for c in range(3):
            value = vector[16 * c : 16 * c + 16]
            if a:
                value = roll(value, -1, 0)
            if b or c_z:
                value = roll(value, -(8 * b + c_z), 1)
            fields.append(value)
    return fields


def push(stiff_ref, stack_ref, rows):
    totals = [None] * len(rows)
    for j in range(24):
        value = stack_ref[16 * j : 16 * j + 16, :]
        for n, i in enumerate(rows):
            product = stiff_ref[24 * j + i : 24 * j + i + 1, :] * value
            totals[n] = product if j == 0 else totals[n] + product
    return totals


def stack_fields(vector, stack_ref):
    for j, value in enumerate(corner_fields(vector)):
        stack_ref[16 * j : 16 * j + 16, :] = value


def global_weights(shape, position, total):
    weight = jnp.zeros(shape, F32)
    for d in range(-3, 4):
        inside = (position + d >= 0) & (position + d < total)
        weight = weight + jnp.where(inside, 4.0 - abs(d), 0.0)
    return weight


def hat(distance):
    return jnp.maximum(0, 4 - jnp.abs(distance)).astype(F32)


def side_kernel(
    matrix_ref, fields_ref, design_ref, from_below_ref, from_above_ref,
    stiff_ref, scale_ref, weight_ref, pushed_ref, stack_ref,
):
    total_x, total_y = C * lax.axis_size("gx"), C * lax.axis_size("gy")
    for j in range(24):
        stiff_ref[24 * j : 24 * j + 24, :] = jnp.broadcast_to(matrix_ref[:, j : j + 1], (24, 128))
    has_below, has_above = neighbours("gy")
    below = from_below_ref[...] * has_below
    above = from_above_ref[...] * has_above
    lane24 = iota((24, 128), 1)
    design = jnp.where(lane24 < 64, design_ref[...], roll(above[0:24], 64, 1))
    row, col = iota((16, 24), 0), iota((16, 24), 1)
    along_x = hat((col - 8) - (row - 4))
    source, target = iota((128, 128), 0), iota((128, 128), 1)
    y_target, z_target = target // 8 - 4, target % 8 - 1
    y_source, z_source = source // 8, source % 8 - 1
    z_valid = (z_target >= 0) & (z_target < NZ) & (z_source >= 0) & (z_source < NZ)
    along_z = jnp.where(z_valid, hat(z_source - z_target), 0.0)
    smooth_in = along_z * hat(y_source - y_target)
    smooth_below = jnp.where(source < 64, along_z * hat(y_source - 8 - y_target), 0.0)
    summed = dot(dot(along_x, design), smooth_in) + dot(dot(along_x, below[0:24]), smooth_below)
    row16, lane16 = iota((16, 128), 0), iota((16, 128), 1)
    z = lane16 % 8 - 1
    x = row16 - 4 + C * lax.axis_index("gx")
    y = lane16 // 8 - 4 + C * lax.axis_index("gy")
    shape = (16, 128)
    normalizer = (
        global_weights(shape, x, total_x) * global_weights(shape, y, total_y) * global_weights(shape, z, NZ)
    )
    inside = (x >= 0) & (x < total_x) & (y >= 0) & (y < total_y) & (z >= 0) & (z < NZ)
    normalizer = jnp.where(inside, normalizer, 1.0)
    density = jnp.where(inside, summed / normalizer, 0.0)
    scale_ref[...] = density * density * density
    weight_ref[...] = -3.0 * density * density / normalizer
    lane = iota((16, 128), 1)
    parts = []
    for c in range(3):
        value = fields_ref[96 + 16 * c : 112 + 16 * c, :]
        value = jnp.where(lane < 32, roll(below[24:40], -32 * c, 1), value)
        value = jnp.where(lane >= 96, roll(above[24:40], 96 - 32 * c, 1), value)
        parts.append(value)
    stack_fields(jnp.concatenate(parts, axis=0), stack_ref)
    for i in range(0, 24, 4):
        rows = list(range(i, i + 4))
        for n, value in zip(rows, push(stiff_ref, stack_ref, rows)):
            pushed_ref[16 * n : 16 * n + 16, :] = value


def second_kernel(
    low_ref, high_ref, from_below_ref, from_above_ref, stiff_ref, scale_ref,
    residual_ref, movable_ref, matrices_ref,
    direction_ref, low_out, high_out, sums_ref,
    stack_ref, turned_ref, solved_ref, placed_ref,
):
    direction = add_sides(low_ref, high_ref, from_below_ref, from_above_ref)
    direction_ref[...] = direction
    stack_fields(direction, stack_ref)
    scale = scale_ref[...]
    row16, lane16 = iota((16, 128), 0), iota((16, 128), 1)
    own = (row16 >= 4) & (row16 < 12) & (lane16 >= 32) & (lane16 < 96)
    parts = {}
    energy = jnp.zeros((16, 128), F32)
    for q in range(8):
        a, lanes = q % 2, 8 * ((q // 2) % 2) + q // 4
        rows = [3 * q, 3 * q + 1, 3 * q + 2]
        for c, value in enumerate(push(stiff_ref, stack_ref, rows)):
            value = value * scale
            energy = energy + value * stack_ref[16 * (3 * q + c) : 16 * (3 * q + c) + 16, :]
            if a:
                value = roll(value, 1, 0)
            parts[c, lanes] = parts[c, lanes] + value if (c, lanes) in parts else value
    image = []
    for c in range(3):
        value = parts[c, 0]
        for lanes in (1, 8, 9):
            value = value + roll(parts[c, lanes], lanes, 1)
        image.append(value)
    image = jnp.concatenate(image, axis=0) * movable_ref[...]
    solved = solve_blocks(image, matrices_ref, turned_ref, solved_ref, placed_ref) * movable_ref[...]
    halves(solved, low_out, high_out)
    sums_ref[0:8, :] = sum_rows(jnp.where(own, energy, 0.0))
    sums_ref[8:16, :] = sum_rows(residual_ref[...] * solved)
    sums_ref[16:24, :] = sum_rows(image * solved)


def third_kernel(
    low_ref, high_ref, from_below_ref, from_above_ref, stiff_ref, scale_ref,
    direction_ref, rho_ref, sums_ref,
    wide_ref, share_ref, stack_ref, other_ref,
):
    wide = add_sides(low_ref, high_ref, from_below_ref, from_above_ref)
    wide_ref[...] = wide
    stack_fields(wide, stack_ref)
    stack_fields(direction_ref[...], other_ref)
    row16, lane16 = iota((16, 128), 0), iota((16, 128), 1)
    own = (row16 >= 4) & (row16 < 12) & (lane16 >= 32) & (lane16 < 96)
    scale = jnp.where(own, scale_ref[...], 0.0)
    both = jnp.zeros((16, 128), F32)
    mixed = jnp.zeros((16, 128), F32)
    for i in range(0, 24, 4):
        rows = list(range(i, i + 4))
        for n, value in zip(rows, push(stiff_ref, stack_ref, rows)):
            both = both + value * stack_ref[16 * n : 16 * n + 16, :]
            mixed = mixed + value * other_ref[16 * n : 16 * n + 16, :]
    sums = [
        rho_ref[...], sums_ref[0:8, :], sums_ref[8:16, :], sums_ref[16:24, :],
        sum_rows(mixed * scale), sum_rows(both * scale),
    ]
    row, lane = iota((8, 128), 0), iota((8, 128), 1)
    table = jnp.zeros((8, 128), F32)
    for n, value in enumerate(sums):
        table = jnp.where(row == n, jnp.sum(value, axis=0, keepdims=True), table)
    table = jnp.where(row == lane, jnp.sum(table, axis=1, keepdims=True), 0.0)
    share_ref[...] = jnp.broadcast_to(jnp.sum(table, axis=0, keepdims=True), share_ref.shape)


def last_kernel(shares_ref, direction_ref, wide_ref, weight_ref, pushed_ref, adjoint_ref, gradient_ref):
    line = jnp.sum(sum_rows(shares_ref[...]), axis=0, keepdims=True)
    rho, curve, cross, image_wide, mixed, both = [line[:, n : n + 1] for n in range(6)]
    step = rho / curve
    rho_next = rho - step * (cross + curve) + step * step * image_wide
    grow = 1.0 + rho_next / rho
    curve_next = grow * grow * curve - grow * step * (mixed + image_wide) + step * step * both
    step_next = rho_next / curve_next
    adjoint = (step + step_next * grow) * direction_ref[...] - (step_next * step) * wide_ref[...]
    source, target = iota((128, 32), 0), iota((128, 32), 1)
    y, z = target % 8, target // 8
    pick = (source == 8 * (y + 4) + z + 1).astype(F32)
    own = dot(jnp.concatenate([adjoint[16 * c + 4 : 16 * c + 12] for c in range(3)], axis=0), pick)
    for z_out in range(NZ):
        adjoint_ref[pl.ds(z_out, 24, stride=NZ), :] = own[:, 8 * z_out : 8 * z_out + 8]
    energy = jnp.zeros((16, 128), F32)
    for j, value in enumerate(corner_fields(adjoint)):
        energy = energy + value * pushed_ref[16 * j : 16 * j + 16, :]
    sensitivity = energy * weight_ref[...]
    row, col = iota((8, 16), 0), iota((8, 16), 1)
    along_x = dot(hat(col - 4 - row), sensitivity)
    y_source, z_source = source // 8 - 4, source % 8 - 1
    valid = (z_source >= 0) & (z_source < NZ)
    gradient = dot(along_x, jnp.where(valid, hat(y_source - y) * hat(z_source - z), 0.0))
    for z_out in range(NZ):
        gradient_ref[pl.ds(z_out, 8, stride=NZ), :] = gradient[:, 8 * z_out : 8 * z_out + 8]


def call(kernel, outs, scratch=(), flops=10**6):
    shapes = [jax.ShapeDtypeStruct(shape, F32) for shape in outs]
    return lambda *args: pl.pallas_call(
        kernel,
        out_shape=shapes,
        in_specs=[VM] * len(args),
        out_specs=[VM] * len(shapes),
        scratch_shapes=list(scratch),
        compiler_params=pltpu.CompilerParams(vmem_limit_bytes=VMEM_LIMIT),
        cost_estimate=pl.CostEstimate(flops=flops, bytes_accessed=10**6, transcendentals=0),
    )(*args)


def shifted(value, axis, step):
    size = lax.axis_size(axis)
    return lax.ppermute(value, axis, [(i, (i + step) % size) for i in range(size)])


def both_ways(to_next, to_previous, axis):
    return shifted(to_next, axis, 1), shifted(to_previous, axis, -1)


def as_rows(values):
    return jnp.swapaxes(values, -1, -2).reshape((-1, C))


def from_rows(values, shape):
    return jnp.swapaxes(values.reshape(shape[:-2] + (NZ, C)), -1, -2)


def local(design, element_matrix, fixed, inverses, state, load):
    size_x, size_y = lax.axis_size("gx"), lax.axis_size("gy")
    inputs = sum(
        jnp.pad(value, [(first, 10 - first - value.shape[0])] + [(0, 0)] * 3)
        for first, value in ((0, load), (6, state), (9, design[None]))
    )
    inputs = inputs + jnp.pad(fixed, [(3, 4)] + [(0, 0)] * 3).astype(F32)
    own, to_right, to_left = call(pack_kernel, [(80, 128), (16, 128), (16, 128)])(as_rows(inputs))
    left, right = both_ways(to_right, to_left, "gx")
    fields, design_wide, up, down = call(widen_kernel, [(144, 128), (24, 128), (40, 128), (40, 128)])(
        own, left, right
    )
    below, above = both_ways(up, down, "gy")
    matrices, solved = call(
        inner_kernel,
        [inverses.shape, (32, 256)],
        [pltpu.VMEM((128, 128), F32), pltpu.SemaphoreType.DMA],
    )(fields, inverses)
    residual, movable, low, high, rho = call(
        first_kernel, [(48, 128), (48, 128), (24, 128), (24, 128), (8, 128)], SOLVE_SCRATCH
    )(fields, below, above, matrices, solved)
    stiff, scale, weight, pushed = call(
        side_kernel,
        [(576, 128), (16, 128), (16, 128), (384, 128)],
        [pltpu.VMEM((384, 128), F32)],
    )(element_matrix, fields, design_wide, below, above)

    def crossed(low, high):
        left, right = both_ways(high, low, "gx")
        low, high, up, down = call(cross_kernel, [(24, 128)] * 4)(low, high, left, right)
        below, above = both_ways(up, down, "gy")
        return low, high, below, above

    sides = crossed(low, high)
    direction, low, high, sums = call(
        second_kernel,
        [(48, 128), (24, 128), (24, 128), (24, 128)],
        [pltpu.VMEM((384, 128), F32)] + SOLVE_SCRATCH,
    )(*sides, stiff, scale, residual, movable, matrices)
    sides = crossed(low, high)
    devices = size_x * size_y
    wide, share = call(
        third_kernel, [(48, 128), (devices, 128)], [pltpu.VMEM((384, 128), F32), pltpu.VMEM((384, 128), F32)]
    )(*sides, stiff, scale, direction, rho, sums)
    shares = lax.all_to_all(share, ("gx", "gy"), 0, 0, tiled=True)
    adjoint, gradient = call(last_kernel, [(96, C), (32, C)])(shares, direction, wide, weight, pushed)
    return from_rows(adjoint, (3, C, C, NZ)), from_rows(gradient, (C, C, NZ))


def solution(mesh):
    placed = (
        P("gx", "gy", None),
        P(),
        P(None, "gx", "gy", None),
        P("gx", "gy", None, None, None),
        P(None, "gx", "gy", None),
        P(None, "gx", "gy", None),
    )
    return jax.shard_map(
        local,
        mesh=mesh,
        in_specs=placed,
        out_specs=(P(None, "gx", "gy", None), P("gx", "gy", None)),
        check_vma=False,
    )
```

```python
import jax
import jax.numpy as jnp
from jax import lax
from jax.experimental import pallas as pl
from jax.experimental.pallas import tpu as pltpu
from jax.sharding import PartitionSpec as P

C = 8
NZ = 4
F32 = jnp.float32
HIGHEST = lax.Precision.HIGHEST
VMEM_LIMIT = 20 * 1024 * 1024
INNER_LIMIT = 44 * 1024 * 1024
VM = pl.BlockSpec(memory_space=pltpu.VMEM)


def iota(shape, dim):
    return lax.broadcasted_iota(jnp.int32, shape, dim)


def dot(left, right):
    return jnp.dot(left, right, precision=HIGHEST, preferred_element_type=F32)


def roll(value, shift, axis):
    size = value.shape[axis]
    return pltpu.roll(value, shift % size, axis)


def lanes_of(value):
    return iota(value.shape, 1)


def neighbours(axis):
    at = lax.axis_index(axis)
    return (at > 0).astype(F32), (at < lax.axis_size(axis) - 1).astype(F32)


def is_even():
    return lax.axis_index("gy") % 2 == 0


def write_pair(even_ref, odd_ref, rows, up, down):
    even_ref[rows, :] = jnp.where(is_even(), up, down)
    odd_ref[rows, :] = jnp.where(is_even(), down, up)


def read_pair(even_ref, odd_ref):
    even, odd = even_ref[...], odd_ref[...]
    has_below, has_above = neighbours("gy")
    return jnp.where(is_even(), odd, even) * has_below, jnp.where(is_even(), even, odd) * has_above


def spread_matrix(z):
    y, lane = iota((8, 128), 0), iota((8, 128), 1)
    return (lane == 8 * (y + 4) + z + 1).astype(F32)


def pack_kernel(inputs_ref, own_ref, right_ref, left_ref):
    own = jnp.zeros((80, 128), F32)
    for z in range(NZ):
        values = inputs_ref[pl.ds(z, 80, stride=NZ), :]
        movable = 1.0 - values[24:48]
        piece = jnp.concatenate([movable * values[0:24], movable, values[48:80]], axis=0)
        own = own + dot(piece, spread_matrix(z))
    own_ref[...] = own
    lane = iota((8, 128), 1)
    row = iota((8, 128), 0)
    design = roll(own[72:80], -32, 1)
    for out_ref, edge, first in ((right_ref, 7, 4), (left_ref, 0, 0)):
        edges = jnp.zeros((8, 128), F32)
        for field in range(6):
            line = own[8 * field + edge : 8 * field + edge + 1]
            edges = jnp.where(row == field, line, edges)
        out_ref[0:8, :] = jnp.where(lane < 64, design, roll(edges, 32, 1))
        upper = [own[48 + 8 * c : 56 + 8 * c] for c in range(3)]
        if first == 4:
            upper = [upper[0], upper[1], upper[2]]
            a = jnp.where(row < 4, roll(upper[0], 4, 0), upper[1])
            b = roll(upper[2], 4, 0)
        else:
            a = jnp.where(row < 4, upper[0], roll(upper[1], 4, 0))
            b = upper[2]
        out_ref[8:16, :] = jnp.where(lane < 64, roll(a, -32, 1), roll(b, 32, 1))


def widen_kernel(own_ref, from_left_ref, from_right_ref, fields_ref, design_ref, even_ref, odd_ref):
    has_left, has_right = neighbours("gx")
    lane = iota((8, 128), 1)
    row = iota((8, 128), 0)
    middle = (lane >= 32) & (lane < 96)
    left, right = from_left_ref[...] * has_left, from_right_ref[...] * has_right
    rows_left = jnp.where(middle, roll(left[0:8], -32, 1), 0.0)
    rows_right = jnp.where(middle, roll(right[0:8], -32, 1), 0.0)
    design = jnp.concatenate([left[0:8], roll(own_ref[72:80, :], -32, 1), right[0:8]], axis=0)
    design_ref[...] = design
    tall_lane = iota((24, 128), 1)
    design = jnp.where(tall_lane < 64, design, 0.0)
    edges_up = [jnp.zeros((8, 128), F32), jnp.zeros((8, 128), F32)]
    edges_down = [jnp.zeros((8, 128), F32), jnp.zeros((8, 128), F32)]
    for field in range(6):
        own = own_ref[8 * field : 8 * field + 8, :]
        turned = roll(own, 4, 0)
        low = jnp.where(row >= 4, turned, jnp.where(row == 3, rows_left[field : field + 1], 0.0))
        high = jnp.where(row < 4, turned, jnp.where(row == 4, rows_right[field : field + 1], 0.0))
        fields_ref[16 * field : 16 * field + 8, :] = low
        fields_ref[16 * field + 8 : 16 * field + 16, :] = high
        at = 64 + 8 * field
        place = (lane >= at) & (lane < at + 8)
        for half, value in enumerate((low, high)):
            edges_up[half] = jnp.where(place, roll(value, at - 88, 1), edges_up[half])
            edges_down[half] = jnp.where(place, roll(value, at - 32, 1), edges_down[half])
    zeros = jnp.zeros((8, 128), F32)
    write_pair(
        even_ref, odd_ref, slice(0, 24),
        jnp.where(tall_lane < 64, design, jnp.concatenate(edges_up + [zeros], axis=0)),
        jnp.where(tall_lane < 64, design, jnp.concatenate(edges_down + [zeros], axis=0)),
    )
    state_left, state_right = left[8:16], right[8:16]
    ups = [zeros, zeros]
    downs = [zeros, zeros]
    for c in range(3):
        turned = roll(own_ref[48 + 8 * c : 56 + 8 * c, :], 4, 0)
        lane_turn = 32 if c < 2 else -32
        got_left = jnp.where(middle, roll(state_left, lane_turn, 1), 0.0)
        got_right = jnp.where(middle, roll(state_right, lane_turn, 1), 0.0)
        if c == 1:
            got_left = roll(got_left, 4, 0)
        else:
            got_right = roll(got_right, 4, 0)
        low = jnp.where(row >= 4, turned, got_left)
        high = jnp.where(row < 4, turned, got_right)
        fields_ref[96 + 16 * c : 104 + 16 * c, :] = low
        fields_ref[104 + 16 * c : 112 + 16 * c, :] = high
        place = (lane >= 32 * c) & (lane < 32 * c + 32)
        for half, value in enumerate((low, high)):
            ups[half] = jnp.where(place, roll(value, 32 * c - 64, 1), ups[half])
            downs[half] = jnp.where(place, roll(value, 32 * c - 32, 1), downs[half])
    for half in range(2):
        write_pair(even_ref, odd_ref, slice(24 + 8 * half, 32 + 8 * half), ups[half], downs[half])


def gather_matrix():
    row, lane = iota((128, 128), 0), iota((128, 128), 1)
    block_y, block_z = row // 32, (row // 16) % 2
    t, u = (row // 4) % 4, row % 4
    return (lane == 8 * (2 * block_y + t + 3) + 2 * block_z + u).astype(F32)


def group_transpose(value):
    row, group = iota((8, 128), 0), iota((8, 128), 1) // 16
    for d in (1, 2, 4):
        row_bit, group_bit = (row // d) % 2, (group // d) % 2
        down = roll(roll(value, d, 0), -16 * d, 1)
        up = roll(roll(value, -d, 0), 16 * d, 1)
        moved = jnp.where(row_bit == 1, down, up)
        value = jnp.where(row_bit == group_bit, value, moved)
    return value


def turn(field, turned_ref):
    turned_ref[:, 0:48] = lax.dot_general(
        gather_matrix(), field, (((1,), (1,)), ((), ())), precision=HIGHEST, preferred_element_type=F32
    )


def solve_column(k, matrices_ref, turned_ref, solved_ref):
    values = turned_ref[16 * k : 16 * k + 16, 0:48]
    totals = [jnp.zeros((16, 192), F32) for _ in range(4)]
    for c in range(3):
        for x in range(10):
            entry = values[:, 16 * c + x + 3 : 16 * c + x + 4]
            for a in range(4):
                s = x - 2 * a
                if 0 <= s < 4:
                    j = 64 * c + 16 * s
                    totals[a] = totals[a] + matrices_ref[a, k // 2, k % 2, j : j + 16, :] * entry
    for a in range(4):
        solved_ref[8 * a + k : 8 * a + k + 1, 0:192] = jnp.sum(
            totals[a][0:8] + totals[a][8:16], axis=0, keepdims=True
        )


def solve_columns(columns, field, matrices_ref, turned_ref, solved_ref):
    turn(field, turned_ref)
    for k in columns:
        solve_column(k, matrices_ref, turned_ref, solved_ref)


def place_blocks(solved_ref, placed_ref):
    placed_ref[...] = jnp.zeros((48, 128), F32)
    for a in range(4):
        first = group_transpose(solved_ref[8 * a : 8 * a + 8, 0:128])
        second = group_transpose(solved_ref[8 * a : 8 * a + 8, 128:256])
        for c, piece in enumerate((first[0:4], first[4:8], second[0:4])):
            at = 16 * c + 2 * a + 3
            placed_ref[at : at + 4, :] = placed_ref[at : at + 4, :] + piece
    return dot(placed_ref[...], gather_matrix())


def solve_blocks(field, matrices_ref, turned_ref, solved_ref, placed_ref):
    solve_columns(range(8), field, matrices_ref, turned_ref, solved_ref)
    return place_blocks(solved_ref, placed_ref)


INNER, OUTER = (2, 3, 4, 5), (0, 1, 6, 7)


def inner_kernel(fields_ref, stored_ref, matrices_ref, solved_ref, turned_ref, arrived):
    copies = {}
    for k in INNER + OUTER:
        at = (slice(None), k // 2, k % 2)
        copies[k] = pltpu.make_async_copy(stored_ref.at[at], matrices_ref.at[at], arrived.at[k])
        copies[k].start()
    turn(fields_ref[0:48, :], turned_ref)
    for k in INNER:
        copies[k].wait()
        solve_column(k, matrices_ref, turned_ref, solved_ref)
    for k in OUTER:
        copies[k].wait()


SOLVE_SCRATCH = [
    pltpu.VMEM((128, 128), F32),
    pltpu.VMEM((32, 256), F32),
    pltpu.VMEM((48, 128), F32),
]


def sum_rows(value):
    total = value[0:8]
    for at in range(8, value.shape[0], 8):
        total = total + value[at : at + 8]
    return total


def halves(value, low_ref, high_ref):
    for c in range(3):
        low_ref[8 * c : 8 * c + 8, :] = value[16 * c : 16 * c + 8]
        high_ref[8 * c : 8 * c + 8, :] = value[16 * c + 8 : 16 * c + 16]


def joined(low, high):
    parts = []
    for c in range(3):
        parts += [low[8 * c : 8 * c + 8], high[8 * c : 8 * c + 8]]
    return jnp.concatenate(parts, axis=0)


def first_kernel(
    fields_ref, even_ref, odd_ref, matrices_ref, inner_ref,
    residual_ref, movable_ref, low_ref, high_ref, rho_ref,
    turned_ref, solved_ref, placed_ref,
):
    lane = iota((16, 128), 1)
    below, above = [value[0:16] for value in read_pair(even_ref, odd_ref)]
    at_below = (lane >= 24) & (lane < 32)
    at_above = (lane >= 96) & (lane < 104)
    for field in range(6):
        value = fields_ref[16 * field : 16 * field + 16, :]
        at = 64 + 8 * field
        value = jnp.where(at_below, roll(below, 24 - at, 1), value)
        value = jnp.where(at_above, roll(above, 96 - at, 1), value)
        out_ref = residual_ref if field < 3 else movable_ref
        out_ref[16 * (field % 3) : 16 * (field % 3) + 16, :] = value
    residual = residual_ref[...]
    solved_ref[...] = inner_ref[...]
    solve_columns(OUTER, residual, matrices_ref, turned_ref, solved_ref)
    solved = place_blocks(solved_ref, placed_ref) * movable_ref[...]
    halves(solved, low_ref, high_ref)
    rho_ref[...] = sum_rows(residual * solved)


def cross_kernel(low_ref, high_ref, from_left_ref, from_right_ref, low_out, high_out, even_ref, odd_ref):
    has_left, has_right = neighbours("gx")
    low = low_ref[...] + from_left_ref[...] * has_left
    high = high_ref[...] + from_right_ref[...] * has_right
    low_out[...] = low
    high_out[...] = high
    lane = iota((24, 128), 1)
    write_pair(
        even_ref, odd_ref, slice(0, 24),
        jnp.where(lane < 64, roll(low, 64, 1), high),
        jnp.where(lane < 64, low, roll(high, 64, 1)),
    )


def add_sides(low_ref, high_ref, even_ref, odd_ref):
    lane = iota((24, 128), 1)
    below, above = read_pair(even_ref, odd_ref)
    low = low_ref[...] + jnp.where(lane < 64, below, roll(above, 64, 1))
    high = high_ref[...] + jnp.where(lane < 64, roll(below, 64, 1), above)
    return joined(low, high)


def corner_fields(vector):
    fields = []
    for q in range(8):
        a, b, c_z = q % 2, (q // 2) % 2, q // 4
        for c in range(3):
            value = vector[16 * c : 16 * c + 16]
            if a:
                value = roll(value, -1, 0)
            if b or c_z:
                value = roll(value, -(8 * b + c_z), 1)
            fields.append(value)
    return fields


def push(stiff_ref, stack_ref, rows):
    totals = [None] * len(rows)
    for j in range(24):
        value = stack_ref[16 * j : 16 * j + 16, :]
        for n, i in enumerate(rows):
            product = stiff_ref[24 * j + i : 24 * j + i + 1, :] * value
            totals[n] = product if j == 0 else totals[n] + product
    return totals


def stack_fields(vector, stack_ref):
    for j, value in enumerate(corner_fields(vector)):
        stack_ref[16 * j : 16 * j + 16, :] = value


def global_weights(shape, position, total):
    weight = jnp.zeros(shape, F32)
    for d in range(-3, 4):
        inside = (position + d >= 0) & (position + d < total)
        weight = weight + jnp.where(inside, 4.0 - abs(d), 0.0)
    return weight


def hat(distance):
    return jnp.maximum(0, 4 - jnp.abs(distance)).astype(F32)


def side_kernel(
    matrix_ref, fields_ref, design_ref, even_ref, odd_ref,
    stiff_ref, scale_ref, weight_ref, pushed_ref, stack_ref,
):
    total_x, total_y = C * lax.axis_size("gx"), C * lax.axis_size("gy")
    for j in range(24):
        stiff_ref[24 * j : 24 * j + 24, :] = jnp.broadcast_to(matrix_ref[:, j : j + 1], (24, 128))
    below, above = read_pair(even_ref, odd_ref)
    lane24 = iota((24, 128), 1)
    design = jnp.where(lane24 < 64, design_ref[...], roll(above[0:24], 64, 1))
    row, col = iota((16, 24), 0), iota((16, 24), 1)
    along_x = hat((col - 8) - (row - 4))
    source, target = iota((128, 128), 0), iota((128, 128), 1)
    y_target, z_target = target // 8 - 4, target % 8 - 1
    y_source, z_source = source // 8, source % 8 - 1
    z_valid = (z_target >= 0) & (z_target < NZ) & (z_source >= 0) & (z_source < NZ)
    along_z = jnp.where(z_valid, hat(z_source - z_target), 0.0)
    smooth_in = along_z * hat(y_source - y_target)
    smooth_below = jnp.where(source < 64, along_z * hat(y_source - 8 - y_target), 0.0)
    summed = dot(dot(along_x, design), smooth_in) + dot(dot(along_x, below[0:24]), smooth_below)
    row16, lane16 = iota((16, 128), 0), iota((16, 128), 1)
    z = lane16 % 8 - 1
    x = row16 - 4 + C * lax.axis_index("gx")
    y = lane16 // 8 - 4 + C * lax.axis_index("gy")
    shape = (16, 128)
    normalizer = (
        global_weights(shape, x, total_x) * global_weights(shape, y, total_y) * global_weights(shape, z, NZ)
    )
    inside = (x >= 0) & (x < total_x) & (y >= 0) & (y < total_y) & (z >= 0) & (z < NZ)
    normalizer = jnp.where(inside, normalizer, 1.0)
    density = jnp.where(inside, summed / normalizer, 0.0)
    scale_ref[...] = density * density * density
    weight_ref[...] = -3.0 * density * density / normalizer
    lane = iota((16, 128), 1)
    parts = []
    for c in range(3):
        value = fields_ref[96 + 16 * c : 112 + 16 * c, :]
        value = jnp.where(lane < 32, roll(below[24:40], -32 * c, 1), value)
        value = jnp.where(lane >= 96, roll(above[24:40], 96 - 32 * c, 1), value)
        parts.append(value)
    stack_fields(jnp.concatenate(parts, axis=0), stack_ref)
    for i in range(0, 24, 4):
        rows = list(range(i, i + 4))
        for n, value in zip(rows, push(stiff_ref, stack_ref, rows)):
            pushed_ref[16 * n : 16 * n + 16, :] = value


def second_kernel(
    low_ref, high_ref, even_ref, odd_ref, stiff_ref, scale_ref,
    residual_ref, movable_ref, matrices_ref,
    direction_ref, low_out, high_out, sums_ref,
    stack_ref, turned_ref, solved_ref, placed_ref,
):
    direction = add_sides(low_ref, high_ref, even_ref, odd_ref)
    direction_ref[...] = direction
    stack_fields(direction, stack_ref)
    scale = scale_ref[...]
    row16, lane16 = iota((16, 128), 0), iota((16, 128), 1)
    own = (row16 >= 4) & (row16 < 12) & (lane16 >= 32) & (lane16 < 96)
    parts = {}
    energy = jnp.zeros((16, 128), F32)
    for q in range(8):
        a, lanes = q % 2, 8 * ((q // 2) % 2) + q // 4
        rows = [3 * q, 3 * q + 1, 3 * q + 2]
        for c, value in enumerate(push(stiff_ref, stack_ref, rows)):
            value = value * scale
            energy = energy + value * stack_ref[16 * (3 * q + c) : 16 * (3 * q + c) + 16, :]
            if a:
                value = roll(value, 1, 0)
            parts[c, lanes] = parts[c, lanes] + value if (c, lanes) in parts else value
    image = []
    for c in range(3):
        value = parts[c, 0]
        for lanes in (1, 8, 9):
            value = value + roll(parts[c, lanes], lanes, 1)
        image.append(value)
    image = jnp.concatenate(image, axis=0) * movable_ref[...]
    solved = solve_blocks(image, matrices_ref, turned_ref, solved_ref, placed_ref) * movable_ref[...]
    halves(solved, low_out, high_out)
    sums_ref[0:8, :] = sum_rows(jnp.where(own, energy, 0.0))
    sums_ref[8:16, :] = sum_rows(residual_ref[...] * solved)
    sums_ref[16:24, :] = sum_rows(image * solved)


def third_kernel(
    low_ref, high_ref, even_ref, odd_ref, stiff_ref, scale_ref,
    direction_ref, rho_ref, sums_ref,
    wide_ref, share_ref, stack_ref, other_ref,
):
    wide = add_sides(low_ref, high_ref, even_ref, odd_ref)
    wide_ref[...] = wide
    stack_fields(wide, stack_ref)
    stack_fields(direction_ref[...], other_ref)
    row16, lane16 = iota((16, 128), 0), iota((16, 128), 1)
    own = (row16 >= 4) & (row16 < 12) & (lane16 >= 32) & (lane16 < 96)
    scale = jnp.where(own, scale_ref[...], 0.0)
    both = jnp.zeros((16, 128), F32)
    mixed = jnp.zeros((16, 128), F32)
    for i in range(0, 24, 4):
        rows = list(range(i, i + 4))
        for n, value in zip(rows, push(stiff_ref, stack_ref, rows)):
            both = both + value * stack_ref[16 * n : 16 * n + 16, :]
            mixed = mixed + value * other_ref[16 * n : 16 * n + 16, :]
    sums = [
        rho_ref[...], sums_ref[0:8, :], sums_ref[8:16, :], sums_ref[16:24, :],
        sum_rows(mixed * scale), sum_rows(both * scale),
    ]
    row, lane = iota((8, 128), 0), iota((8, 128), 1)
    table = jnp.zeros((8, 128), F32)
    for n, value in enumerate(sums):
        table = jnp.where(row == n, jnp.sum(value, axis=0, keepdims=True), table)
    table = jnp.where(row == lane, jnp.sum(table, axis=1, keepdims=True), 0.0)
    share_ref[...] = jnp.broadcast_to(jnp.sum(table, axis=0, keepdims=True), share_ref.shape)


def last_kernel(shares_ref, direction_ref, wide_ref, weight_ref, pushed_ref, adjoint_ref, gradient_ref):
    line = jnp.sum(sum_rows(shares_ref[...]), axis=0, keepdims=True)
    rho, curve, cross, image_wide, mixed, both = [line[:, n : n + 1] for n in range(6)]
    step = rho / curve
    rho_next = rho - step * (cross + curve) + step * step * image_wide
    grow = 1.0 + rho_next / rho
    curve_next = grow * grow * curve - grow * step * (mixed + image_wide) + step * step * both
    step_next = rho_next / curve_next
    adjoint = (step + step_next * grow) * direction_ref[...] - (step_next * step) * wide_ref[...]
    source, target = iota((128, 32), 0), iota((128, 32), 1)
    y, z = target % 8, target // 8
    pick = (source == 8 * (y + 4) + z + 1).astype(F32)
    own = dot(jnp.concatenate([adjoint[16 * c + 4 : 16 * c + 12] for c in range(3)], axis=0), pick)
    for z_out in range(NZ):
        adjoint_ref[pl.ds(z_out, 24, stride=NZ), :] = own[:, 8 * z_out : 8 * z_out + 8]
    energy = jnp.zeros((16, 128), F32)
    for j, value in enumerate(corner_fields(adjoint)):
        energy = energy + value * pushed_ref[16 * j : 16 * j + 16, :]
    sensitivity = energy * weight_ref[...]
    row, col = iota((8, 16), 0), iota((8, 16), 1)
    along_x = dot(hat(col - 4 - row), sensitivity)
    y_source, z_source = source // 8 - 4, source % 8 - 1
    valid = (z_source >= 0) & (z_source < NZ)
    gradient = dot(along_x, jnp.where(valid, hat(y_source - y) * hat(z_source - z), 0.0))
    for z_out in range(NZ):
        gradient_ref[pl.ds(z_out, 8, stride=NZ), :] = gradient[:, 8 * z_out : 8 * z_out + 8]


def call(kernel, outs, scratch=(), specs=None, limit=VMEM_LIMIT):
    shapes = [jax.ShapeDtypeStruct(shape, F32) for shape in outs]
    return lambda *args: pl.pallas_call(
        kernel,
        out_shape=shapes,
        in_specs=specs or [VM] * len(args),
        out_specs=[VM] * len(shapes),
        scratch_shapes=list(scratch),
        compiler_params=pltpu.CompilerParams(vmem_limit_bytes=limit),
        cost_estimate=pl.CostEstimate(flops=10**6, bytes_accessed=10**6, transcendentals=0),
    )(*args)


def shifted(value, axis, step):
    size = lax.axis_size(axis)
    return lax.ppermute(value, axis, [(i, (i + step) % size) for i in range(size)])


def both_ways(to_next, to_previous, axis):
    return shifted(to_next, axis, 1), shifted(to_previous, axis, -1)


def paired(even, odd):
    size_x, size_y = lax.axis_size("gx"), lax.axis_size("gy")
    pairs = []
    for i in range(size_x):
        for j in range(size_y):
            inside = 0 < j < size_y - 1
            other = (i, j + 1 if j % 2 else j - 1) if inside else (i ^ 1, j)
            pairs.append((i * size_y + j, other[0] * size_y + other[1]))
    from_even = lax.ppermute(even, "gy", [(j, j ^ 1) for j in range(size_y)])
    return from_even, lax.ppermute(odd, ("gx", "gy"), pairs)


def as_rows(values):
    return jnp.swapaxes(values, -1, -2).reshape((-1, C))


def from_rows(values, shape):
    return jnp.swapaxes(values.reshape(shape[:-2] + (NZ, C)), -1, -2)


def local(design, element_matrix, fixed, inverses, state, load):
    size_x, size_y = lax.axis_size("gx"), lax.axis_size("gy")
    inputs = sum(
        jnp.pad(value, [(first, 10 - first - value.shape[0])] + [(0, 0)] * 3)
        for first, value in ((0, load), (6, state), (9, design[None]))
    )
    inputs = inputs + jnp.pad(fixed, [(3, 4)] + [(0, 0)] * 3).astype(F32)
    own, to_right, to_left = call(pack_kernel, [(80, 128), (16, 128), (16, 128)])(as_rows(inputs))
    left, right = both_ways(to_right, to_left, "gx")
    fields, design_wide, even, odd = call(widen_kernel, [(144, 128), (24, 128), (40, 128), (40, 128)])(
        own, left, right
    )
    even, odd = paired(even, odd)
    matrices, solved = call(
        inner_kernel,
        [inverses.shape, (32, 256)],
        [pltpu.VMEM((128, 128), F32), pltpu.SemaphoreType.DMA((8,))],
        [VM, pl.BlockSpec(memory_space=pl.ANY)],
        INNER_LIMIT,
    )(fields, inverses)
    residual, movable, low, high, rho = call(
        first_kernel, [(48, 128), (48, 128), (24, 128), (24, 128), (8, 128)], SOLVE_SCRATCH
    )(fields, even, odd, matrices, solved)
    stiff, scale, weight, pushed = call(
        side_kernel,
        [(576, 128), (16, 128), (16, 128), (384, 128)],
        [pltpu.VMEM((384, 128), F32)],
    )(element_matrix, fields, design_wide, even, odd)

    def crossed(low, high):
        left, right = both_ways(high, low, "gx")
        low, high, even, odd = call(cross_kernel, [(24, 128)] * 4)(low, high, left, right)
        return low, high, *paired(even, odd)

    sides = crossed(low, high)
    direction, low, high, sums = call(
        second_kernel,
        [(48, 128), (24, 128), (24, 128), (24, 128)],
        [pltpu.VMEM((384, 128), F32)] + SOLVE_SCRATCH,
    )(*sides, stiff, scale, residual, movable, matrices)
    sides = crossed(low, high)
    devices = size_x * size_y
    wide, share = call(
        third_kernel, [(48, 128), (devices, 128)], [pltpu.VMEM((384, 128), F32), pltpu.VMEM((384, 128), F32)]
    )(*sides, stiff, scale, direction, rho, sums)
    shares = lax.all_to_all(share, ("gx", "gy"), 0, 0, tiled=True)
    adjoint, gradient = call(last_kernel, [(96, C), (32, C)])(shares, direction, wide, weight, pushed)
    return from_rows(adjoint, (3, C, C, NZ)), from_rows(gradient, (C, C, NZ))


def solution(mesh):
    placed = (
        P("gx", "gy", None),
        P(),
        P(None, "gx", "gy", None),
        P("gx", "gy", None, None, None),
        P(None, "gx", "gy", None),
        P(None, "gx", "gy", None),
    )
    return jax.shard_map(
        local,
        mesh=mesh,
        in_specs=placed,
        out_specs=(P(None, "gx", "gy", None), P("gx", "gy", None)),
        check_vma=False,
    )
```

```python
import jax
import jax.numpy as jnp
from jax import lax
from jax.experimental import pallas as pl
from jax.experimental.pallas import tpu as pltpu
from jax.sharding import PartitionSpec as P

C = 8
NZ = 4
F32 = jnp.float32
HIGHEST = lax.Precision.HIGHEST
VMEM_LIMIT = 20 * 1024 * 1024
INNER_LIMIT = 44 * 1024 * 1024
VM = pl.BlockSpec(memory_space=pltpu.VMEM)


def iota(shape, dim):
    return lax.broadcasted_iota(jnp.int32, shape, dim)


def dot(left, right):
    return jnp.dot(left, right, precision=HIGHEST, preferred_element_type=F32)


def roll(value, shift, axis):
    size = value.shape[axis]
    return pltpu.roll(value, shift % size, axis)


def lanes_of(value):
    return iota(value.shape, 1)


def neighbours(axis):
    at = lax.axis_index(axis)
    return (at > 0).astype(F32), (at < lax.axis_size(axis) - 1).astype(F32)


def is_even():
    return lax.axis_index("gy") % 2 == 0


def write_pair(even_ref, odd_ref, rows, up, down):
    even_ref[rows, :] = jnp.where(is_even(), up, down)
    odd_ref[rows, :] = jnp.where(is_even(), down, up)


def read_pair(even, odd):
    has_below, has_above = neighbours("gy")
    return jnp.where(is_even(), odd, even) * has_below, jnp.where(is_even(), even, odd) * has_above


def spread_matrix(z):
    y, lane = iota((8, 128), 0), iota((8, 128), 1)
    return (lane == 8 * (y + 4) + z + 1).astype(F32)


def pack_kernel(inputs_ref, own_ref, right_ref, left_ref):
    own = jnp.zeros((80, 128), F32)
    for z in range(NZ):
        values = inputs_ref[pl.ds(z, 80, stride=NZ), :]
        movable = 1.0 - values[24:48]
        piece = jnp.concatenate([movable * values[0:24], movable, values[48:80]], axis=0)
        own = own + dot(piece, spread_matrix(z))
    own_ref[...] = own
    lane = iota((8, 128), 1)
    row = iota((8, 128), 0)
    design = roll(own[72:80], -32, 1)
    for out_ref, edge, first in ((right_ref, 7, 4), (left_ref, 0, 0)):
        edges = jnp.zeros((8, 128), F32)
        for field in range(6):
            line = own[8 * field + edge : 8 * field + edge + 1]
            edges = jnp.where(row == field, line, edges)
        out_ref[0:8, :] = jnp.where(lane < 64, design, roll(edges, 32, 1))
        upper = [own[48 + 8 * c : 56 + 8 * c] for c in range(3)]
        if first == 4:
            upper = [upper[0], upper[1], upper[2]]
            a = jnp.where(row < 4, roll(upper[0], 4, 0), upper[1])
            b = roll(upper[2], 4, 0)
        else:
            a = jnp.where(row < 4, upper[0], roll(upper[1], 4, 0))
            b = upper[2]
        out_ref[8:16, :] = jnp.where(lane < 64, roll(a, -32, 1), roll(b, 32, 1))


def widen_kernel(own_ref, from_left_ref, from_right_ref, fields_ref, design_ref, even_ref, odd_ref):
    has_left, has_right = neighbours("gx")
    lane = iota((8, 128), 1)
    row = iota((8, 128), 0)
    middle = (lane >= 32) & (lane < 96)
    left, right = from_left_ref[...] * has_left, from_right_ref[...] * has_right
    rows_left = jnp.where(middle, roll(left[0:8], -32, 1), 0.0)
    rows_right = jnp.where(middle, roll(right[0:8], -32, 1), 0.0)
    design = jnp.concatenate([left[0:8], roll(own_ref[72:80, :], -32, 1), right[0:8]], axis=0)
    design_ref[...] = design
    tall_lane = iota((24, 128), 1)
    design = jnp.where(tall_lane < 64, design, 0.0)
    edges_up = [jnp.zeros((8, 128), F32), jnp.zeros((8, 128), F32)]
    edges_down = [jnp.zeros((8, 128), F32), jnp.zeros((8, 128), F32)]
    for field in range(6):
        own = own_ref[8 * field : 8 * field + 8, :]
        turned = roll(own, 4, 0)
        low = jnp.where(row >= 4, turned, jnp.where(row == 3, rows_left[field : field + 1], 0.0))
        high = jnp.where(row < 4, turned, jnp.where(row == 4, rows_right[field : field + 1], 0.0))
        fields_ref[16 * field : 16 * field + 8, :] = low
        fields_ref[16 * field + 8 : 16 * field + 16, :] = high
        at = 64 + 8 * field
        place = (lane >= at) & (lane < at + 8)
        for half, value in enumerate((low, high)):
            edges_up[half] = jnp.where(place, roll(value, at - 88, 1), edges_up[half])
            edges_down[half] = jnp.where(place, roll(value, at - 32, 1), edges_down[half])
    zeros = jnp.zeros((8, 128), F32)
    write_pair(
        even_ref, odd_ref, slice(0, 24),
        jnp.where(tall_lane < 64, design, jnp.concatenate(edges_up + [zeros], axis=0)),
        jnp.where(tall_lane < 64, design, jnp.concatenate(edges_down + [zeros], axis=0)),
    )
    state_left, state_right = left[8:16], right[8:16]
    ups = [zeros, zeros]
    downs = [zeros, zeros]
    for c in range(3):
        turned = roll(own_ref[48 + 8 * c : 56 + 8 * c, :], 4, 0)
        lane_turn = 32 if c < 2 else -32
        got_left = jnp.where(middle, roll(state_left, lane_turn, 1), 0.0)
        got_right = jnp.where(middle, roll(state_right, lane_turn, 1), 0.0)
        if c == 1:
            got_left = roll(got_left, 4, 0)
        else:
            got_right = roll(got_right, 4, 0)
        low = jnp.where(row >= 4, turned, got_left)
        high = jnp.where(row < 4, turned, got_right)
        fields_ref[96 + 16 * c : 104 + 16 * c, :] = low
        fields_ref[104 + 16 * c : 112 + 16 * c, :] = high
        place = (lane >= 32 * c) & (lane < 32 * c + 32)
        for half, value in enumerate((low, high)):
            ups[half] = jnp.where(place, roll(value, 32 * c - 64, 1), ups[half])
            downs[half] = jnp.where(place, roll(value, 32 * c - 32, 1), downs[half])
    for half in range(2):
        write_pair(even_ref, odd_ref, slice(24 + 8 * half, 32 + 8 * half), ups[half], downs[half])


def gather_matrix():
    row, lane = iota((128, 128), 0), iota((128, 128), 1)
    block_y, block_z = row // 32, (row // 16) % 2
    t, u = (row // 4) % 4, row % 4
    return (lane == 8 * (2 * block_y + t + 3) + 2 * block_z + u).astype(F32)


def group_transpose(value):
    row, group = iota((8, 128), 0), iota((8, 128), 1) // 16
    for d in (1, 2, 4):
        row_bit, group_bit = (row // d) % 2, (group // d) % 2
        down = roll(roll(value, d, 0), -16 * d, 1)
        up = roll(roll(value, -d, 0), 16 * d, 1)
        moved = jnp.where(row_bit == 1, down, up)
        value = jnp.where(row_bit == group_bit, value, moved)
    return value


def turn(field, turned_ref):
    row, lane = iota((80, 128), 0), iota((80, 128), 1)
    block_z, pair, tt, u = row // 40, (row // 8) % 5, (row // 4) % 2, row % 4
    pick = (lane == 8 * (2 * pair + tt + 3) + 2 * block_z + u).astype(F32)
    turned_ref[:, 0:48] = lax.dot_general(
        pick, field, (((1,), (1,)), ((), ())), precision=HIGHEST, preferred_element_type=F32
    )


def solve_columns(blocks_y, block_z, matrices_ref, turned_ref, solved_ref):
    totals = {}
    for pair in range(5):
        uses = [(block_y, pair - block_y) for block_y in blocks_y if 0 <= pair - block_y < 2]
        at = 40 * block_z + 8 * pair
        values = turned_ref[at : at + 8, 0:48]
        for c in range(3 if uses else 0):
            for x in range(10):
                entry = jnp.broadcast_to(values[:, 16 * c + x + 3 : 16 * c + x + 4], (8, 192))
                for block_y, half in uses:
                    for a in range(4):
                        s = x - 2 * a
                        if 0 <= s < 4:
                            j = 64 * c + 16 * s + 8 * half
                            term = matrices_ref[a, block_y, block_z, j : j + 8, :] * entry
                            key = (block_y, a)
                            totals[key] = totals[key] + term if key in totals else term
    for (block_y, a), total in totals.items():
        at = 8 * a + 2 * block_y + block_z
        solved_ref[at : at + 1, 0:192] = jnp.sum(total, axis=0, keepdims=True)


def place_blocks(solved_ref, placed_ref):
    placed_ref[...] = jnp.zeros((48, 128), F32)
    for a in range(4):
        first = group_transpose(solved_ref[8 * a : 8 * a + 8, 0:128])
        second = group_transpose(solved_ref[8 * a : 8 * a + 8, 128:256])
        for c, piece in enumerate((first[0:4], first[4:8], second[0:4])):
            at = 16 * c + 2 * a + 3
            placed_ref[at : at + 4, :] = placed_ref[at : at + 4, :] + piece
    return dot(placed_ref[...], gather_matrix())


def solve_blocks(field, matrices_ref, turned_ref, solved_ref, placed_ref):
    turn(field, turned_ref)
    for block_z in range(2):
        solve_columns(range(4), block_z, matrices_ref, turned_ref, solved_ref)
    return place_blocks(solved_ref, placed_ref)


INNER, OUTER = (1, 2), (0, 3)


def inner_kernel(fields_ref, stored_ref, matrices_ref, solved_ref, turned_ref, arrived):
    copies = {}
    for block_y, block_z in [(y, z) for ys in (INNER, OUTER) for z in range(2) for y in ys]:
        at = (slice(None), block_y, block_z)
        copies[block_y, block_z] = pltpu.make_async_copy(
            stored_ref.at[at], matrices_ref.at[at], arrived.at[2 * block_y + block_z]
        )
        copies[block_y, block_z].start()
    turn(fields_ref[0:48, :], turned_ref)
    for block_z in range(2):
        for block_y in INNER:
            copies[block_y, block_z].wait()
        solve_columns(INNER, block_z, matrices_ref, turned_ref, solved_ref)
    for block_y in OUTER:
        for block_z in range(2):
            copies[block_y, block_z].wait()


SOLVE_SCRATCH = [
    pltpu.VMEM((80, 128), F32),
    pltpu.VMEM((32, 256), F32),
    pltpu.VMEM((48, 128), F32),
]


def sum_rows(value):
    total = value[0:8]
    for at in range(8, value.shape[0], 8):
        total = total + value[at : at + 8]
    return total


def halves(value, low_ref, high_ref):
    for c in range(3):
        low_ref[8 * c : 8 * c + 8, :] = value[16 * c : 16 * c + 8]
        high_ref[8 * c : 8 * c + 8, :] = value[16 * c + 8 : 16 * c + 16]


def joined(low, high):
    parts = []
    for c in range(3):
        parts += [low[8 * c : 8 * c + 8], high[8 * c : 8 * c + 8]]
    return jnp.concatenate(parts, axis=0)


def first_kernel(
    fields_ref, even_ref, odd_ref, matrices_ref, inner_ref, matrix_ref,
    residual_ref, movable_ref, low_ref, high_ref, rho_ref,
    turned_ref, solved_ref, placed_ref,
):
    lane = iota((16, 128), 1)
    below, above = read_pair(even_ref[0:16, :], odd_ref[0:16, :])
    at_below = (lane >= 24) & (lane < 32)
    at_above = (lane >= 96) & (lane < 104)
    for field in range(6):
        value = fields_ref[16 * field : 16 * field + 16, :]
        at = 64 + 8 * field
        value = jnp.where(at_below, roll(below, 24 - at, 1), value)
        value = jnp.where(at_above, roll(above, 96 - at, 1), value)
        out_ref = residual_ref if field < 3 else movable_ref
        out_ref[16 * (field % 3) : 16 * (field % 3) + 16, :] = value
    residual = residual_ref[...]
    solved_ref[...] = inner_ref[...]
    turn(residual, turned_ref)
    for block_z in range(2):
        solve_columns(OUTER, block_z, matrices_ref, turned_ref, solved_ref)
    solved = place_blocks(solved_ref, placed_ref) * movable_ref[...]
    rho_ref[...] = sum_rows(residual * solved)
    inverse = matrices_ref[0, 0, 0, 0:1, 0:1] * matrix_ref[0:1, 0:1]
    slot = lanes_of(solved) % 8
    solved = jnp.where(slot == FACTOR, 1.0 / inverse, jnp.where(slot == INVERSE, inverse, solved))
    halves(solved, low_ref, high_ref)


FACTOR, INVERSE = 6, 7
LEFT, RIGHT, EVEN, ODD, MINE, MINE_INVERSE = range(0, 48, 8)


def tall(tile):
    return jnp.concatenate([tile] * 3, axis=0)


def cross_kernel(low_ref, high_ref, from_left_ref, from_right_ref, *refs):
    *ratios, low_out, high_out, even_ref, odd_ref = refs
    has_left, has_right = neighbours("gx")
    low, high = low_ref[...], high_ref[...]
    left, right = from_left_ref[...] * has_left, from_right_ref[...] * has_right
    lane = iota((24, 128), 1)
    if ratios:
        low = low + left * tall(ratios[0][LEFT : LEFT + 8, :])
        high = high + right * tall(ratios[0][RIGHT : RIGHT + 8, :])
    else:
        node = lane % 8 < FACTOR
        low = low + jnp.where(node, left, 0.0)
        high = high + jnp.where(node, right, 0.0)
    low_out[...] = low
    high_out[...] = high
    write_pair(
        even_ref, odd_ref, slice(0, 24),
        jnp.where(lane < 64, roll(low, 64, 1), high),
        jnp.where(lane < 64, low, roll(high, 64, 1)),
    )


def add_sides(low, high, even, odd):
    lane = iota((24, 128), 1)
    below, above = read_pair(even, odd)
    low = low + jnp.where(lane < 64, below, roll(above, 64, 1))
    high = high + jnp.where(lane < 64, roll(below, 64, 1), above)
    return joined(low, high)


def corner_fields(vector):
    fields = []
    for q in range(8):
        a, b, c_z = q % 2, (q // 2) % 2, q // 4
        for c in range(3):
            value = vector[16 * c : 16 * c + 16]
            if a:
                value = roll(value, -1, 0)
            if b or c_z:
                value = roll(value, -(8 * b + c_z), 1)
            fields.append(value)
    return fields


def push(stiff_ref, stack_ref, rows):
    totals = [None] * len(rows)
    for j in range(24):
        value = stack_ref[16 * j : 16 * j + 16, :]
        for n, i in enumerate(rows):
            product = stiff_ref[24 * j + i : 24 * j + i + 1, :] * value
            totals[n] = product if j == 0 else totals[n] + product
    return totals


def stack_fields(vector, stack_ref):
    for j, value in enumerate(corner_fields(vector)):
        stack_ref[16 * j : 16 * j + 16, :] = value


def global_weights(shape, position, total):
    weight = jnp.zeros(shape, F32)
    for d in range(-3, 4):
        inside = (position + d >= 0) & (position + d < total)
        weight = weight + jnp.where(inside, 4.0 - abs(d), 0.0)
    return weight


def hat(distance):
    return jnp.maximum(0, 4 - jnp.abs(distance)).astype(F32)


def side_kernel(
    matrix_ref, fields_ref, design_ref, even_ref, odd_ref,
    stiff_ref, scale_ref, weight_ref, pushed_ref, stack_ref,
):
    total_x, total_y = C * lax.axis_size("gx"), C * lax.axis_size("gy")
    for j in range(24):
        stiff_ref[24 * j : 24 * j + 24, :] = jnp.broadcast_to(matrix_ref[:, j : j + 1], (24, 128))
    below, above = read_pair(even_ref[...], odd_ref[...])
    lane24 = iota((24, 128), 1)
    design = jnp.where(lane24 < 64, design_ref[...], roll(above[0:24], 64, 1))
    row, col = iota((16, 24), 0), iota((16, 24), 1)
    along_x = hat((col - 8) - (row - 4))
    source, target = iota((128, 128), 0), iota((128, 128), 1)
    y_target, z_target = target // 8 - 4, target % 8 - 1
    y_source, z_source = source // 8, source % 8 - 1
    z_valid = (z_target >= 0) & (z_target < NZ) & (z_source >= 0) & (z_source < NZ)
    along_z = jnp.where(z_valid, hat(z_source - z_target), 0.0)
    smooth_in = along_z * hat(y_source - y_target)
    smooth_below = jnp.where(source < 64, along_z * hat(y_source - 8 - y_target), 0.0)
    summed = dot(dot(along_x, design), smooth_in) + dot(dot(along_x, below[0:24]), smooth_below)
    row16, lane16 = iota((16, 128), 0), iota((16, 128), 1)
    z = lane16 % 8 - 1
    x = row16 - 4 + C * lax.axis_index("gx")
    y = lane16 // 8 - 4 + C * lax.axis_index("gy")
    shape = (16, 128)
    normalizer = (
        global_weights(shape, x, total_x) * global_weights(shape, y, total_y) * global_weights(shape, z, NZ)
    )
    inside = (x >= 0) & (x < total_x) & (y >= 0) & (y < total_y) & (z >= 0) & (z < NZ)
    normalizer = jnp.where(inside, normalizer, 1.0)
    density = jnp.where(inside, summed / normalizer, 0.0)
    scale_ref[...] = density * density * density
    weight_ref[...] = -3.0 * density * density / normalizer
    lane = iota((16, 128), 1)
    parts = []
    for c in range(3):
        value = fields_ref[96 + 16 * c : 112 + 16 * c, :]
        value = jnp.where(lane < 32, roll(below[24:40], -32 * c, 1), value)
        value = jnp.where(lane >= 96, roll(above[24:40], 96 - 32 * c, 1), value)
        parts.append(value)
    stack_fields(jnp.concatenate(parts, axis=0), stack_ref)
    for i in range(0, 24, 4):
        rows = list(range(i, i + 4))
        for n, value in zip(rows, push(stiff_ref, stack_ref, rows)):
            pushed_ref[16 * n : 16 * n + 16, :] = value


def second_kernel(
    from_left_ref, from_right_ref, low_ref, high_ref, even_ref, odd_ref, stiff_ref, scale_ref,
    residual_ref, movable_ref, matrices_ref,
    direction_ref, low_out, high_out, sums_ref, ratios_ref,
    stack_ref, turned_ref, solved_ref, placed_ref,
):
    direction = add_sides(low_ref[...], high_ref[...], even_ref[...], odd_ref[...])
    factor, inverse = low_ref[0:1, FACTOR : FACTOR + 1], low_ref[0:1, INVERSE : INVERSE + 1]
    for at, ref in ((LEFT, from_left_ref), (RIGHT, from_right_ref), (EVEN, even_ref), (ODD, odd_ref)):
        ratios_ref[at : at + 8, :] = jnp.broadcast_to(factor * ref[0:1, INVERSE : INVERSE + 1], (8, 128))
    ratios_ref[MINE : MINE + 8, :] = jnp.broadcast_to(factor, (8, 128))
    ratios_ref[MINE_INVERSE : MINE_INVERSE + 8, :] = jnp.broadcast_to(inverse, (8, 128))
    direction_ref[...] = direction
    stack_fields(direction, stack_ref)
    scale = scale_ref[...]
    row16, lane16 = iota((16, 128), 0), iota((16, 128), 1)
    own = (row16 >= 4) & (row16 < 12) & (lane16 >= 32) & (lane16 < 96)
    parts = {}
    energy = jnp.zeros((16, 128), F32)
    for q in range(8):
        a, lanes = q % 2, 8 * ((q // 2) % 2) + q // 4
        rows = [3 * q, 3 * q + 1, 3 * q + 2]
        for c, value in enumerate(push(stiff_ref, stack_ref, rows)):
            value = value * scale
            energy = energy + value * stack_ref[16 * (3 * q + c) : 16 * (3 * q + c) + 16, :]
            if a:
                value = roll(value, 1, 0)
            parts[c, lanes] = parts[c, lanes] + value if (c, lanes) in parts else value
    image = []
    for c in range(3):
        value = parts[c, 0]
        for lanes in (1, 8, 9):
            value = value + roll(parts[c, lanes], lanes, 1)
        image.append(value)
    image = jnp.concatenate(image, axis=0) * movable_ref[...]
    solved = solve_blocks(image, matrices_ref, turned_ref, solved_ref, placed_ref) * movable_ref[...]
    solved = solved * factor
    halves(solved, low_out, high_out)
    sums_ref[0:8, :] = sum_rows(jnp.where(own, energy, 0.0))
    sums_ref[8:16, :] = sum_rows(residual_ref[...] * solved)
    sums_ref[16:24, :] = sum_rows(image * solved)


def third_kernel(
    low_ref, high_ref, even_ref, odd_ref, stiff_ref, scale_ref,
    direction_ref, rho_ref, sums_ref, ratios_ref,
    wide_ref, share_ref, stack_ref, other_ref,
):
    wide = add_sides(
        low_ref[...], high_ref[...],
        even_ref[...] * tall(ratios_ref[EVEN : EVEN + 8, :]), odd_ref[...] * tall(ratios_ref[ODD : ODD + 8, :]),
    )
    wide_ref[...] = wide
    stack_fields(wide, stack_ref)
    stack_fields(direction_ref[...], other_ref)
    row16, lane16 = iota((16, 128), 0), iota((16, 128), 1)
    own = (row16 >= 4) & (row16 < 12) & (lane16 >= 32) & (lane16 < 96)
    scale = jnp.where(own, scale_ref[...], 0.0)
    both = jnp.zeros((16, 128), F32)
    mixed = jnp.zeros((16, 128), F32)
    for i in range(0, 24, 4):
        rows = list(range(i, i + 4))
        for n, value in zip(rows, push(stiff_ref, stack_ref, rows)):
            both = both + value * stack_ref[16 * n : 16 * n + 16, :]
            mixed = mixed + value * other_ref[16 * n : 16 * n + 16, :]
    sums = [
        rho_ref[...], sums_ref[0:8, :], sums_ref[8:16, :], sums_ref[16:24, :],
        sum_rows(mixed * scale), sum_rows(both * scale),
    ]
    row, lane = iota((8, 128), 0), iota((8, 128), 1)
    table = jnp.zeros((8, 128), F32)
    for n, value in enumerate(sums):
        table = jnp.where(row == n, jnp.sum(value, axis=0, keepdims=True), table)
    table = jnp.where(row == lane, jnp.sum(table, axis=1, keepdims=True), 0.0)
    line = jnp.sum(table, axis=0, keepdims=True)
    line = jnp.where(lanes_of(line) == 6, ratios_ref[MINE_INVERSE : MINE_INVERSE + 1, :], line)
    share_ref[...] = jnp.broadcast_to(line, share_ref.shape)


def last_kernel(shares_ref, direction_ref, wide_ref, ratios_ref, weight_ref, pushed_ref, adjoint_ref, gradient_ref):
    shares = shares_ref[...]
    ratio = shares[:, 6:7] * ratios_ref[MINE : MINE + 1, :]
    lane = lanes_of(shares)
    weights = jnp.where(lane < 2, 1.0, jnp.where(lane == 5, ratio * ratio, ratio))
    line = jnp.sum(sum_rows(shares * weights), axis=0, keepdims=True)
    rho, curve, cross, image_wide, mixed, both = [line[:, n : n + 1] for n in range(6)]
    step = rho / curve
    unscale = step * ratios_ref[MINE_INVERSE : MINE_INVERSE + 1, 0:1]
    cross, image_wide, mixed, both = cross * unscale, image_wide * unscale, mixed * unscale, both * (unscale * unscale)
    rho_next = rho - cross - step * curve + step * image_wide
    grow = 1.0 + rho_next / rho
    curve_next = grow * grow * curve - grow * (mixed + image_wide) + both
    step_next = rho_next / curve_next
    adjoint = (step + step_next * grow) * direction_ref[...] - (step_next * unscale) * wide_ref[...]
    source, target = iota((128, 32), 0), iota((128, 32), 1)
    y, z = target % 8, target // 8
    pick = (source == 8 * (y + 4) + z + 1).astype(F32)
    own = dot(jnp.concatenate([adjoint[16 * c + 4 : 16 * c + 12] for c in range(3)], axis=0), pick)
    for z_out in range(NZ):
        adjoint_ref[pl.ds(z_out, 24, stride=NZ), :] = own[:, 8 * z_out : 8 * z_out + 8]
    terms = [value * pushed_ref[16 * j : 16 * j + 16, :] for j, value in enumerate(corner_fields(adjoint))]
    while len(terms) > 1:
        terms = [sum(terms[n : n + 3]) for n in range(0, len(terms), 3)]
    energy = terms[0]
    sensitivity = energy * weight_ref[...]
    row, col = iota((8, 16), 0), iota((8, 16), 1)
    along_x = dot(hat(col - 4 - row), sensitivity)
    y_source, z_source = source // 8 - 4, source % 8 - 1
    valid = (z_source >= 0) & (z_source < NZ)
    gradient = dot(along_x, jnp.where(valid, hat(y_source - y) * hat(z_source - z), 0.0))
    for z_out in range(NZ):
        gradient_ref[pl.ds(z_out, 8, stride=NZ), :] = gradient[:, 8 * z_out : 8 * z_out + 8]


def call(kernel, outs, scratch=(), specs=None, limit=VMEM_LIMIT):
    shapes = [jax.ShapeDtypeStruct(shape, F32) for shape in outs]
    return lambda *args: pl.pallas_call(
        kernel,
        out_shape=shapes,
        in_specs=specs or [VM] * len(args),
        out_specs=[VM] * len(shapes),
        scratch_shapes=list(scratch),
        compiler_params=pltpu.CompilerParams(vmem_limit_bytes=limit),
        cost_estimate=pl.CostEstimate(flops=10**6, bytes_accessed=10**6, transcendentals=0),
    )(*args)


def shifted(value, axis, step):
    size = lax.axis_size(axis)
    return lax.ppermute(value, axis, [(i, (i + step) % size) for i in range(size)])


def both_ways(to_next, to_previous, axis):
    return shifted(to_next, axis, 1), shifted(to_previous, axis, -1)


def paired(even, odd):
    size_x, size_y = lax.axis_size("gx"), lax.axis_size("gy")
    pairs = []
    for i in range(size_x):
        for j in range(size_y):
            inside = 0 < j < size_y - 1
            other = (i, j + 1 if j % 2 else j - 1) if inside else (i ^ 1, j)
            pairs.append((i * size_y + j, other[0] * size_y + other[1]))
    from_even = lax.ppermute(even, "gy", [(j, j ^ 1) for j in range(size_y)])
    return from_even, lax.ppermute(odd, ("gx", "gy"), pairs)


def as_rows(values):
    return jnp.swapaxes(values, -1, -2).reshape((-1, C))


def from_rows(values, shape):
    return jnp.swapaxes(values.reshape(shape[:-2] + (NZ, C)), -1, -2)


def local(design, element_matrix, fixed, inverses, state, load):
    size_x, size_y = lax.axis_size("gx"), lax.axis_size("gy")
    inputs = sum(
        jnp.pad(value, [(first, 10 - first - value.shape[0])] + [(0, 0)] * 3)
        for first, value in ((0, load), (6, state), (9, design[None]))
    )
    inputs = inputs + jnp.pad(fixed, [(3, 4)] + [(0, 0)] * 3).astype(F32)
    own, to_right, to_left = call(pack_kernel, [(80, 128), (16, 128), (16, 128)])(as_rows(inputs))
    left, right = both_ways(to_right, to_left, "gx")
    fields, design_wide, even, odd = call(widen_kernel, [(144, 128), (24, 128), (40, 128), (40, 128)])(
        own, left, right
    )
    even, odd = paired(even, odd)
    matrices, solved = call(
        inner_kernel,
        [inverses.shape, (32, 256)],
        [pltpu.VMEM((80, 128), F32), pltpu.SemaphoreType.DMA((8,))],
        [VM, pl.BlockSpec(memory_space=pl.ANY)],
        INNER_LIMIT,
    )(fields, inverses)
    residual, movable, low, high, rho = call(
        first_kernel, [(48, 128), (48, 128), (24, 128), (24, 128), (8, 128)], SOLVE_SCRATCH
    )(fields, even, odd, matrices, solved, element_matrix)
    stiff, scale, weight, pushed = call(
        side_kernel,
        [(576, 128), (16, 128), (16, 128), (384, 128)],
        [pltpu.VMEM((384, 128), F32)],
    )(element_matrix, fields, design_wide, even, odd)

    def crossed(low, high, *ratios):
        left, right = both_ways(high, low, "gx")
        low, high, even, odd = call(cross_kernel, [(24, 128)] * 4)(low, high, left, right, *ratios)
        return left, right, low, high, *paired(even, odd)

    sides = crossed(low, high)
    direction, low, high, sums, ratios = call(
        second_kernel,
        [(48, 128), (24, 128), (24, 128), (24, 128), (48, 128)],
        [pltpu.VMEM((384, 128), F32)] + SOLVE_SCRATCH,
    )(*sides, stiff, scale, residual, movable, matrices)
    sides = crossed(low, high, ratios)[2:]
    devices = size_x * size_y
    wide, share = call(
        third_kernel, [(48, 128), (devices, 128)], [pltpu.VMEM((384, 128), F32), pltpu.VMEM((384, 128), F32)]
    )(*sides, stiff, scale, direction, rho, sums, ratios)
    shares = lax.all_to_all(share, ("gx", "gy"), 0, 0, tiled=True)
    adjoint, gradient = call(last_kernel, [(96, C), (32, C)])(shares, direction, wide, ratios, weight, pushed)
    return from_rows(adjoint, (3, C, C, NZ)), from_rows(gradient, (C, C, NZ))


def solution(mesh):
    placed = (
        P("gx", "gy", None),
        P(),
        P(None, "gx", "gy", None),
        P("gx", "gy", None, None, None),
        P(None, "gx", "gy", None),
        P(None, "gx", "gy", None),
    )
    return jax.shard_map(
        local,
        mesh=mesh,
        in_specs=placed,
        out_specs=(P(None, "gx", "gy", None), P("gx", "gy", None)),
        check_vma=False,
    )
```

```python
import jax
import jax.numpy as jnp
from jax import lax
from jax.experimental import pallas as pl
from jax.experimental.pallas import tpu as pltpu
from jax.sharding import PartitionSpec as P

C = 8
NZ = 4
F32 = jnp.float32
HIGHEST = lax.Precision.HIGHEST
VMEM_LIMIT = 20 * 1024 * 1024
BRING_LIMIT = 46 * 1024 * 1024
VM = pl.BlockSpec(memory_space=pltpu.VMEM)


def iota(shape, dim):
    return lax.broadcasted_iota(jnp.int32, shape, dim)


def dot(left, right):
    return jnp.dot(left, right, precision=HIGHEST, preferred_element_type=F32)


def parts_of(value):
    parts = []
    for _ in range(3):
        parts.append(value.astype(jnp.bfloat16).astype(F32))
        value = value - parts[-1]
    return parts


def dot_picks(left, right, dims=((1,), (0,)), exact_left=False):
    pairs = [(left, part) for part in parts_of(right)] if exact_left else [(part, right) for part in parts_of(left)]
    total = 0.0
    for first, second in reversed(pairs):
        total = total + lax.dot_general(
            first, second, (dims, ((), ())), precision=lax.Precision.DEFAULT, preferred_element_type=F32
        )
    return total


def roll(value, shift, axis):
    size = value.shape[axis]
    return pltpu.roll(value, shift % size, axis)


def lanes_of(value):
    return iota(value.shape, 1)


def neighbours(axis):
    at = lax.axis_index(axis)
    return (at > 0).astype(F32), (at < lax.axis_size(axis) - 1).astype(F32)


def is_even():
    return lax.axis_index("gy") % 2 == 0


def write_pair(even_ref, odd_ref, rows, up, down):
    even_ref[rows, :] = jnp.where(is_even(), up, down)
    odd_ref[rows, :] = jnp.where(is_even(), down, up)


def read_pair(even, odd):
    has_below, has_above = neighbours("gy")
    return jnp.where(is_even(), odd, even) * has_below, jnp.where(is_even(), even, odd) * has_above


def spread_matrix(z):
    y, lane = iota((8, 128), 0), iota((8, 128), 1)
    return (lane == 8 * (y + 4) + z + 1).astype(F32)


def pack_kernel(inputs_ref, own_ref, right_ref, left_ref):
    own = jnp.zeros((80, 128), F32)
    for z in range(NZ):
        values = inputs_ref[pl.ds(z, 80, stride=NZ), :]
        movable = 1.0 - values[24:48]
        piece = jnp.concatenate([movable * values[0:24], movable, values[48:80]], axis=0)
        own = own + dot_picks(piece, spread_matrix(z))
    own_ref[...] = own
    lane = iota((8, 128), 1)
    row = iota((8, 128), 0)
    design = roll(own[72:80], -32, 1)
    for out_ref, edge, first in ((right_ref, 7, 4), (left_ref, 0, 0)):
        edges = jnp.zeros((8, 128), F32)
        for field in range(6):
            line = own[8 * field + edge : 8 * field + edge + 1]
            edges = jnp.where(row == field, line, edges)
        out_ref[0:8, :] = jnp.where(lane < 64, design, roll(edges, 32, 1))
        upper = [own[48 + 8 * c : 56 + 8 * c] for c in range(3)]
        if first == 4:
            upper = [upper[0], upper[1], upper[2]]
            a = jnp.where(row < 4, roll(upper[0], 4, 0), upper[1])
            b = roll(upper[2], 4, 0)
        else:
            a = jnp.where(row < 4, upper[0], roll(upper[1], 4, 0))
            b = upper[2]
        out_ref[8:16, :] = jnp.where(lane < 64, roll(a, -32, 1), roll(b, 32, 1))


def widen_kernel(after_ref, own_ref, from_left_ref, from_right_ref, fields_ref, design_ref, even_ref, odd_ref):
    has_left, has_right = neighbours("gx")
    lane = iota((8, 128), 1)
    row = iota((8, 128), 0)
    middle = (lane >= 32) & (lane < 96)
    left, right = from_left_ref[...] * has_left, from_right_ref[...] * has_right
    rows_left = jnp.where(middle, roll(left[0:8], -32, 1), 0.0)
    rows_right = jnp.where(middle, roll(right[0:8], -32, 1), 0.0)
    design = jnp.concatenate([left[0:8], roll(own_ref[72:80, :], -32, 1), right[0:8]], axis=0)
    design_ref[...] = design
    tall_lane = iota((24, 128), 1)
    design = jnp.where(tall_lane < 64, design, 0.0)
    edges_up = [jnp.zeros((8, 128), F32), jnp.zeros((8, 128), F32)]
    edges_down = [jnp.zeros((8, 128), F32), jnp.zeros((8, 128), F32)]
    for field in range(6):
        own = own_ref[8 * field : 8 * field + 8, :]
        turned = roll(own, 4, 0)
        low = jnp.where(row >= 4, turned, jnp.where(row == 3, rows_left[field : field + 1], 0.0))
        high = jnp.where(row < 4, turned, jnp.where(row == 4, rows_right[field : field + 1], 0.0))
        fields_ref[16 * field : 16 * field + 8, :] = low
        fields_ref[16 * field + 8 : 16 * field + 16, :] = high
        at = 64 + 8 * field
        place = (lane >= at) & (lane < at + 8)
        for half, value in enumerate((low, high)):
            edges_up[half] = jnp.where(place, roll(value, at - 88, 1), edges_up[half])
            edges_down[half] = jnp.where(place, roll(value, at - 32, 1), edges_down[half])
    zeros = jnp.zeros((8, 128), F32)
    write_pair(
        even_ref, odd_ref, slice(0, 24),
        jnp.where(tall_lane < 64, design, jnp.concatenate(edges_up + [zeros], axis=0)),
        jnp.where(tall_lane < 64, design, jnp.concatenate(edges_down + [zeros], axis=0)),
    )
    state_left, state_right = left[8:16], right[8:16]
    ups = [zeros, zeros]
    downs = [zeros, zeros]
    for c in range(3):
        turned = roll(own_ref[48 + 8 * c : 56 + 8 * c, :], 4, 0)
        lane_turn = 32 if c < 2 else -32
        got_left = jnp.where(middle, roll(state_left, lane_turn, 1), 0.0)
        got_right = jnp.where(middle, roll(state_right, lane_turn, 1), 0.0)
        if c == 1:
            got_left = roll(got_left, 4, 0)
        else:
            got_right = roll(got_right, 4, 0)
        low = jnp.where(row >= 4, turned, got_left)
        high = jnp.where(row < 4, turned, got_right)
        fields_ref[96 + 16 * c : 104 + 16 * c, :] = low
        fields_ref[104 + 16 * c : 112 + 16 * c, :] = high
        place = (lane >= 32 * c) & (lane < 32 * c + 32)
        for half, value in enumerate((low, high)):
            ups[half] = jnp.where(place, roll(value, 32 * c - 64, 1), ups[half])
            downs[half] = jnp.where(place, roll(value, 32 * c - 32, 1), downs[half])
    for half in range(2):
        write_pair(even_ref, odd_ref, slice(24 + 8 * half, 32 + 8 * half), ups[half], downs[half])


def gather_matrix():
    row, lane = iota((128, 128), 0), iota((128, 128), 1)
    block_y, block_z = row // 32, (row // 16) % 2
    t, u = (row // 4) % 4, row % 4
    return (lane == 8 * (2 * block_y + t + 3) + 2 * block_z + u).astype(F32)


def group_transpose(value):
    row, group = iota((8, 128), 0), iota((8, 128), 1) // 16
    for d in (1, 2, 4):
        row_bit, group_bit = (row // d) % 2, (group // d) % 2
        down = roll(roll(value, d, 0), -16 * d, 1)
        up = roll(roll(value, -d, 0), 16 * d, 1)
        moved = jnp.where(row_bit == 1, down, up)
        value = jnp.where(row_bit == group_bit, value, moved)
    return value


def turn(field, turned_ref):
    row, lane = iota((80, 128), 0), iota((80, 128), 1)
    block_z, pair, tt, u = row // 40, (row // 8) % 5, (row // 4) % 2, row % 4
    pick = (lane == 8 * (2 * pair + tt + 3) + 2 * block_z + u).astype(F32)
    turned_ref[:, 0:48] = dot_picks(pick, field, ((1,), (1,)), exact_left=True)


def solve_columns(blocks_y, block_z, matrices, turned_ref, solved_ref):
    totals = {}
    for pair in range(5):
        uses = [(block_y, pair - block_y) for block_y in blocks_y if 0 <= pair - block_y < 2]
        at = 40 * block_z + 8 * pair
        values = turned_ref[at : at + 8, 0:48]
        for c in range(3 if uses else 0):
            for x in range(10):
                entry = jnp.broadcast_to(values[:, 16 * c + x + 3 : 16 * c + x + 4], (8, 192))
                for block_y, half in uses:
                    for a in range(4):
                        s = x - 2 * a
                        if 0 <= s < 4:
                            j = 64 * c + 16 * s + 8 * half
                            term = matrices[block_y][a, block_y // 2, block_z, j : j + 8, :] * entry
                            key = (block_y, a)
                            totals[key] = totals[key] + term if key in totals else term
    for (block_y, a), total in totals.items():
        at = 8 * a + 2 * block_y + block_z
        solved_ref[at : at + 1, 0:192] = jnp.sum(total, axis=0, keepdims=True)


def place_blocks(solved_ref, placed_ref):
    placed_ref[...] = jnp.zeros((48, 128), F32)
    for a in range(4):
        first = group_transpose(solved_ref[8 * a : 8 * a + 8, 0:128])
        second = group_transpose(solved_ref[8 * a : 8 * a + 8, 128:256])
        for c, piece in enumerate((first[0:4], first[4:8], second[0:4])):
            at = 16 * c + 2 * a + 3
            placed_ref[at : at + 4, :] = placed_ref[at : at + 4, :] + piece
    return dot_picks(placed_ref[...], gather_matrix())


INNER, OUTER = (1, 2), (0, 3)


def bring(blocks_y, stored_ref, kept_ref, arrived):
    copies = {}
    for block_z in range(2):
        for block_y in blocks_y:
            copies[block_y, block_z] = pltpu.make_async_copy(
                stored_ref.at[:, block_y, block_z],
                kept_ref.at[:, block_y // 2, block_z],
                arrived.at[2 * (block_y // 2) + block_z],
            )
            copies[block_y, block_z].start()
    return copies


def outer_kernel(own_ref, stored_ref, kept_ref, arrived):
    for copy in bring(OUTER, stored_ref, kept_ref, arrived).values():
        copy.wait()


def inner_kernel(fields_ref, stored_ref, kept_ref, solved_ref, turned_ref, arrived):
    copies = bring(INNER, stored_ref, kept_ref, arrived)
    turn(fields_ref[0:48, :], turned_ref)
    for block_z in range(2):
        for block_y in INNER:
            copies[block_y, block_z].wait()
        solve_columns(INNER, block_z, {y: kept_ref for y in INNER}, turned_ref, solved_ref)


SOLVE_SCRATCH = [
    pltpu.VMEM((80, 128), F32),
    pltpu.VMEM((32, 256), F32),
    pltpu.VMEM((48, 128), F32),
]


def sum_rows(value):
    total = value[0:8]
    for at in range(8, value.shape[0], 8):
        total = total + value[at : at + 8]
    return total


def halves(value, low_ref, high_ref):
    for c in range(3):
        low_ref[8 * c : 8 * c + 8, :] = value[16 * c : 16 * c + 8]
        high_ref[8 * c : 8 * c + 8, :] = value[16 * c + 8 : 16 * c + 16]


def joined(low, high):
    parts = []
    for c in range(3):
        parts += [low[8 * c : 8 * c + 8], high[8 * c : 8 * c + 8]]
    return jnp.concatenate(parts, axis=0)


def first_kernel(
    fields_ref, even_ref, odd_ref, outer_ref, inner_ref, matrix_ref,
    residual_ref, movable_ref, low_ref, high_ref, rho_ref,
    turned_ref, solved_ref, placed_ref,
):
    lane = iota((16, 128), 1)
    below, above = read_pair(even_ref[0:16, :], odd_ref[0:16, :])
    at_below = (lane >= 24) & (lane < 32)
    at_above = (lane >= 96) & (lane < 104)
    for field in range(6):
        value = fields_ref[16 * field : 16 * field + 16, :]
        at = 64 + 8 * field
        value = jnp.where(at_below, roll(below, 24 - at, 1), value)
        value = jnp.where(at_above, roll(above, 96 - at, 1), value)
        out_ref = residual_ref if field < 3 else movable_ref
        out_ref[16 * (field % 3) : 16 * (field % 3) + 16, :] = value
    residual = residual_ref[...]
    solved_ref[...] = inner_ref[...]
    turn(residual, turned_ref)
    for block_z in range(2):
        solve_columns(OUTER, block_z, {y: outer_ref for y in OUTER}, turned_ref, solved_ref)
    solved = place_blocks(solved_ref, placed_ref) * movable_ref[...]
    rho_ref[...] = sum_rows(residual * solved)
    inverse = outer_ref[0, 0, 0, 0:1, 0:1] * matrix_ref[0:1, 0:1]
    slot = lanes_of(solved) % 8
    solved = jnp.where(slot == FACTOR, 1.0 / inverse, jnp.where(slot == INVERSE, inverse, solved))
    halves(solved, low_ref, high_ref)


FACTOR, INVERSE = 6, 7
LEFT, RIGHT, EVEN, ODD, MINE, MINE_INVERSE = range(0, 48, 8)


def tall(tile):
    return jnp.concatenate([tile] * 3, axis=0)


def cross_kernel(low_ref, high_ref, from_left_ref, from_right_ref, *refs):
    *ratios, low_out, high_out, even_ref, odd_ref = refs
    has_left, has_right = neighbours("gx")
    low, high = low_ref[...], high_ref[...]
    left, right = from_left_ref[...] * has_left, from_right_ref[...] * has_right
    lane = iota((24, 128), 1)
    if ratios:
        low = low + left * tall(ratios[0][LEFT : LEFT + 8, :])
        high = high + right * tall(ratios[0][RIGHT : RIGHT + 8, :])
    else:
        node = lane % 8 < FACTOR
        low = low + jnp.where(node, left, 0.0)
        high = high + jnp.where(node, right, 0.0)
    low_out[...] = low
    high_out[...] = high
    write_pair(
        even_ref, odd_ref, slice(0, 24),
        jnp.where(lane < 64, roll(low, 64, 1), high),
        jnp.where(lane < 64, low, roll(high, 64, 1)),
    )


def add_sides(low, high, even, odd):
    lane = iota((24, 128), 1)
    below, above = read_pair(even, odd)
    low = low + jnp.where(lane < 64, below, roll(above, 64, 1))
    high = high + jnp.where(lane < 64, roll(below, 64, 1), above)
    return joined(low, high)


def corner_fields(vector):
    fields = []
    for q in range(8):
        a, b, c_z = q % 2, (q // 2) % 2, q // 4
        for c in range(3):
            value = vector[16 * c : 16 * c + 16]
            if a:
                value = roll(value, -1, 0)
            if b or c_z:
                value = roll(value, -(8 * b + c_z), 1)
            fields.append(value)
    return fields


def push(stiff_ref, stack_ref, rows):
    totals = [None] * len(rows)
    for j in range(24):
        value = stack_ref[16 * j : 16 * j + 16, :]
        for n, i in enumerate(rows):
            product = stiff_ref[24 * j + i : 24 * j + i + 1, :] * value
            totals[n] = product if j == 0 else totals[n] + product
    return totals


def stack_fields(vector, stack_ref):
    for j, value in enumerate(corner_fields(vector)):
        stack_ref[16 * j : 16 * j + 16, :] = value


def global_weights(shape, position, total):
    weight = jnp.zeros(shape, F32)
    for d in range(-3, 4):
        inside = (position + d >= 0) & (position + d < total)
        weight = weight + jnp.where(inside, 4.0 - abs(d), 0.0)
    return weight


def hat(distance):
    return jnp.maximum(0, 4 - jnp.abs(distance)).astype(F32)


def side_kernel(
    matrix_ref, fields_ref, design_ref, even_ref, odd_ref,
    stiff_ref, scale_ref, weight_ref, pushed_ref, stack_ref,
):
    total_x, total_y = C * lax.axis_size("gx"), C * lax.axis_size("gy")
    for j in range(24):
        stiff_ref[24 * j : 24 * j + 24, :] = jnp.broadcast_to(matrix_ref[:, j : j + 1], (24, 128))
    below, above = read_pair(even_ref[...], odd_ref[...])
    lane24 = iota((24, 128), 1)
    design = jnp.where(lane24 < 64, design_ref[...], roll(above[0:24], 64, 1))
    row, col = iota((16, 24), 0), iota((16, 24), 1)
    along_x = hat((col - 8) - (row - 4))
    source, target = iota((128, 128), 0), iota((128, 128), 1)
    y_target, z_target = target // 8 - 4, target % 8 - 1
    y_source, z_source = source // 8, source % 8 - 1
    z_valid = (z_target >= 0) & (z_target < NZ) & (z_source >= 0) & (z_source < NZ)
    along_z = jnp.where(z_valid, hat(z_source - z_target), 0.0)
    smooth_in = along_z * hat(y_source - y_target)
    smooth_below = jnp.where(source < 64, along_z * hat(y_source - 8 - y_target), 0.0)
    summed = dot(dot(along_x, design), smooth_in) + dot(dot(along_x, below[0:24]), smooth_below)
    row16, lane16 = iota((16, 128), 0), iota((16, 128), 1)
    z = lane16 % 8 - 1
    x = row16 - 4 + C * lax.axis_index("gx")
    y = lane16 // 8 - 4 + C * lax.axis_index("gy")
    shape = (16, 128)
    normalizer = (
        global_weights(shape, x, total_x) * global_weights(shape, y, total_y) * global_weights(shape, z, NZ)
    )
    inside = (x >= 0) & (x < total_x) & (y >= 0) & (y < total_y) & (z >= 0) & (z < NZ)
    normalizer = jnp.where(inside, normalizer, 1.0)
    density = jnp.where(inside, summed / normalizer, 0.0)
    scale_ref[...] = density * density * density
    weight_ref[...] = -3.0 * density * density / normalizer
    lane = iota((16, 128), 1)
    parts = []
    for c in range(3):
        value = fields_ref[96 + 16 * c : 112 + 16 * c, :]
        value = jnp.where(lane < 32, roll(below[24:40], -32 * c, 1), value)
        value = jnp.where(lane >= 96, roll(above[24:40], 96 - 32 * c, 1), value)
        parts.append(value)
    stack_fields(jnp.concatenate(parts, axis=0), stack_ref)
    for i in range(0, 24, 4):
        rows = list(range(i, i + 4))
        for n, value in zip(rows, push(stiff_ref, stack_ref, rows)):
            pushed_ref[16 * n : 16 * n + 16, :] = value


def second_kernel(
    from_left_ref, from_right_ref, low_ref, high_ref, even_ref, odd_ref, stiff_ref, scale_ref,
    residual_ref, movable_ref, outer_ref, inner_ref,
    direction_ref, low_out, high_out, sums_ref, ratios_ref,
    stack_ref, turned_ref, solved_ref, placed_ref,
):
    direction = add_sides(low_ref[...], high_ref[...], even_ref[...], odd_ref[...])
    factor, inverse = low_ref[0:1, FACTOR : FACTOR + 1], low_ref[0:1, INVERSE : INVERSE + 1]
    for at, ref in ((LEFT, from_left_ref), (RIGHT, from_right_ref), (EVEN, even_ref), (ODD, odd_ref)):
        ratios_ref[at : at + 8, :] = jnp.broadcast_to(factor * ref[0:1, INVERSE : INVERSE + 1], (8, 128))
    ratios_ref[MINE : MINE + 8, :] = jnp.broadcast_to(factor, (8, 128))
    ratios_ref[MINE_INVERSE : MINE_INVERSE + 8, :] = jnp.broadcast_to(inverse, (8, 128))
    direction_ref[...] = direction
    stack_fields(direction, stack_ref)
    scale = scale_ref[...]
    row16, lane16 = iota((16, 128), 0), iota((16, 128), 1)
    own = (row16 >= 4) & (row16 < 12) & (lane16 >= 32) & (lane16 < 96)
    parts = {}
    energy = jnp.zeros((16, 128), F32)
    for q in range(8):
        a, lanes = q % 2, 8 * ((q // 2) % 2) + q // 4
        rows = [3 * q, 3 * q + 1, 3 * q + 2]
        for c, value in enumerate(push(stiff_ref, stack_ref, rows)):
            value = value * scale
            energy = energy + value * stack_ref[16 * (3 * q + c) : 16 * (3 * q + c) + 16, :]
            if a:
                value = roll(value, 1, 0)
            parts[c, lanes] = parts[c, lanes] + value if (c, lanes) in parts else value
    image = []
    for c in range(3):
        value = parts[c, 0]
        for lanes in (1, 8, 9):
            value = value + roll(parts[c, lanes], lanes, 1)
        image.append(value)
    image = jnp.concatenate(image, axis=0) * movable_ref[...]
    turn(image, turned_ref)
    matrices = {0: outer_ref, 1: inner_ref, 2: inner_ref, 3: outer_ref}
    for block_z in range(2):
        solve_columns(range(4), block_z, matrices, turned_ref, solved_ref)
    solved = place_blocks(solved_ref, placed_ref) * movable_ref[...]
    solved = solved * factor
    halves(solved, low_out, high_out)
    sums_ref[0:8, :] = sum_rows(jnp.where(own, energy, 0.0))
    sums_ref[8:16, :] = sum_rows(residual_ref[...] * solved)
    sums_ref[16:24, :] = sum_rows(image * solved)


def third_kernel(
    low_ref, high_ref, even_ref, odd_ref, stiff_ref, scale_ref,
    direction_ref, rho_ref, sums_ref, ratios_ref,
    wide_ref, share_ref, stack_ref, other_ref,
):
    wide = add_sides(
        low_ref[...], high_ref[...],
        even_ref[...] * tall(ratios_ref[EVEN : EVEN + 8, :]), odd_ref[...] * tall(ratios_ref[ODD : ODD + 8, :]),
    )
    wide_ref[...] = wide
    stack_fields(wide, stack_ref)
    stack_fields(direction_ref[...], other_ref)
    row16, lane16 = iota((16, 128), 0), iota((16, 128), 1)
    own = (row16 >= 4) & (row16 < 12) & (lane16 >= 32) & (lane16 < 96)
    scale = jnp.where(own, scale_ref[...], 0.0)
    both = jnp.zeros((16, 128), F32)
    mixed = jnp.zeros((16, 128), F32)
    for i in range(0, 24, 4):
        rows = list(range(i, i + 4))
        for n, value in zip(rows, push(stiff_ref, stack_ref, rows)):
            both = both + value * stack_ref[16 * n : 16 * n + 16, :]
            mixed = mixed + value * other_ref[16 * n : 16 * n + 16, :]
    sums = [
        rho_ref[...], sums_ref[0:8, :], sums_ref[8:16, :], sums_ref[16:24, :],
        sum_rows(mixed * scale), sum_rows(both * scale),
    ]
    row, lane = iota((8, 128), 0), iota((8, 128), 1)
    table = jnp.zeros((8, 128), F32)
    for n, value in enumerate(sums):
        table = jnp.where(row == n, jnp.sum(value, axis=0, keepdims=True), table)
    table = jnp.where(row == lane, jnp.sum(table, axis=1, keepdims=True), 0.0)
    line = jnp.sum(table, axis=0, keepdims=True)
    line = jnp.where(lanes_of(line) == 6, ratios_ref[MINE_INVERSE : MINE_INVERSE + 1, :], line)
    share_ref[...] = jnp.broadcast_to(line, share_ref.shape)


def last_kernel(shares_ref, direction_ref, wide_ref, ratios_ref, weight_ref, pushed_ref, adjoint_ref, gradient_ref, smooth_ref):
    shares = shares_ref[...]
    ratio = shares[:, 6:7] * ratios_ref[MINE : MINE + 1, :]
    lane = lanes_of(shares)
    weights = jnp.where(lane < 2, 1.0, jnp.where(lane == 5, ratio * ratio, ratio))
    line = jnp.sum(sum_rows(shares * weights), axis=0, keepdims=True)
    rho, curve, cross, image_wide, mixed, both = [line[:, n : n + 1] for n in range(6)]
    step = rho / curve
    unscale = step * ratios_ref[MINE_INVERSE : MINE_INVERSE + 1, 0:1]
    cross, image_wide, mixed, both = cross * unscale, image_wide * unscale, mixed * unscale, both * (unscale * unscale)
    rho_next = rho - cross - step * curve + step * image_wide
    grow = 1.0 + rho_next / rho
    curve_next = grow * grow * curve - grow * (mixed + image_wide) + both
    step_next = rho_next / curve_next
    adjoint = (step + step_next * grow) * direction_ref[...] - (step_next * unscale) * wide_ref[...]
    source, target = iota((128, 32), 0), iota((128, 32), 1)
    y, z = target % 8, target // 8
    pick = (source == 8 * (y + 4) + z + 1).astype(F32)
    own = dot_picks(jnp.concatenate([adjoint[16 * c + 4 : 16 * c + 12] for c in range(3)], axis=0), pick)
    for z_out in range(NZ):
        adjoint_ref[pl.ds(z_out, 24, stride=NZ), :] = own[:, 8 * z_out : 8 * z_out + 8]
    terms = [value * pushed_ref[16 * j : 16 * j + 16, :] for j, value in enumerate(corner_fields(adjoint))]
    while len(terms) > 1:
        terms = [sum(terms[n : n + 3]) for n in range(0, len(terms), 3)]
    energy = terms[0]
    sensitivity = energy * weight_ref[...]
    y_source, z_source = source // 8 - 4, source % 8 - 1
    valid = (z_source >= 0) & (z_source < NZ)
    smooth_ref[...] = dot_picks(sensitivity, jnp.where(valid, hat(y_source - y) * hat(z_source - z), 0.0))
    gradient = 4.0 * smooth_ref[4:12, :]
    for d in range(1, 4):
        gradient = gradient + (4.0 - d) * (smooth_ref[4 - d : 12 - d, :] + smooth_ref[4 + d : 12 + d, :])
    for z_out in range(NZ):
        gradient_ref[pl.ds(z_out, 8, stride=NZ), :] = gradient[:, 8 * z_out : 8 * z_out + 8]


def call(kernel, outs, scratch=(), specs=None, limit=VMEM_LIMIT):
    shapes = [jax.ShapeDtypeStruct(shape, F32) for shape in outs]
    return lambda *args: pl.pallas_call(
        kernel,
        out_shape=shapes,
        in_specs=specs or [VM] * len(args),
        out_specs=[VM] * len(shapes),
        scratch_shapes=list(scratch),
        compiler_params=pltpu.CompilerParams(vmem_limit_bytes=limit),
        cost_estimate=pl.CostEstimate(flops=10**6, bytes_accessed=10**6, transcendentals=0),
    )(*args)


def shifted(value, axis, step):
    size = lax.axis_size(axis)
    return lax.ppermute(value, axis, [(i, (i + step) % size) for i in range(size)])


def both_ways(to_next, to_previous, axis):
    return shifted(to_next, axis, 1), shifted(to_previous, axis, -1)


def paired(even, odd):
    size_x, size_y = lax.axis_size("gx"), lax.axis_size("gy")
    pairs = []
    for i in range(size_x):
        for j in range(size_y):
            inside = 0 < j < size_y - 1
            other = (i, j + 1 if j % 2 else j - 1) if inside else (i ^ 1, j)
            pairs.append((i * size_y + j, other[0] * size_y + other[1]))
    from_even = lax.ppermute(even, "gy", [(j, j ^ 1) for j in range(size_y)])
    return from_even, lax.ppermute(odd, ("gx", "gy"), pairs)


def as_rows(values):
    return jnp.swapaxes(values, -1, -2).reshape((-1, C))


def from_rows(values, shape):
    return jnp.swapaxes(values.reshape(shape[:-2] + (NZ, C)), -1, -2)


def local(design, element_matrix, fixed, inverses, state, load):
    size_x, size_y = lax.axis_size("gx"), lax.axis_size("gy")
    inputs = sum(
        jnp.pad(value, [(first, 10 - first - value.shape[0])] + [(0, 0)] * 3)
        for first, value in ((0, load), (6, state), (9, design[None]))
    )
    inputs = inputs + jnp.pad(fixed, [(3, 4)] + [(0, 0)] * 3).astype(F32)
    own, to_right, to_left = call(pack_kernel, [(80, 128), (16, 128), (16, 128)])(as_rows(inputs))
    left, right = both_ways(to_right, to_left, "gx")
    size_a, size_b, *rest = inverses.shape
    half = (size_a, size_b // 2, *rest)
    mixed_specs = [VM, pl.BlockSpec(memory_space=pl.ANY)]
    arrived = pltpu.SemaphoreType.DMA((4,))
    (outer,) = call(outer_kernel, [half], [arrived], mixed_specs, BRING_LIMIT)(own, inverses)
    fields, design_wide, even, odd = call(widen_kernel, [(144, 128), (24, 128), (40, 128), (40, 128)])(
        outer, own, left, right
    )
    even, odd = paired(even, odd)
    inner, solved = call(
        inner_kernel, [half, (32, 256)], [pltpu.VMEM((80, 128), F32), arrived], mixed_specs, BRING_LIMIT
    )(fields, inverses)
    residual, movable, low, high, rho = call(
        first_kernel, [(48, 128), (48, 128), (24, 128), (24, 128), (8, 128)], SOLVE_SCRATCH
    )(fields, even, odd, outer, solved, element_matrix)
    stiff, scale, weight, pushed = call(
        side_kernel,
        [(576, 128), (16, 128), (16, 128), (384, 128)],
        [pltpu.VMEM((384, 128), F32)],
    )(element_matrix, fields, design_wide, even, odd)

    def crossed(low, high, *ratios):
        left, right = both_ways(high, low, "gx")
        low, high, even, odd = call(cross_kernel, [(24, 128)] * 4)(low, high, left, right, *ratios)
        return left, right, low, high, *paired(even, odd)

    sides = crossed(low, high)
    direction, low, high, sums, ratios = call(
        second_kernel,
        [(48, 128), (24, 128), (24, 128), (24, 128), (48, 128)],
        [pltpu.VMEM((384, 128), F32)] + SOLVE_SCRATCH,
    )(*sides, stiff, scale, residual, movable, outer, inner)
    sides = crossed(low, high, ratios)[2:]
    devices = size_x * size_y
    wide, share = call(
        third_kernel, [(48, 128), (devices, 128)], [pltpu.VMEM((384, 128), F32), pltpu.VMEM((384, 128), F32)]
    )(*sides, stiff, scale, direction, rho, sums, ratios)
    shares = lax.all_to_all(share, ("gx", "gy"), 0, 0, tiled=True)
    adjoint, gradient = call(last_kernel, [(96, C), (32, C)], [pltpu.VMEM((16, 32), F32)])(shares, direction, wide, ratios, weight, pushed)
    return from_rows(adjoint, (3, C, C, NZ)), from_rows(gradient, (C, C, NZ))


def solution(mesh):
    placed = (
        P("gx", "gy", None),
        P(),
        P(None, "gx", "gy", None),
        P("gx", "gy", None, None, None),
        P(None, "gx", "gy", None),
        P(None, "gx", "gy", None),
    )
    return jax.shard_map(
        local,
        mesh=mesh,
        in_specs=placed,
        out_specs=(P(None, "gx", "gy", None), P("gx", "gy", None)),
        check_vma=False,
    )
```

```python
import jax
import jax.numpy as jnp
from jax import lax
from jax.experimental import pallas as pl
from jax.experimental.pallas import tpu as pltpu
from jax.sharding import PartitionSpec as P

C = 8
NZ = 4
F32 = jnp.float32
HIGHEST = lax.Precision.HIGHEST
VMEM_LIMIT = 20 * 1024 * 1024
BRING_LIMIT = 46 * 1024 * 1024
VM = pl.BlockSpec(memory_space=pltpu.VMEM)


def iota(shape, dim):
    return lax.broadcasted_iota(jnp.int32, shape, dim)


def dot(left, right):
    return jnp.dot(left, right, precision=HIGHEST, preferred_element_type=F32)


def parts_of(value):
    parts = []
    for _ in range(3):
        parts.append(value.astype(jnp.bfloat16).astype(F32))
        value = value - parts[-1]
    return parts


def dot_picks(left, right, dims=((1,), (0,)), exact_left=False):
    pairs = [(left, part) for part in parts_of(right)] if exact_left else [(part, right) for part in parts_of(left)]
    total = 0.0
    for first, second in reversed(pairs):
        total = total + lax.dot_general(
            first, second, (dims, ((), ())), precision=lax.Precision.DEFAULT, preferred_element_type=F32
        )
    return total


def roll(value, shift, axis):
    size = value.shape[axis]
    return pltpu.roll(value, shift % size, axis)


def lanes_of(value):
    return iota(value.shape, 1)


def neighbours(axis):
    at = lax.axis_index(axis)
    return (at > 0).astype(F32), (at < lax.axis_size(axis) - 1).astype(F32)


def is_even():
    return lax.axis_index("gy") % 2 == 0


def write_pair(even_ref, odd_ref, rows, up, down):
    even_ref[rows, :] = jnp.where(is_even(), up, down)
    odd_ref[rows, :] = jnp.where(is_even(), down, up)


def read_pair(even, odd):
    has_below, has_above = neighbours("gy")
    return jnp.where(is_even(), odd, even) * has_below, jnp.where(is_even(), even, odd) * has_above


def spread_matrix(z):
    y, lane = iota((8, 128), 0), iota((8, 128), 1)
    return (lane == 8 * (y + 4) + z + 1).astype(F32)


def pack_kernel(inputs_ref, own_ref, right_ref, left_ref):
    own = jnp.zeros((80, 128), F32)
    for z in range(NZ):
        values = inputs_ref[pl.ds(z, 80, stride=NZ), :]
        movable = 1.0 - values[24:48]
        piece = jnp.concatenate([movable * values[0:24], movable, values[48:80]], axis=0)
        own = own + dot_picks(piece, spread_matrix(z))
    own_ref[...] = own
    lane = iota((8, 128), 1)
    row = iota((8, 128), 0)
    design = roll(own[72:80], -32, 1)
    for out_ref, edge, first in ((right_ref, 7, 4), (left_ref, 0, 0)):
        edges = jnp.zeros((8, 128), F32)
        for field in range(6):
            line = own[8 * field + edge : 8 * field + edge + 1]
            edges = jnp.where(row == field, line, edges)
        out_ref[0:8, :] = jnp.where(lane < 64, design, roll(edges, 32, 1))
        upper = [own[48 + 8 * c : 56 + 8 * c] for c in range(3)]
        if first == 4:
            upper = [upper[0], upper[1], upper[2]]
            a = jnp.where(row < 4, roll(upper[0], 4, 0), upper[1])
            b = roll(upper[2], 4, 0)
        else:
            a = jnp.where(row < 4, upper[0], roll(upper[1], 4, 0))
            b = upper[2]
        out_ref[8:16, :] = jnp.where(lane < 64, roll(a, -32, 1), roll(b, 32, 1))


def widen_kernel(after_ref, own_ref, from_left_ref, from_right_ref, fields_ref, design_ref, even_ref, odd_ref):
    has_left, has_right = neighbours("gx")
    lane = iota((8, 128), 1)
    row = iota((8, 128), 0)
    middle = (lane >= 32) & (lane < 96)
    left, right = from_left_ref[...] * has_left, from_right_ref[...] * has_right
    rows_left = jnp.where(middle, roll(left[0:8], -32, 1), 0.0)
    rows_right = jnp.where(middle, roll(right[0:8], -32, 1), 0.0)
    design = jnp.concatenate([left[0:8], roll(own_ref[72:80, :], -32, 1), right[0:8]], axis=0)
    design_ref[...] = design
    tall_lane = iota((24, 128), 1)
    design = jnp.where(tall_lane < 64, design, 0.0)
    edges_up = [jnp.zeros((8, 128), F32), jnp.zeros((8, 128), F32)]
    edges_down = [jnp.zeros((8, 128), F32), jnp.zeros((8, 128), F32)]
    for field in range(6):
        own = own_ref[8 * field : 8 * field + 8, :]
        turned = roll(own, 4, 0)
        low = jnp.where(row >= 4, turned, jnp.where(row == 3, rows_left[field : field + 1], 0.0))
        high = jnp.where(row < 4, turned, jnp.where(row == 4, rows_right[field : field + 1], 0.0))
        fields_ref[16 * field : 16 * field + 8, :] = low
        fields_ref[16 * field + 8 : 16 * field + 16, :] = high
        at = 64 + 8 * field
        place = (lane >= at) & (lane < at + 8)
        for half, value in enumerate((low, high)):
            edges_up[half] = jnp.where(place, roll(value, at - 88, 1), edges_up[half])
            edges_down[half] = jnp.where(place, roll(value, at - 32, 1), edges_down[half])
    zeros = jnp.zeros((8, 128), F32)
    write_pair(
        even_ref, odd_ref, slice(0, 24),
        jnp.where(tall_lane < 64, design, jnp.concatenate(edges_up + [zeros], axis=0)),
        jnp.where(tall_lane < 64, design, jnp.concatenate(edges_down + [zeros], axis=0)),
    )
    state_left, state_right = left[8:16], right[8:16]
    ups = [zeros, zeros]
    downs = [zeros, zeros]
    for c in range(3):
        turned = roll(own_ref[48 + 8 * c : 56 + 8 * c, :], 4, 0)
        lane_turn = 32 if c < 2 else -32
        got_left = jnp.where(middle, roll(state_left, lane_turn, 1), 0.0)
        got_right = jnp.where(middle, roll(state_right, lane_turn, 1), 0.0)
        if c == 1:
            got_left = roll(got_left, 4, 0)
        else:
            got_right = roll(got_right, 4, 0)
        low = jnp.where(row >= 4, turned, got_left)
        high = jnp.where(row < 4, turned, got_right)
        fields_ref[96 + 16 * c : 104 + 16 * c, :] = low
        fields_ref[104 + 16 * c : 112 + 16 * c, :] = high
        place = (lane >= 32 * c) & (lane < 32 * c + 32)
        for half, value in enumerate((low, high)):
            ups[half] = jnp.where(place, roll(value, 32 * c - 64, 1), ups[half])
            downs[half] = jnp.where(place, roll(value, 32 * c - 32, 1), downs[half])
    for half in range(2):
        write_pair(even_ref, odd_ref, slice(24 + 8 * half, 32 + 8 * half), ups[half], downs[half])


def gather_matrix():
    row, lane = iota((128, 128), 0), iota((128, 128), 1)
    block_y, block_z = row // 32, (row // 16) % 2
    t, u = (row // 4) % 4, row % 4
    return (lane == 8 * (2 * block_y + t + 3) + 2 * block_z + u).astype(F32)


def group_transpose(value):
    row, group = iota((8, 128), 0), iota((8, 128), 1) // 16
    for d in (1, 2, 4):
        row_bit, group_bit = (row // d) % 2, (group // d) % 2
        down = roll(roll(value, d, 0), -16 * d, 1)
        up = roll(roll(value, -d, 0), 16 * d, 1)
        moved = jnp.where(row_bit == 1, down, up)
        value = jnp.where(row_bit == group_bit, value, moved)
    return value


def turn(field, turned_ref):
    row, lane = iota((80, 128), 0), iota((80, 128), 1)
    block_z, pair, tt, u = row // 40, (row // 8) % 5, (row // 4) % 2, row % 4
    pick = (lane == 8 * (2 * pair + tt + 3) + 2 * block_z + u).astype(F32)
    turned_ref[:, 0:48] = dot_picks(pick, field, ((1,), (1,)), exact_left=True)


def solve_columns(blocks_y, block_z, matrices, turned_ref, solved_ref):
    totals = {}
    for pair in range(5):
        uses = [(block_y, pair - block_y) for block_y in blocks_y if 0 <= pair - block_y < 2]
        at = 40 * block_z + 8 * pair
        values = turned_ref[at : at + 8, 0:48]
        for c in range(3 if uses else 0):
            for x in range(10):
                entry = jnp.broadcast_to(values[:, 16 * c + x + 3 : 16 * c + x + 4], (8, 192))
                for block_y, half in uses:
                    for a in range(4):
                        s = x - 2 * a
                        if 0 <= s < 4:
                            j = 64 * c + 16 * s + 8 * half
                            term = matrices[block_y][a, block_y // 2, block_z, j : j + 8, :] * entry
                            key = (block_y, a)
                            totals[key] = totals[key] + term if key in totals else term
    for (block_y, a), total in totals.items():
        at = 8 * a + 2 * block_y + block_z
        solved_ref[at : at + 1, 0:192] = jnp.sum(total, axis=0, keepdims=True)


def place_blocks(solved_ref, placed_ref):
    placed_ref[...] = jnp.zeros((48, 128), F32)
    for a in range(4):
        first = group_transpose(solved_ref[8 * a : 8 * a + 8, 0:128])
        second = group_transpose(solved_ref[8 * a : 8 * a + 8, 128:256])
        for c, piece in enumerate((first[0:4], first[4:8], second[0:4])):
            at = 16 * c + 2 * a + 3
            placed_ref[at : at + 4, :] = placed_ref[at : at + 4, :] + piece
    return dot_picks(placed_ref[...], gather_matrix())


INNER, OUTER = (1, 2), (0, 3)


def bring(blocks_y, stored_ref, kept_ref, arrived):
    copies = {}
    for block_z in range(2):
        for block_y in blocks_y:
            copies[block_y, block_z] = pltpu.make_async_copy(
                stored_ref.at[:, block_y, block_z],
                kept_ref.at[:, block_y // 2, block_z],
                arrived.at[2 * (block_y // 2) + block_z],
            )
            copies[block_y, block_z].start()
    return copies


def outer_kernel(own_ref, stored_ref, kept_ref, arrived):
    for copy in bring(OUTER, stored_ref, kept_ref, arrived).values():
        copy.wait()


def inner_kernel(fields_ref, stored_ref, kept_ref, solved_ref, turned_ref, arrived):
    copies = bring(INNER, stored_ref, kept_ref, arrived)
    turn(fields_ref[0:48, :], turned_ref)
    for block_z in range(2):
        for block_y in INNER:
            copies[block_y, block_z].wait()
        solve_columns(INNER, block_z, {y: kept_ref for y in INNER}, turned_ref, solved_ref)


SOLVE_SCRATCH = [
    pltpu.VMEM((80, 128), F32),
    pltpu.VMEM((32, 256), F32),
    pltpu.VMEM((48, 128), F32),
]


def sum_rows(value):
    total = value[0:8]
    for at in range(8, value.shape[0], 8):
        total = total + value[at : at + 8]
    return total


def halves(value, low_ref, high_ref):
    for c in range(3):
        low_ref[8 * c : 8 * c + 8, :] = value[16 * c : 16 * c + 8]
        high_ref[8 * c : 8 * c + 8, :] = value[16 * c + 8 : 16 * c + 16]


def joined(low, high):
    parts = []
    for c in range(3):
        parts += [low[8 * c : 8 * c + 8], high[8 * c : 8 * c + 8]]
    return jnp.concatenate(parts, axis=0)


def first_kernel(
    fields_ref, even_ref, odd_ref, outer_ref, inner_ref, matrix_ref,
    residual_ref, movable_ref, low_ref, high_ref, rho_ref,
    turned_ref, solved_ref, placed_ref,
):
    lane = iota((16, 128), 1)
    below, above = read_pair(even_ref[0:16, :], odd_ref[0:16, :])
    at_below = (lane >= 24) & (lane < 32)
    at_above = (lane >= 96) & (lane < 104)
    for field in range(6):
        value = fields_ref[16 * field : 16 * field + 16, :]
        at = 64 + 8 * field
        value = jnp.where(at_below, roll(below, 24 - at, 1), value)
        value = jnp.where(at_above, roll(above, 96 - at, 1), value)
        out_ref = residual_ref if field < 3 else movable_ref
        out_ref[16 * (field % 3) : 16 * (field % 3) + 16, :] = value
    residual = residual_ref[...]
    solved_ref[...] = inner_ref[...]
    turn(residual, turned_ref)
    for block_z in range(2):
        solve_columns(OUTER, block_z, {y: outer_ref for y in OUTER}, turned_ref, solved_ref)
    solved = place_blocks(solved_ref, placed_ref) * movable_ref[...]
    rho_ref[...] = sum_rows(residual * solved)
    inverse = outer_ref[0, 0, 0, 0:1, 0:1] * matrix_ref[0:1, 0:1]
    slot = lanes_of(solved) % 8
    solved = jnp.where(slot == FACTOR, 1.0 / inverse, jnp.where(slot == INVERSE, inverse, solved))
    halves(solved, low_ref, high_ref)


FACTOR, INVERSE = 6, 7
LEFT, RIGHT, EVEN, ODD, MINE, MINE_INVERSE = range(0, 48, 8)


def tall(tile):
    return jnp.concatenate([tile] * 3, axis=0)


def cross_kernel(low_ref, high_ref, from_left_ref, from_right_ref, *refs):
    *ratios, low_out, high_out, even_ref, odd_ref = refs
    has_left, has_right = neighbours("gx")
    low, high = low_ref[...], high_ref[...]
    left, right = from_left_ref[...] * has_left, from_right_ref[...] * has_right
    lane = iota((24, 128), 1)
    if ratios:
        low = low + left * tall(ratios[0][LEFT : LEFT + 8, :])
        high = high + right * tall(ratios[0][RIGHT : RIGHT + 8, :])
    else:
        node = lane % 8 < FACTOR
        low = low + jnp.where(node, left, 0.0)
        high = high + jnp.where(node, right, 0.0)
    low_out[...] = low
    high_out[...] = high
    write_pair(
        even_ref, odd_ref, slice(0, 24),
        jnp.where(lane < 64, roll(low, 64, 1), high),
        jnp.where(lane < 64, low, roll(high, 64, 1)),
    )


def add_sides(low, high, even, odd):
    lane = iota((24, 128), 1)
    below, above = read_pair(even, odd)
    low = low + jnp.where(lane < 64, below, roll(above, 64, 1))
    high = high + jnp.where(lane < 64, roll(below, 64, 1), above)
    return joined(low, high)


def corner_fields(vector):
    fields = []
    for q in range(8):
        a, b, c_z = q % 2, (q // 2) % 2, q // 4
        for c in range(3):
            value = vector[16 * c : 16 * c + 16]
            if a:
                value = roll(value, -1, 0)
            if b or c_z:
                value = roll(value, -(8 * b + c_z), 1)
            fields.append(value)
    return fields


def push(stiff_ref, stack_ref, rows):
    totals = [None] * len(rows)
    for j in range(24):
        value = stack_ref[16 * j : 16 * j + 16, :]
        for n, i in enumerate(rows):
            product = stiff_ref[24 * j + i : 24 * j + i + 1, :] * value
            totals[n] = product if j == 0 else totals[n] + product
    return totals


def stack_fields(vector, stack_ref):
    for j, value in enumerate(corner_fields(vector)):
        stack_ref[16 * j : 16 * j + 16, :] = value


def global_weights(shape, position, total):
    weight = jnp.zeros(shape, F32)
    for d in range(-3, 4):
        inside = (position + d >= 0) & (position + d < total)
        weight = weight + jnp.where(inside, 4.0 - abs(d), 0.0)
    return weight


def hat(distance):
    return jnp.maximum(0, 4 - jnp.abs(distance)).astype(F32)


def side_kernel(
    matrix_ref, fields_ref, design_ref, even_ref, odd_ref,
    stiff_ref, scale_ref, weight_ref, pushed_ref, stack_ref,
):
    total_x, total_y = C * lax.axis_size("gx"), C * lax.axis_size("gy")
    for j in range(24):
        stiff_ref[24 * j : 24 * j + 24, :] = jnp.broadcast_to(matrix_ref[:, j : j + 1], (24, 128))
    below, above = read_pair(even_ref[...], odd_ref[...])
    lane24 = iota((24, 128), 1)
    design = jnp.where(lane24 < 64, design_ref[...], roll(above[0:24], 64, 1))
    row, col = iota((16, 24), 0), iota((16, 24), 1)
    along_x = hat((col - 8) - (row - 4))
    source, target = iota((128, 128), 0), iota((128, 128), 1)
    y_target, z_target = target // 8 - 4, target % 8 - 1
    y_source, z_source = source // 8, source % 8 - 1
    z_valid = (z_target >= 0) & (z_target < NZ) & (z_source >= 0) & (z_source < NZ)
    along_z = jnp.where(z_valid, hat(z_source - z_target), 0.0)
    smooth_in = along_z * hat(y_source - y_target)
    smooth_below = jnp.where(source < 64, along_z * hat(y_source - 8 - y_target), 0.0)
    summed = dot(dot(along_x, design), smooth_in) + dot(dot(along_x, below[0:24]), smooth_below)
    row16, lane16 = iota((16, 128), 0), iota((16, 128), 1)
    z = lane16 % 8 - 1
    x = row16 - 4 + C * lax.axis_index("gx")
    y = lane16 // 8 - 4 + C * lax.axis_index("gy")
    shape = (16, 128)
    normalizer = (
        global_weights(shape, x, total_x) * global_weights(shape, y, total_y) * global_weights(shape, z, NZ)
    )
    inside = (x >= 0) & (x < total_x) & (y >= 0) & (y < total_y) & (z >= 0) & (z < NZ)
    normalizer = jnp.where(inside, normalizer, 1.0)
    density = jnp.where(inside, summed / normalizer, 0.0)
    scale_ref[...] = density * density * density
    weight_ref[...] = -3.0 * density * density / normalizer
    lane = iota((16, 128), 1)
    parts = []
    for c in range(3):
        value = fields_ref[96 + 16 * c : 112 + 16 * c, :]
        value = jnp.where(lane < 32, roll(below[24:40], -32 * c, 1), value)
        value = jnp.where(lane >= 96, roll(above[24:40], 96 - 32 * c, 1), value)
        parts.append(value)
    stack_fields(jnp.concatenate(parts, axis=0), stack_ref)
    for i in range(0, 24, 4):
        rows = list(range(i, i + 4))
        for n, value in zip(rows, push(stiff_ref, stack_ref, rows)):
            pushed_ref[16 * n : 16 * n + 16, :] = value


def second_kernel(
    from_left_ref, from_right_ref, low_ref, high_ref, even_ref, odd_ref, stiff_ref, scale_ref,
    residual_ref, movable_ref, outer_ref, inner_ref,
    direction_ref, low_out, high_out, sums_ref, ratios_ref,
    stack_ref, turned_ref, solved_ref, placed_ref,
):
    direction = add_sides(low_ref[...], high_ref[...], even_ref[...], odd_ref[...])
    factor, inverse = low_ref[0:1, FACTOR : FACTOR + 1], low_ref[0:1, INVERSE : INVERSE + 1]
    for at, ref in ((LEFT, from_left_ref), (RIGHT, from_right_ref), (EVEN, even_ref), (ODD, odd_ref)):
        ratios_ref[at : at + 8, :] = jnp.broadcast_to(factor * ref[0:1, INVERSE : INVERSE + 1], (8, 128))
    ratios_ref[MINE : MINE + 8, :] = jnp.broadcast_to(factor, (8, 128))
    ratios_ref[MINE_INVERSE : MINE_INVERSE + 8, :] = jnp.broadcast_to(inverse, (8, 128))
    direction_ref[...] = direction
    stack_fields(direction, stack_ref)
    scale = scale_ref[...]
    row16, lane16 = iota((16, 128), 0), iota((16, 128), 1)
    own = (row16 >= 4) & (row16 < 12) & (lane16 >= 32) & (lane16 < 96)
    parts = {}
    for q in range(8):
        a, lanes = q % 2, 8 * ((q // 2) % 2) + q // 4
        rows = [3 * q, 3 * q + 1, 3 * q + 2]
        for c, value in enumerate(push(stiff_ref, stack_ref, rows)):
            value = value * scale
            if a:
                value = roll(value, 1, 0)
            parts[c, lanes] = parts[c, lanes] + value if (c, lanes) in parts else value
    image = []
    for c in range(3):
        value = parts[c, 0]
        for lanes in (1, 8, 9):
            value = value + roll(parts[c, lanes], lanes, 1)
        image.append(value)
    image = jnp.concatenate(image, axis=0) * movable_ref[...]
    turn(image, turned_ref)
    matrices = {0: outer_ref, 1: inner_ref, 2: inner_ref, 3: outer_ref}
    for block_z in range(2):
        solve_columns(range(4), block_z, matrices, turned_ref, solved_ref)
    solved = place_blocks(solved_ref, placed_ref) * movable_ref[...]
    solved = solved * factor
    halves(solved, low_out, high_out)
    product = direction * image
    product = product[0:16] + product[16:32] + product[32:48]
    sums_ref[0:8, :] = sum_rows(jnp.where(own, product, 0.0))
    sums_ref[8:16, :] = sum_rows(residual_ref[...] * solved)
    sums_ref[16:24, :] = sum_rows(image * solved)


def third_kernel(
    low_ref, high_ref, even_ref, odd_ref, stiff_ref, scale_ref,
    rho_ref, sums_ref, ratios_ref,
    wide_ref, share_ref, stack_ref,
):
    wide = add_sides(
        low_ref[...], high_ref[...],
        even_ref[...] * tall(ratios_ref[EVEN : EVEN + 8, :]), odd_ref[...] * tall(ratios_ref[ODD : ODD + 8, :]),
    )
    wide_ref[...] = wide
    stack_fields(wide, stack_ref)
    row16, lane16 = iota((16, 128), 0), iota((16, 128), 1)
    own = (row16 >= 4) & (row16 < 12) & (lane16 >= 32) & (lane16 < 96)
    scale = jnp.where(own, scale_ref[...], 0.0)
    both = jnp.zeros((16, 128), F32)
    for i in range(0, 24, 4):
        rows = list(range(i, i + 4))
        for n, value in zip(rows, push(stiff_ref, stack_ref, rows)):
            both = both + value * stack_ref[16 * n : 16 * n + 16, :]
    sums = [
        rho_ref[...], sums_ref[0:8, :], sums_ref[8:16, :], sums_ref[16:24, :],
        sum_rows(both * scale),
    ]
    row, lane = iota((8, 128), 0), iota((8, 128), 1)
    table = jnp.zeros((8, 128), F32)
    for n, value in enumerate(sums):
        table = jnp.where(row == n, jnp.sum(value, axis=0, keepdims=True), table)
    table = jnp.where(row == lane, jnp.sum(table, axis=1, keepdims=True), 0.0)
    line = jnp.sum(table, axis=0, keepdims=True)
    line = jnp.where(lanes_of(line) == 6, ratios_ref[MINE_INVERSE : MINE_INVERSE + 1, :], line)
    share_ref[...] = jnp.broadcast_to(line, share_ref.shape)


def last_kernel(shares_ref, direction_ref, wide_ref, ratios_ref, weight_ref, pushed_ref, adjoint_ref, gradient_ref, smooth_ref):
    shares = shares_ref[...]
    ratio = shares[:, 6:7] * ratios_ref[MINE : MINE + 1, :]
    lane = lanes_of(shares)
    weights = jnp.where(lane < 2, 1.0, jnp.where(lane == 4, ratio * ratio, ratio))
    line = jnp.sum(sum_rows(shares * weights), axis=0, keepdims=True)
    rho, curve, cross, image_wide, both = [line[:, n : n + 1] for n in range(5)]
    step = rho / curve
    unscale = step * ratios_ref[MINE_INVERSE : MINE_INVERSE + 1, 0:1]
    cross, image_wide, both = cross * unscale, image_wide * unscale, both * (unscale * unscale)
    rho_next = rho - cross - step * curve + step * image_wide
    grow = 1.0 + rho_next / rho
    curve_next = grow * grow * curve - 2.0 * grow * image_wide + both
    step_next = rho_next / curve_next
    adjoint = (step + step_next * grow) * direction_ref[...] - (step_next * unscale) * wide_ref[...]
    source, target = iota((128, 32), 0), iota((128, 32), 1)
    y, z = target % 8, target // 8
    pick = (source == 8 * (y + 4) + z + 1).astype(F32)
    own = dot_picks(jnp.concatenate([adjoint[16 * c + 4 : 16 * c + 12] for c in range(3)], axis=0), pick)
    for z_out in range(NZ):
        adjoint_ref[pl.ds(z_out, 24, stride=NZ), :] = own[:, 8 * z_out : 8 * z_out + 8]
    terms = [value * pushed_ref[16 * j : 16 * j + 16, :] for j, value in enumerate(corner_fields(adjoint))]
    while len(terms) > 1:
        terms = [sum(terms[n : n + 3]) for n in range(0, len(terms), 3)]
    energy = terms[0]
    sensitivity = energy * weight_ref[...]
    y_source, z_source = source // 8 - 4, source % 8 - 1
    valid = (z_source >= 0) & (z_source < NZ)
    smooth_ref[...] = dot_picks(sensitivity, jnp.where(valid, hat(y_source - y) * hat(z_source - z), 0.0))
    gradient = 4.0 * smooth_ref[4:12, :]
    for d in range(1, 4):
        gradient = gradient + (4.0 - d) * (smooth_ref[4 - d : 12 - d, :] + smooth_ref[4 + d : 12 + d, :])
    for z_out in range(NZ):
        gradient_ref[pl.ds(z_out, 8, stride=NZ), :] = gradient[:, 8 * z_out : 8 * z_out + 8]


def call(kernel, outs, scratch=(), specs=None, limit=VMEM_LIMIT):
    shapes = [jax.ShapeDtypeStruct(shape, F32) for shape in outs]
    return lambda *args: pl.pallas_call(
        kernel,
        out_shape=shapes,
        in_specs=specs or [VM] * len(args),
        out_specs=[VM] * len(shapes),
        scratch_shapes=list(scratch),
        compiler_params=pltpu.CompilerParams(vmem_limit_bytes=limit),
        cost_estimate=pl.CostEstimate(flops=10**6, bytes_accessed=10**6, transcendentals=0),
    )(*args)


def shifted(value, axis, step):
    size = lax.axis_size(axis)
    return lax.ppermute(value, axis, [(i, (i + step) % size) for i in range(size)])


def both_ways(to_next, to_previous, axis):
    return shifted(to_next, axis, 1), shifted(to_previous, axis, -1)


def paired(even, odd):
    size_x, size_y = lax.axis_size("gx"), lax.axis_size("gy")
    pairs = []
    for i in range(size_x):
        for j in range(size_y):
            inside = 0 < j < size_y - 1
            other = (i, j + 1 if j % 2 else j - 1) if inside else (i ^ 1, j)
            pairs.append((i * size_y + j, other[0] * size_y + other[1]))
    from_even = lax.ppermute(even, "gy", [(j, j ^ 1) for j in range(size_y)])
    return from_even, lax.ppermute(odd, ("gx", "gy"), pairs)


def as_rows(values):
    return jnp.swapaxes(values, -1, -2).reshape((-1, C))


def from_rows(values, shape):
    return jnp.swapaxes(values.reshape(shape[:-2] + (NZ, C)), -1, -2)


def local(design, element_matrix, fixed, inverses, state, load):
    size_x, size_y = lax.axis_size("gx"), lax.axis_size("gy")
    inputs = sum(
        jnp.pad(value, [(first, 10 - first - value.shape[0])] + [(0, 0)] * 3)
        for first, value in ((0, load), (6, state), (9, design[None]))
    )
    inputs = inputs + jnp.pad(fixed, [(3, 4)] + [(0, 0)] * 3).astype(F32)
    own, to_right, to_left = call(pack_kernel, [(80, 128), (16, 128), (16, 128)])(as_rows(inputs))
    left, right = both_ways(to_right, to_left, "gx")
    size_a, size_b, *rest = inverses.shape
    half = (size_a, size_b // 2, *rest)
    mixed_specs = [VM, pl.BlockSpec(memory_space=pl.ANY)]
    arrived = pltpu.SemaphoreType.DMA((4,))
    (outer,) = call(outer_kernel, [half], [arrived], mixed_specs, BRING_LIMIT)(own, inverses)
    fields, design_wide, even, odd = call(widen_kernel, [(144, 128), (24, 128), (40, 128), (40, 128)])(
        outer, own, left, right
    )
    even, odd = paired(even, odd)
    inner, solved = call(
        inner_kernel, [half, (32, 256)], [pltpu.VMEM((80, 128), F32), arrived], mixed_specs, BRING_LIMIT
    )(fields, inverses)
    residual, movable, low, high, rho = call(
        first_kernel, [(48, 128), (48, 128), (24, 128), (24, 128), (8, 128)], SOLVE_SCRATCH
    )(fields, even, odd, outer, solved, element_matrix)
    stiff, scale, weight, pushed = call(
        side_kernel,
        [(576, 128), (16, 128), (16, 128), (384, 128)],
        [pltpu.VMEM((384, 128), F32)],
    )(element_matrix, fields, design_wide, even, odd)

    def crossed(low, high, *ratios):
        left, right = both_ways(high, low, "gx")
        low, high, even, odd = call(cross_kernel, [(24, 128)] * 4)(low, high, left, right, *ratios)
        return left, right, low, high, *paired(even, odd)

    sides = crossed(low, high)
    direction, low, high, sums, ratios = call(
        second_kernel,
        [(48, 128), (24, 128), (24, 128), (24, 128), (48, 128)],
        [pltpu.VMEM((384, 128), F32)] + SOLVE_SCRATCH,
    )(*sides, stiff, scale, residual, movable, outer, inner)
    sides = crossed(low, high, ratios)[2:]
    devices = size_x * size_y
    wide, share = call(
        third_kernel, [(48, 128), (devices, 128)], [pltpu.VMEM((384, 128), F32)]
    )(*sides, stiff, scale, rho, sums, ratios)
    shares = lax.all_to_all(share, ("gx", "gy"), 0, 0, tiled=True)
    adjoint, gradient = call(last_kernel, [(96, C), (32, C)], [pltpu.VMEM((16, 32), F32)])(shares, direction, wide, ratios, weight, pushed)
    return from_rows(adjoint, (3, C, C, NZ)), from_rows(gradient, (C, C, NZ))


def solution(mesh):
    placed = (
        P("gx", "gy", None),
        P(),
        P(None, "gx", "gy", None),
        P("gx", "gy", None, None, None),
        P(None, "gx", "gy", None),
        P(None, "gx", "gy", None),
    )
    return jax.shard_map(
        local,
        mesh=mesh,
        in_specs=placed,
        out_specs=(P(None, "gx", "gy", None), P("gx", "gy", None)),
        check_vma=False,
    )
```

```python
import jax
import jax.numpy as jnp
from jax import lax
from jax.experimental import pallas as pl
from jax.experimental.pallas import tpu as pltpu
from jax.sharding import PartitionSpec as P

C = 8
NZ = 4
F32 = jnp.float32
HIGHEST = lax.Precision.HIGHEST
VMEM_LIMIT = 20 * 1024 * 1024
BRING_LIMIT = 46 * 1024 * 1024
VM = pl.BlockSpec(memory_space=pltpu.VMEM)


def iota(shape, dim):
    return lax.broadcasted_iota(jnp.int32, shape, dim)


def dot(left, right):
    return jnp.dot(left, right, precision=HIGHEST, preferred_element_type=F32)


def parts_of(value):
    parts = []
    for _ in range(3):
        parts.append(value.astype(jnp.bfloat16).astype(F32))
        value = value - parts[-1]
    return parts


def dot_picks(left, right, dims=((1,), (0,)), exact_left=False):
    pairs = [(left, part) for part in parts_of(right)] if exact_left else [(part, right) for part in parts_of(left)]
    total = 0.0
    for first, second in reversed(pairs):
        total = total + lax.dot_general(
            first, second, (dims, ((), ())), precision=lax.Precision.DEFAULT, preferred_element_type=F32
        )
    return total


def roll(value, shift, axis):
    size = value.shape[axis]
    return pltpu.roll(value, shift % size, axis)


def lanes_of(value):
    return iota(value.shape, 1)


def neighbours(axis):
    at = lax.axis_index(axis)
    return (at > 0).astype(F32), (at < lax.axis_size(axis) - 1).astype(F32)


def is_even():
    return lax.axis_index("gy") % 2 == 0


def write_pair(even_ref, odd_ref, rows, up, down):
    even_ref[rows, :] = jnp.where(is_even(), up, down)
    odd_ref[rows, :] = jnp.where(is_even(), down, up)


def read_pair(even, odd):
    has_below, has_above = neighbours("gy")
    return jnp.where(is_even(), odd, even) * has_below, jnp.where(is_even(), even, odd) * has_above


def spread_matrix(z):
    y, lane = iota((8, 128), 0), iota((8, 128), 1)
    return (lane == 8 * (y + 4) + z + 1).astype(F32)


def pack_kernel(inputs_ref, own_ref, right_ref, left_ref):
    own = jnp.zeros((80, 128), F32)
    for z in range(NZ):
        values = inputs_ref[pl.ds(z, 80, stride=NZ), :]
        movable = 1.0 - values[24:48]
        piece = jnp.concatenate([movable * values[0:24], movable, values[48:80]], axis=0)
        own = own + dot_picks(piece, spread_matrix(z))
    own_ref[...] = own
    lane = iota((8, 128), 1)
    row = iota((8, 128), 0)
    design = roll(own[72:80], -32, 1)
    for out_ref, edge, first in ((right_ref, 7, 4), (left_ref, 0, 0)):
        edges = jnp.zeros((8, 128), F32)
        for field in range(6):
            line = own[8 * field + edge : 8 * field + edge + 1]
            edges = jnp.where(row == field, line, edges)
        out_ref[0:8, :] = jnp.where(lane < 64, design, roll(edges, 32, 1))
        upper = [own[48 + 8 * c : 56 + 8 * c] for c in range(3)]
        if first == 4:
            upper = [upper[0], upper[1], upper[2]]
            a = jnp.where(row < 4, roll(upper[0], 4, 0), upper[1])
            b = roll(upper[2], 4, 0)
        else:
            a = jnp.where(row < 4, upper[0], roll(upper[1], 4, 0))
            b = upper[2]
        out_ref[8:16, :] = jnp.where(lane < 64, roll(a, -32, 1), roll(b, 32, 1))


def widen_kernel(after_ref, own_ref, from_left_ref, from_right_ref, fields_ref, design_ref, even_ref, odd_ref):
    has_left, has_right = neighbours("gx")
    lane = iota((8, 128), 1)
    row = iota((8, 128), 0)
    middle = (lane >= 32) & (lane < 96)
    left, right = from_left_ref[...] * has_left, from_right_ref[...] * has_right
    rows_left = jnp.where(middle, roll(left[0:8], -32, 1), 0.0)
    rows_right = jnp.where(middle, roll(right[0:8], -32, 1), 0.0)
    design = jnp.concatenate([left[0:8], roll(own_ref[72:80, :], -32, 1), right[0:8]], axis=0)
    design_ref[...] = design
    tall_lane = iota((24, 128), 1)
    design = jnp.where(tall_lane < 64, design, 0.0)
    edges_up = [jnp.zeros((8, 128), F32), jnp.zeros((8, 128), F32)]
    edges_down = [jnp.zeros((8, 128), F32), jnp.zeros((8, 128), F32)]
    for field in range(6):
        own = own_ref[8 * field : 8 * field + 8, :]
        turned = roll(own, 4, 0)
        low = jnp.where(row >= 4, turned, jnp.where(row == 3, rows_left[field : field + 1], 0.0))
        high = jnp.where(row < 4, turned, jnp.where(row == 4, rows_right[field : field + 1], 0.0))
        fields_ref[16 * field : 16 * field + 8, :] = low
        fields_ref[16 * field + 8 : 16 * field + 16, :] = high
        at = 64 + 8 * field
        place = (lane >= at) & (lane < at + 8)
        for half, value in enumerate((low, high)):
            edges_up[half] = jnp.where(place, roll(value, at - 88, 1), edges_up[half])
            edges_down[half] = jnp.where(place, roll(value, at - 32, 1), edges_down[half])
    zeros = jnp.zeros((8, 128), F32)
    write_pair(
        even_ref, odd_ref, slice(0, 24),
        jnp.where(tall_lane < 64, design, jnp.concatenate(edges_up + [zeros], axis=0)),
        jnp.where(tall_lane < 64, design, jnp.concatenate(edges_down + [zeros], axis=0)),
    )
    state_left, state_right = left[8:16], right[8:16]
    ups = [zeros, zeros]
    downs = [zeros, zeros]
    for c in range(3):
        turned = roll(own_ref[48 + 8 * c : 56 + 8 * c, :], 4, 0)
        lane_turn = 32 if c < 2 else -32
        got_left = jnp.where(middle, roll(state_left, lane_turn, 1), 0.0)
        got_right = jnp.where(middle, roll(state_right, lane_turn, 1), 0.0)
        if c == 1:
            got_left = roll(got_left, 4, 0)
        else:
            got_right = roll(got_right, 4, 0)
        low = jnp.where(row >= 4, turned, got_left)
        high = jnp.where(row < 4, turned, got_right)
        fields_ref[96 + 16 * c : 104 + 16 * c, :] = low
        fields_ref[104 + 16 * c : 112 + 16 * c, :] = high
        place = (lane >= 32 * c) & (lane < 32 * c + 32)
        for half, value in enumerate((low, high)):
            ups[half] = jnp.where(place, roll(value, 32 * c - 64, 1), ups[half])
            downs[half] = jnp.where(place, roll(value, 32 * c - 32, 1), downs[half])
    for half in range(2):
        write_pair(even_ref, odd_ref, slice(24 + 8 * half, 32 + 8 * half), ups[half], downs[half])


def gather_matrix():
    row, lane = iota((128, 128), 0), iota((128, 128), 1)
    block_y, block_z = row // 32, (row // 16) % 2
    t, u = (row // 4) % 4, row % 4
    return (lane == 8 * (2 * block_y + t + 3) + 2 * block_z + u).astype(F32)


def group_transpose(value):
    row, group = iota((8, 128), 0), iota((8, 128), 1) // 16
    for d in (1, 2, 4):
        row_bit, group_bit = (row // d) % 2, (group // d) % 2
        down = roll(roll(value, d, 0), -16 * d, 1)
        up = roll(roll(value, -d, 0), 16 * d, 1)
        moved = jnp.where(row_bit == 1, down, up)
        value = jnp.where(row_bit == group_bit, value, moved)
    return value


def turn(field, turned_ref):
    row, lane = iota((80, 128), 0), iota((80, 128), 1)
    block_z, pair, tt, u = row // 40, (row // 8) % 5, (row // 4) % 2, row % 4
    pick = (lane == 8 * (2 * pair + tt + 3) + 2 * block_z + u).astype(F32)
    turned_ref[:, 0:48] = dot_picks(pick, field, ((1,), (1,)), exact_left=True)


def solve_columns(blocks_y, block_z, matrices, turned_ref, solved_ref):
    totals = {}
    for pair in range(5):
        uses = [(block_y, pair - block_y) for block_y in blocks_y if 0 <= pair - block_y < 2]
        at = 40 * block_z + 8 * pair
        values = turned_ref[at : at + 8, 0:48]
        for c in range(3 if uses else 0):
            for x in range(10):
                entry = jnp.broadcast_to(values[:, 16 * c + x + 3 : 16 * c + x + 4], (8, 192))
                for block_y, half in uses:
                    for a in range(4):
                        s = x - 2 * a
                        if 0 <= s < 4:
                            j = 64 * c + 16 * s + 8 * half
                            term = matrices[block_y][a, block_y // 2, block_z, j : j + 8, :] * entry
                            key = (block_y, a)
                            totals[key] = totals[key] + term if key in totals else term
    for (block_y, a), total in totals.items():
        at = 8 * a + 2 * block_y + block_z
        solved_ref[at : at + 1, 0:192] = jnp.sum(total, axis=0, keepdims=True)


def place_blocks(solved_ref, placed_ref):
    placed_ref[...] = jnp.zeros((48, 128), F32)
    for a in range(4):
        first = group_transpose(solved_ref[8 * a : 8 * a + 8, 0:128])
        second = group_transpose(solved_ref[8 * a : 8 * a + 8, 128:256])
        for c, piece in enumerate((first[0:4], first[4:8], second[0:4])):
            at = 16 * c + 2 * a + 3
            placed_ref[at : at + 4, :] = placed_ref[at : at + 4, :] + piece
    return dot_picks(placed_ref[...], gather_matrix())


INNER, OUTER = (1, 2), (0, 3)


def bring(blocks_y, stored_ref, kept_ref, arrived):
    copies = {}
    for block_z in range(2):
        for block_y in blocks_y:
            copies[block_y, block_z] = pltpu.make_async_copy(
                stored_ref.at[:, block_y, block_z],
                kept_ref.at[:, block_y // 2, block_z],
                arrived.at[2 * (block_y // 2) + block_z],
            )
            copies[block_y, block_z].start()
    return copies


def outer_kernel(own_ref, stored_ref, kept_ref, arrived):
    for copy in bring(OUTER, stored_ref, kept_ref, arrived).values():
        copy.wait()


def inner_kernel(fields_ref, stored_ref, kept_ref, solved_ref, turned_ref, arrived):
    copies = bring(INNER, stored_ref, kept_ref, arrived)
    turn(fields_ref[0:48, :], turned_ref)
    for block_z in range(2):
        for block_y in INNER:
            copies[block_y, block_z].wait()
        solve_columns(INNER, block_z, {y: kept_ref for y in INNER}, turned_ref, solved_ref)


SOLVE_SCRATCH = [
    pltpu.VMEM((80, 128), F32),
    pltpu.VMEM((32, 256), F32),
    pltpu.VMEM((48, 128), F32),
]


def sum_rows(value):
    total = value[0:8]
    for at in range(8, value.shape[0], 8):
        total = total + value[at : at + 8]
    return total


def halves(value, low_ref, high_ref):
    for c in range(3):
        low_ref[8 * c : 8 * c + 8, :] = value[16 * c : 16 * c + 8]
        high_ref[8 * c : 8 * c + 8, :] = value[16 * c + 8 : 16 * c + 16]


def joined(low, high):
    parts = []
    for c in range(3):
        parts += [low[8 * c : 8 * c + 8], high[8 * c : 8 * c + 8]]
    return jnp.concatenate(parts, axis=0)


def first_kernel(
    fields_ref, even_ref, odd_ref, outer_ref, inner_ref, matrix_ref,
    residual_ref, movable_ref, low_ref, high_ref, rho_ref,
    turned_ref, solved_ref, placed_ref,
):
    lane = iota((16, 128), 1)
    below, above = read_pair(even_ref[0:16, :], odd_ref[0:16, :])
    at_below = (lane >= 24) & (lane < 32)
    at_above = (lane >= 96) & (lane < 104)
    for field in range(6):
        value = fields_ref[16 * field : 16 * field + 16, :]
        at = 64 + 8 * field
        value = jnp.where(at_below, roll(below, 24 - at, 1), value)
        value = jnp.where(at_above, roll(above, 96 - at, 1), value)
        out_ref = residual_ref if field < 3 else movable_ref
        out_ref[16 * (field % 3) : 16 * (field % 3) + 16, :] = value
    residual = residual_ref[...]
    solved_ref[...] = inner_ref[...]
    turn(residual, turned_ref)
    for block_z in range(2):
        solve_columns(OUTER, block_z, {y: outer_ref for y in OUTER}, turned_ref, solved_ref)
    solved = place_blocks(solved_ref, placed_ref) * movable_ref[...]
    rho_ref[...] = sum_rows(residual * solved)
    inverse = outer_ref[0, 0, 0, 0:1, 0:1] * matrix_ref[0:1, 0:1]
    slot = lanes_of(solved) % 8
    solved = jnp.where(slot == FACTOR, 1.0 / inverse, jnp.where(slot == INVERSE, inverse, solved))
    halves(solved, low_ref, high_ref)


FACTOR, INVERSE = 6, 7
LEFT, RIGHT, EVEN, ODD, MINE, MINE_INVERSE = range(0, 48, 8)


def tall(tile):
    return jnp.concatenate([tile] * 3, axis=0)


def cross_kernel(low_ref, high_ref, from_left_ref, from_right_ref, *refs):
    *ratios, low_out, high_out, even_ref, odd_ref = refs
    has_left, has_right = neighbours("gx")
    low, high = low_ref[...], high_ref[...]
    left, right = from_left_ref[...] * has_left, from_right_ref[...] * has_right
    lane = iota((24, 128), 1)
    if ratios:
        low = low + left * tall(ratios[0][LEFT : LEFT + 8, :])
        high = high + right * tall(ratios[0][RIGHT : RIGHT + 8, :])
    else:
        node = lane % 8 < FACTOR
        low = low + jnp.where(node, left, 0.0)
        high = high + jnp.where(node, right, 0.0)
    low_out[...] = low
    high_out[...] = high
    write_pair(
        even_ref, odd_ref, slice(0, 24),
        jnp.where(lane < 64, roll(low, 64, 1), high),
        jnp.where(lane < 64, low, roll(high, 64, 1)),
    )


def add_sides(low, high, even, odd):
    lane = iota((24, 128), 1)
    below, above = read_pair(even, odd)
    low = low + jnp.where(lane < 64, below, roll(above, 64, 1))
    high = high + jnp.where(lane < 64, roll(below, 64, 1), above)
    return joined(low, high)


def corner_fields(vector):
    fields = []
    for q in range(8):
        a, b, c_z = q % 2, (q // 2) % 2, q // 4
        for c in range(3):
            value = vector[16 * c : 16 * c + 16]
            if a:
                value = roll(value, -1, 0)
            if b or c_z:
                value = roll(value, -(8 * b + c_z), 1)
            fields.append(value)
    return fields


def push(stiff_ref, stack_ref, rows):
    totals = [None] * len(rows)
    for j in range(24):
        value = stack_ref[16 * j : 16 * j + 16, :]
        for n, i in enumerate(rows):
            product = stiff_ref[24 * j + i : 24 * j + i + 1, :] * value
            totals[n] = product if j == 0 else totals[n] + product
    return totals


def stack_fields(vector, stack_ref):
    for j, value in enumerate(corner_fields(vector)):
        stack_ref[16 * j : 16 * j + 16, :] = value


def global_weights(shape, position, total):
    weight = jnp.zeros(shape, F32)
    for d in range(-3, 4):
        inside = (position + d >= 0) & (position + d < total)
        weight = weight + jnp.where(inside, 4.0 - abs(d), 0.0)
    return weight


def hat(distance):
    return jnp.maximum(0, 4 - jnp.abs(distance)).astype(F32)


def side_kernel(
    matrix_ref, fields_ref, design_ref, even_ref, odd_ref,
    stiff_ref, scale_ref, weight_ref, pushed_ref, stack_ref,
):
    total_x, total_y = C * lax.axis_size("gx"), C * lax.axis_size("gy")
    for j in range(24):
        stiff_ref[24 * j : 24 * j + 24, :] = jnp.broadcast_to(matrix_ref[:, j : j + 1], (24, 128))
    below, above = read_pair(even_ref[...], odd_ref[...])
    lane24 = iota((24, 128), 1)
    design = jnp.where(lane24 < 64, design_ref[...], roll(above[0:24], 64, 1))
    row, col = iota((16, 24), 0), iota((16, 24), 1)
    along_x = hat((col - 8) - (row - 4))
    source, target = iota((128, 128), 0), iota((128, 128), 1)
    y_target, z_target = target // 8 - 4, target % 8 - 1
    y_source, z_source = source // 8, source % 8 - 1
    z_valid = (z_target >= 0) & (z_target < NZ) & (z_source >= 0) & (z_source < NZ)
    along_z = jnp.where(z_valid, hat(z_source - z_target), 0.0)
    smooth_in = along_z * hat(y_source - y_target)
    smooth_below = jnp.where(source < 64, along_z * hat(y_source - 8 - y_target), 0.0)
    summed = dot(dot(along_x, design), smooth_in) + dot(dot(along_x, below[0:24]), smooth_below)
    row16, lane16 = iota((16, 128), 0), iota((16, 128), 1)
    z = lane16 % 8 - 1
    x = row16 - 4 + C * lax.axis_index("gx")
    y = lane16 // 8 - 4 + C * lax.axis_index("gy")
    shape = (16, 128)
    normalizer = (
        global_weights(shape, x, total_x) * global_weights(shape, y, total_y) * global_weights(shape, z, NZ)
    )
    inside = (x >= 0) & (x < total_x) & (y >= 0) & (y < total_y) & (z >= 0) & (z < NZ)
    normalizer = jnp.where(inside, normalizer, 1.0)
    density = jnp.where(inside, summed / normalizer, 0.0)
    scale_ref[...] = density * density * density
    weight_ref[...] = -3.0 * density * density / normalizer
    lane = iota((16, 128), 1)
    parts = []
    for c in range(3):
        value = fields_ref[96 + 16 * c : 112 + 16 * c, :]
        value = jnp.where(lane < 32, roll(below[24:40], -32 * c, 1), value)
        value = jnp.where(lane >= 96, roll(above[24:40], 96 - 32 * c, 1), value)
        parts.append(value)
    stack_fields(jnp.concatenate(parts, axis=0), stack_ref)
    for i in range(0, 24, 4):
        rows = list(range(i, i + 4))
        for n, value in zip(rows, push(stiff_ref, stack_ref, rows)):
            pushed_ref[16 * n : 16 * n + 16, :] = value


def second_kernel(
    from_left_ref, from_right_ref, low_ref, high_ref, even_ref, odd_ref, stiff_ref, scale_ref,
    residual_ref, movable_ref, outer_ref, inner_ref,
    direction_ref, low_out, high_out, sums_ref, ratios_ref,
    stack_ref, turned_ref, solved_ref, placed_ref,
):
    direction = add_sides(low_ref[...], high_ref[...], even_ref[...], odd_ref[...])
    factor, inverse = low_ref[0:1, FACTOR : FACTOR + 1], low_ref[0:1, INVERSE : INVERSE + 1]
    for at, ref in ((LEFT, from_left_ref), (RIGHT, from_right_ref), (EVEN, even_ref), (ODD, odd_ref)):
        ratios_ref[at : at + 8, :] = jnp.broadcast_to(factor * ref[0:1, INVERSE : INVERSE + 1], (8, 128))
    ratios_ref[MINE : MINE + 8, :] = jnp.broadcast_to(factor, (8, 128))
    ratios_ref[MINE_INVERSE : MINE_INVERSE + 8, :] = jnp.broadcast_to(inverse, (8, 128))
    direction_ref[...] = direction
    stack_fields(direction, stack_ref)
    scale = scale_ref[...]
    row16, lane16 = iota((16, 128), 0), iota((16, 128), 1)
    own = (row16 >= 4) & (row16 < 12) & (lane16 >= 32) & (lane16 < 96)
    parts = {}
    energy = jnp.zeros((16, 128), F32)
    for q in range(8):
        a, lanes = q % 2, 8 * ((q // 2) % 2) + q // 4
        rows = [3 * q, 3 * q + 1, 3 * q + 2]
        for c, value in enumerate(push(stiff_ref, stack_ref, rows)):
            value = value * scale
            energy = energy + value * stack_ref[16 * (3 * q + c) : 16 * (3 * q + c) + 16, :]
            if a:
                value = roll(value, 1, 0)
            parts[c, lanes] = parts[c, lanes] + value if (c, lanes) in parts else value
    image = []
    for c in range(3):
        value = parts[c, 0]
        for lanes in (1, 8, 9):
            value = value + roll(parts[c, lanes], lanes, 1)
        image.append(value)
    image = jnp.concatenate(image, axis=0) * movable_ref[...]
    turn(image, turned_ref)
    matrices = {0: outer_ref, 1: inner_ref, 2: inner_ref, 3: outer_ref}
    for block_z in range(2):
        solve_columns(range(4), block_z, matrices, turned_ref, solved_ref)
    solved = place_blocks(solved_ref, placed_ref) * movable_ref[...]
    solved = solved * factor
    halves(solved, low_out, high_out)
    sums_ref[0:8, :] = sum_rows(jnp.where(own, energy, 0.0))
    sums_ref[8:16, :] = sum_rows(residual_ref[...] * solved)
    sums_ref[16:24, :] = sum_rows(image * solved)


def third_kernel(
    low_ref, high_ref, even_ref, odd_ref, stiff_ref, scale_ref,
    rho_ref, sums_ref, ratios_ref,
    wide_ref, share_ref, stack_ref,
):
    wide = add_sides(
        low_ref[...], high_ref[...],
        even_ref[...] * tall(ratios_ref[EVEN : EVEN + 8, :]), odd_ref[...] * tall(ratios_ref[ODD : ODD + 8, :]),
    )
    wide_ref[...] = wide
    stack_fields(wide, stack_ref)
    row16, lane16 = iota((16, 128), 0), iota((16, 128), 1)
    own = (row16 >= 4) & (row16 < 12) & (lane16 >= 32) & (lane16 < 96)
    scale = jnp.where(own, scale_ref[...], 0.0)
    both = jnp.zeros((16, 128), F32)
    for i in range(0, 24, 4):
        rows = list(range(i, i + 4))
        for n, value in zip(rows, push(stiff_ref, stack_ref, rows)):
            both = both + value * stack_ref[16 * n : 16 * n + 16, :]
    sums = [
        rho_ref[...], sums_ref[0:8, :], sums_ref[8:16, :], sums_ref[16:24, :],
        sum_rows(both * scale),
    ]
    row, lane = iota((8, 128), 0), iota((8, 128), 1)
    table = jnp.zeros((8, 128), F32)
    for n, value in enumerate(sums):
        table = jnp.where(row == n, jnp.sum(value, axis=0, keepdims=True), table)
    table = jnp.where(row == lane, jnp.sum(table, axis=1, keepdims=True), 0.0)
    line = jnp.sum(table, axis=0, keepdims=True)
    line = jnp.where(lanes_of(line) == 6, ratios_ref[MINE_INVERSE : MINE_INVERSE + 1, :], line)
    share_ref[...] = jnp.broadcast_to(line, share_ref.shape)


def last_kernel(shares_ref, direction_ref, wide_ref, ratios_ref, weight_ref, pushed_ref, adjoint_ref, gradient_ref, smooth_ref):
    shares = shares_ref[...]
    ratio = shares[:, 6:7] * ratios_ref[MINE : MINE + 1, :]
    lane = lanes_of(shares)
    weights = jnp.where(lane < 2, 1.0, jnp.where(lane == 4, ratio * ratio, ratio))
    line = jnp.sum(sum_rows(shares * weights), axis=0, keepdims=True)
    rho, curve, cross, image_wide, both = [line[:, n : n + 1] for n in range(5)]
    step = rho / curve
    unscale = step * ratios_ref[MINE_INVERSE : MINE_INVERSE + 1, 0:1]
    cross, image_wide, both = cross * unscale, image_wide * unscale, both * (unscale * unscale)
    rho_next = rho - cross - step * curve + step * image_wide
    grow = 1.0 + rho_next / rho
    curve_next = grow * grow * curve - 2.0 * grow * image_wide + both
    step_next = rho_next / curve_next
    adjoint = (step + step_next * grow) * direction_ref[...] - (step_next * unscale) * wide_ref[...]
    source, target = iota((128, 32), 0), iota((128, 32), 1)
    y, z = target % 8, target // 8
    pick = (source == 8 * (y + 4) + z + 1).astype(F32)
    own = dot_picks(jnp.concatenate([adjoint[16 * c + 4 : 16 * c + 12] for c in range(3)], axis=0), pick)
    for z_out in range(NZ):
        adjoint_ref[pl.ds(z_out, 24, stride=NZ), :] = own[:, 8 * z_out : 8 * z_out + 8]
    terms = [value * pushed_ref[16 * j : 16 * j + 16, :] for j, value in enumerate(corner_fields(adjoint))]
    while len(terms) > 1:
        terms = [sum(terms[n : n + 3]) for n in range(0, len(terms), 3)]
    energy = terms[0]
    sensitivity = energy * weight_ref[...]
    y_source, z_source = source // 8 - 4, source % 8 - 1
    valid = (z_source >= 0) & (z_source < NZ)
    smooth_ref[...] = dot_picks(sensitivity, jnp.where(valid, hat(y_source - y) * hat(z_source - z), 0.0))
    gradient = 4.0 * smooth_ref[4:12, :]
    for d in range(1, 4):
        gradient = gradient + (4.0 - d) * (smooth_ref[4 - d : 12 - d, :] + smooth_ref[4 + d : 12 + d, :])
    for z_out in range(NZ):
        gradient_ref[pl.ds(z_out, 8, stride=NZ), :] = gradient[:, 8 * z_out : 8 * z_out + 8]


def call(kernel, outs, scratch=(), specs=None, limit=VMEM_LIMIT):
    shapes = [jax.ShapeDtypeStruct(shape, F32) for shape in outs]
    return lambda *args: pl.pallas_call(
        kernel,
        out_shape=shapes,
        in_specs=specs or [VM] * len(args),
        out_specs=[VM] * len(shapes),
        scratch_shapes=list(scratch),
        compiler_params=pltpu.CompilerParams(vmem_limit_bytes=limit),
        cost_estimate=pl.CostEstimate(flops=10**6, bytes_accessed=10**6, transcendentals=0),
    )(*args)


def shifted(value, axis, step):
    size = lax.axis_size(axis)
    return lax.ppermute(value, axis, [(i, (i + step) % size) for i in range(size)])


def both_ways(to_next, to_previous, axis):
    return shifted(to_next, axis, 1), shifted(to_previous, axis, -1)


def paired(even, odd):
    size_x, size_y = lax.axis_size("gx"), lax.axis_size("gy")
    pairs = []
    for i in range(size_x):
        for j in range(size_y):
            inside = 0 < j < size_y - 1
            other = (i, j + 1 if j % 2 else j - 1) if inside else (i ^ 1, j)
            pairs.append((i * size_y + j, other[0] * size_y + other[1]))
    from_even = lax.ppermute(even, "gy", [(j, j ^ 1) for j in range(size_y)])
    return from_even, lax.ppermute(odd, ("gx", "gy"), pairs)


def as_rows(values):
    return jnp.swapaxes(values, -1, -2).reshape((-1, C))


def from_rows(values, shape):
    return jnp.swapaxes(values.reshape(shape[:-2] + (NZ, C)), -1, -2)


def local(design, element_matrix, fixed, inverses, state, load):
    size_x, size_y = lax.axis_size("gx"), lax.axis_size("gy")
    inputs = sum(
        jnp.pad(value, [(first, 10 - first - value.shape[0])] + [(0, 0)] * 3)
        for first, value in ((0, load), (6, state), (9, design[None]))
    )
    inputs = inputs + jnp.pad(fixed, [(3, 4)] + [(0, 0)] * 3).astype(F32)
    own, to_right, to_left = call(pack_kernel, [(80, 128), (16, 128), (16, 128)])(as_rows(inputs))
    left, right = both_ways(to_right, to_left, "gx")
    size_a, size_b, *rest = inverses.shape
    half = (size_a, size_b // 2, *rest)
    mixed_specs = [VM, pl.BlockSpec(memory_space=pl.ANY)]
    arrived = pltpu.SemaphoreType.DMA((4,))
    (outer,) = call(outer_kernel, [half], [arrived], mixed_specs, BRING_LIMIT)(own, inverses)
    fields, design_wide, even, odd = call(widen_kernel, [(144, 128), (24, 128), (40, 128), (40, 128)])(
        outer, own, left, right
    )
    even, odd = paired(even, odd)
    inner, solved = call(
        inner_kernel, [half, (32, 256)], [pltpu.VMEM((80, 128), F32), arrived], mixed_specs, BRING_LIMIT
    )(fields, inverses)
    residual, movable, low, high, rho = call(
        first_kernel, [(48, 128), (48, 128), (24, 128), (24, 128), (8, 128)], SOLVE_SCRATCH
    )(fields, even, odd, outer, solved, element_matrix)
    stiff, scale, weight, pushed = call(
        side_kernel,
        [(576, 128), (16, 128), (16, 128), (384, 128)],
        [pltpu.VMEM((384, 128), F32)],
    )(element_matrix, fields, design_wide, even, odd)

    def crossed(low, high, *ratios):
        left, right = both_ways(high, low, "gx")
        low, high, even, odd = call(cross_kernel, [(24, 128)] * 4)(low, high, left, right, *ratios)
        return left, right, low, high, *paired(even, odd)

    sides = crossed(low, high)
    direction, low, high, sums, ratios = call(
        second_kernel,
        [(48, 128), (24, 128), (24, 128), (24, 128), (48, 128)],
        [pltpu.VMEM((384, 128), F32)] + SOLVE_SCRATCH,
    )(*sides, stiff, scale, residual, movable, outer, inner)
    sides = crossed(low, high, ratios)[2:]
    devices = size_x * size_y
    wide, share = call(
        third_kernel, [(48, 128), (devices, 128)], [pltpu.VMEM((384, 128), F32)]
    )(*sides, stiff, scale, rho, sums, ratios)
    shares = lax.all_to_all(share, ("gx", "gy"), 0, 0, tiled=True)
    adjoint, gradient = call(last_kernel, [(96, C), (32, C)], [pltpu.VMEM((16, 32), F32)])(shares, direction, wide, ratios, weight, pushed)
    return from_rows(adjoint, (3, C, C, NZ)), from_rows(gradient, (C, C, NZ))


def solution(mesh):
    placed = (
        P("gx", "gy", None),
        P(),
        P(None, "gx", "gy", None),
        P("gx", "gy", None, None, None),
        P(None, "gx", "gy", None),
        P(None, "gx", "gy", None),
    )
    return jax.shard_map(
        local,
        mesh=mesh,
        in_specs=placed,
        out_specs=(P(None, "gx", "gy", None), P("gx", "gy", None)),
        check_vma=False,
    )
```
